32 devices in a mesh: fsdp: 4 (over x, core), ctx: 8 (over z, y).
Axes of the slice: x: 2, y: 2, z: 4, core: 2. Of those that a mesh axis runs over, the one named last changes fastest.
Arguments:
- tokens: bfloat16 [5120, 2048], P(('fsdp', 'ctx')), may hold values from -6 to 6
- first_gain: bfloat16 [2048], P('fsdp'), may hold values from 0.099609375 to 1.8984375
- query_weight: bfloat16 [2048, 2048], P('fsdp'), may hold values from -0.125 to 0.125
- key_matrix: bfloat16 [2048, 512], P('fsdp'), may hold values from -0.125 to 0.125
- value_matrix: bfloat16 [2048, 512], P('fsdp'), may hold values from -0.125 to 0.125
- out_weight: bfloat16 [2048, 2048], P('fsdp'), may hold values from -1 to 1
- second_gain: bfloat16 [2048], P('fsdp'), may hold values from 0.099609375 to 1.8984375
- gate_weight: bfloat16 [2048, 8192], P('fsdp'), may hold values from -0.125 to 0.125
- up_weight: bfloat16 [2048, 8192], P('fsdp'), may hold values from -0.125 to 0.125
- down_weight: bfloat16 [8192, 2048], P('fsdp'), may hold values from -0.0625 to 0.0625
- lengths: int32 [4, 4], P('fsdp'), may hold values from 1 to 1024, as said below
- block_order: int32 [16], replicated, may hold values from 0 to 15, as said below
- cotangent: bfloat16 [5120, 2048], P(('fsdp', 'ctx')), may hold values from -6 to 6
Outputs:
- layer_out: bfloat16 [5120, 2048], P(('fsdp', 'ctx'))
- tokens_grad: float32 [5120, 2048], P(('fsdp', 'ctx'))
- first_gain_grad: float32 [2048], P(('fsdp', 'ctx'))
- query_grad: float32 [2048, 2048], P(('fsdp', 'ctx'))
- key_grad: float32 [2048, 512], P(('fsdp', 'ctx'))
- value_grad: float32 [2048, 512], P(('fsdp', 'ctx'))
- out_grad: float32 [2048, 2048], P(('fsdp', 'ctx'))
- second_gain_grad: float32 [2048], P(('fsdp', 'ctx'))
- gate_grad: float32 [2048, 8192], P(('fsdp', 'ctx'))
- up_grad: float32 [2048, 8192], P(('fsdp', 'ctx'))
- down_grad: float32 [8192, 2048], P(('fsdp', 'ctx'))
The draws below stay inside these ranges and needn't reach their ends.
Inputs may be any that keep to these rules, and one draw needn't show every extreme that they name: Each row holds the lengths of the 4 sequences packed one after another in one group; they sum to 1280, and the first is exactly 1024, the longest. `block_order`: A permutation of the 16 blocks in which entry 2c is below 8 and entry 2c + 1 equals 15 minus entry 2c.
All inputs are finite; a program needn't handle non-finite values.
Results may differ from the reference program's by a relative error of at most 0.02.
Values may be sent and summed in bfloat16 or wider, within the bound.
No kernel may reach another device: no remote copies, remote signals or barrier semaphores. Data moves between devices by JAX's collectives and lax.ppermute only.
A program may use at most 576 MiB of HBM per device.

```python
import math
import jax
import jax.numpy as jnp
from jax import lax

MODEL_WIDTH = 2048
QUERY_HEADS = 32
KEY_VALUE_HEADS = 8
HEAD_SIZE = 64
FF = 8192
TOK_DEV = 160
BLOCK = 80
GROUP_TOKENS = 1280
LONG = 1024
NBLK = 16
TOTAL_TOKENS = 5120
N_FSDP = 4


def draw_lengths(key, part):
    key = jax.random.fold_in(key, 11)
    first_key, second_key = jax.random.split(key)
    group_count = TOTAL_TOKENS // GROUP_TOKENS
    rest_total = GROUP_TOKENS - LONG
    first_cut = jax.random.randint(first_key, (group_count,), 1, rest_total // 2 + 1, dtype=jnp.int32)
    second_cut = jax.random.randint(second_key, (group_count,), rest_total // 2 + 1, rest_total, dtype=jnp.int32)
    longest = jnp.full((group_count,), LONG, dtype=jnp.int32)
    return jnp.stack([longest, first_cut, second_cut - first_cut, rest_total - second_cut], axis=1).astype(jnp.int32)


def draw_block_order(key, part):
    key = jax.random.fold_in(key, 23)
    early = jax.random.permutation(key, NBLK // 2).astype(jnp.int32)
    return jnp.stack([early, NBLK - 1 - early], axis=1).reshape(NBLK).astype(jnp.int32)


def levels(rng, dims, shards, least, top_value):
    def one(dim, parts):
        steps = jax.random.uniform(jax.random.fold_in(jax.random.fold_in(rng, 6), dim), (parts,), jnp.float32, least / len(shards), top_value / len(shards))
        return jnp.repeat(jnp.exp(steps), dims[dim] // parts).reshape((-1,) + (1,) * (len(dims) - dim - 1))

    loudness = one(*shards[0])
    for cut in shards[1:]:
        loudness = loudness * one(*cut)
    return loudness


def scatter_about(stream_key, extent, deviation, reach, cuts=(), kind=jnp.bfloat16):
    drawn = deviation * jax.random.normal(stream_key, extent, jnp.float32)
    if cuts:
        drawn = drawn * levels(stream_key, extent, cuts, -0.22, 0.18)
    return jnp.clip(drawn, -reach, reach).astype(kind)


def setup_inputs(seed: int = 0) -> dict:
    seeds = jax.random.split(jax.random.key(seed), 14)
    return {
        "tokens": scatter_about(seeds[0], (TOTAL_TOKENS, MODEL_WIDTH), 1.0, 6.0, ((0, 32),)),
        "first_gain": jnp.clip(1.0 + 0.18 * jax.random.normal(seeds[1], (MODEL_WIDTH,), jnp.float32), 0.099609375, 1.8984375).astype(jnp.bfloat16),
        "query_weight": scatter_about(seeds[2], (MODEL_WIDTH, QUERY_HEADS * HEAD_SIZE), MODEL_WIDTH ** -0.5, 0.125, ((0, 4),)),
        "key_matrix": scatter_about(seeds[3], (MODEL_WIDTH, KEY_VALUE_HEADS * HEAD_SIZE), MODEL_WIDTH ** -0.5, 0.125, ((0, 4),)),
        "value_matrix": scatter_about(seeds[4], (MODEL_WIDTH, KEY_VALUE_HEADS * HEAD_SIZE), MODEL_WIDTH ** -0.5, 0.125, ((0, 4),)),
        "out_weight": scatter_about(seeds[5], (QUERY_HEADS * HEAD_SIZE, MODEL_WIDTH), (QUERY_HEADS * HEAD_SIZE // 64) ** -0.5, 1.0, ((0, 4),)),
        "second_gain": jnp.clip(1.0 + 0.18 * jax.random.normal(seeds[6], (MODEL_WIDTH,), jnp.float32), 0.099609375, 1.8984375).astype(jnp.bfloat16),
        "gate_weight": scatter_about(seeds[7], (MODEL_WIDTH, FF), MODEL_WIDTH ** -0.5, 0.125, ((0, 4),)),
        "up_weight": scatter_about(seeds[8], (MODEL_WIDTH, FF), MODEL_WIDTH ** -0.5, 0.125, ((0, 4),)),
        "down_weight": scatter_about(seeds[9], (FF, MODEL_WIDTH), FF ** -0.5, 0.0625, ((0, 4),)),
        "lengths": draw_lengths(jax.random.fold_in(seeds[13], 71), 0),
        "block_order": draw_block_order(jax.random.fold_in(seeds[13], 71), 0),
        "cotangent": scatter_about(seeds[12], (TOTAL_TOKENS, MODEL_WIDTH), 1.0, 6.0, ((0, 32),)),
    }


NORM_EPS = 1e-05
ROPE_BASE = 500000.0
MASKED_SCORE = -1e+30

@jax.custom_vjp
def lower_precision(v):
    return lax.optimization_barrier(v.astype(jnp.bfloat16)).astype(jnp.float32)

@jax.custom_vjp
def lower_precision_back(v):
    return v

def low_keep(v):
    return (lower_precision(v), None)

def low_pass(kept, grad):
    return (grad,)

def back_keep(v):
    return (v, None)

def back_low(kept, grad):
    return (lower_precision(grad),)
lower_precision.defvjp(low_keep, low_pass)
lower_precision_back.defvjp(back_keep, back_low)

def rope_tables(position):
    freqs = ROPE_BASE ** (-(jnp.arange(HEAD_SIZE // 2, dtype=jnp.float32) * 2.0 / HEAD_SIZE))
    angle = position.astype(jnp.float32)[:, None] * freqs[None, :]
    return (jnp.cos(angle)[:, None, :], jnp.sin(angle)[:, None, :])

def apply_rotary(rotated_in, cosine_table, sine_values):
    half_size = rotated_in.shape[-1] // 2
    first_half = rotated_in[..., :half_size]
    second_half = rotated_in[..., half_size:]
    return jnp.concatenate([first_half * cosine_table - second_half * sine_values, second_half * cosine_table + first_half * sine_values], axis=-1)

def token_layout(lengths, block_order):
    row_ids = jnp.arange(GROUP_TOKENS, dtype=jnp.int32)
    dealt = (2 * (row_ids // TOK_DEV) + row_ids % TOK_DEV // BLOCK).astype(jnp.int32)
    packed = (jnp.take(block_order, dealt) * BLOCK + row_ids % BLOCK).astype(jnp.int32)
    seq_ends = jnp.cumsum(lengths, axis=1).astype(jnp.int32)
    seq_starts = (seq_ends - lengths).astype(jnp.int32)
    seq_ids = lax.optimization_barrier(jnp.sum((packed[None, :, None] >= seq_ends[:, None, :]).astype(jnp.int32), axis=2)).astype(jnp.int32)
    position = (packed[None, :] - jnp.take_along_axis(seq_starts, seq_ids, axis=1)).astype(jnp.int32)
    packed_all = jnp.broadcast_to(packed[None, :], seq_ids.shape)
    return (seq_ids, packed_all, position)

def layer_forward(inputs_f, first_gain, query_weight, key_matrix, value_matrix, out_weight, second_gain, gate_weight, up_weight, down_weight, seq_ids, packed, position):
    best = lax.Precision.HIGHEST

    def matrix_product(left_in, right_in):
        return jnp.dot(left_in, right_in, precision=best, preferred_element_type=jnp.float32)
    normed_one = inputs_f * lax.rsqrt(lax.optimization_barrier(jnp.mean(inputs_f * inputs_f, axis=-1, keepdims=True)) + NORM_EPS)
    first_hidden = lower_precision(normed_one * first_gain)
    cosine_table, sine_values = rope_tables(position.reshape(TOTAL_TOKENS))
    query_pre = lower_precision_back(matrix_product(first_hidden, query_weight)).reshape(TOTAL_TOKENS, QUERY_HEADS, HEAD_SIZE)
    key_before_rotary = lower_precision_back(matrix_product(first_hidden, key_matrix)).reshape(TOTAL_TOKENS, KEY_VALUE_HEADS, HEAD_SIZE)
    query_rows = lower_precision(apply_rotary(query_pre, cosine_table, sine_values))
    key_row_matrix = lower_precision(apply_rotary(key_before_rotary, cosine_table, sine_values))
    value_rows = lower_precision(lower_precision_back(matrix_product(first_hidden, value_matrix))).reshape(TOTAL_TOKENS, KEY_VALUE_HEADS, HEAD_SIZE)
    reference_rows = 4 * TOK_DEV
    grouped_queries = query_rows.reshape(N_FSDP, GROUP_TOKENS // reference_rows, reference_rows, KEY_VALUE_HEADS, QUERY_HEADS // KEY_VALUE_HEADS, HEAD_SIZE)
    grouped_keys = key_row_matrix.reshape(N_FSDP, GROUP_TOKENS, KEY_VALUE_HEADS, HEAD_SIZE)
    grouped_values = value_rows.reshape(N_FSDP, GROUP_TOKENS, KEY_VALUE_HEADS, HEAD_SIZE)
    score_scale = 1.0 / math.sqrt(HEAD_SIZE)

    def one_group(group_args):
        group_query, group_key, group_value, group_seq, group_packed = group_args

        def one_block(block_args):
            block_query, block_seq, block_packed = block_args
            raw_scores = lower_precision_back(jnp.einsum('qgrd,tgd->grqt', block_query, group_key, precision=best))
            allowed = (block_seq[:, None] == group_seq[None, :]) & (group_packed[None, :] <= block_packed[:, None])
            scores = jnp.where(allowed, raw_scores * score_scale, MASKED_SCORE)
            weights = jax.nn.softmax(scores, axis=-1)
            return jnp.einsum('grqt,tgd->qgrd', lower_precision(weights), group_value, precision=best)
        return lax.map(jax.checkpoint(one_block), (group_query, group_seq.reshape(-1, reference_rows), group_packed.reshape(-1, reference_rows)))
    attended_raw = lax.map(one_group, (grouped_queries, grouped_keys, grouped_values, seq_ids, packed))
    attended = lower_precision(lower_precision_back(attended_raw.reshape(TOTAL_TOKENS, QUERY_HEADS * HEAD_SIZE)))
    residual = inputs_f + lower_precision_back(matrix_product(attended, out_weight))
    normed_two = residual * lax.rsqrt(lax.optimization_barrier(jnp.mean(residual * residual, axis=-1, keepdims=True)) + NORM_EPS)
    hidden_two = lower_precision(normed_two * second_gain)
    gate_proj = lower_precision_back(matrix_product(hidden_two, gate_weight))
    up_proj = lower_precision_back(matrix_product(hidden_two, up_weight))
    activated = lower_precision(jax.nn.silu(gate_proj) * up_proj)
    return residual + lower_precision_back(matrix_product(activated, down_weight))

def reference(tokens, first_gain, query_weight, key_matrix, value_matrix, out_weight, second_gain, gate_weight, up_weight, down_weight, lengths, block_order, cotangent):
    seq_ids, packed, position = token_layout(lengths, block_order)
    floats = [array_in.astype(jnp.float32) for array_in in (tokens, first_gain, query_weight, key_matrix, value_matrix, out_weight, second_gain, gate_weight, up_weight, down_weight)]

    def closed(*params):
        return layer_forward(*params, seq_ids, packed, position)
    output, pullback = jax.vjp(closed, *floats)
    gradients = pullback(cotangent.astype(jnp.float32))
    return (output.astype(jnp.bfloat16), gradients[0], gradients[1], gradients[2], gradients[3], gradients[4], gradients[5], gradients[6], gradients[7], gradients[8], gradients[9])
```

```python
import math

import jax
import jax.numpy as jnp
from jax import lax
from jax.sharding import PartitionSpec as P

QUERY_HEADS = 32
KEY_VALUE_HEADS = 8
HEAD_SIZE = 64

NORM_EPS = 1e-05
ROPE_BASE = 500000.0
MASKED_SCORE = -1e30
BF = jnp.bfloat16
F32 = jnp.float32


def rope_tables(position):
    freqs = ROPE_BASE ** (-(jnp.arange(HEAD_SIZE // 2, dtype=F32) * 2.0 / HEAD_SIZE))
    angle = position.astype(F32)[:, None] * freqs[None, :]
    return (jnp.cos(angle)[:, None, :], jnp.sin(angle)[:, None, :])


def apply_rotary(rotated_in, cosine_table, sine_values):
    half_size = rotated_in.shape[-1] // 2
    first_half = rotated_in[..., :half_size]
    second_half = rotated_in[..., half_size:]
    return jnp.concatenate(
        [
            first_half * cosine_table - second_half * sine_values,
            second_half * cosine_table + first_half * sine_values,
        ],
        axis=-1,
    )


def packed_rows(order_part, block_rows):
    offsets = jnp.arange(block_rows, dtype=jnp.int32)
    return (order_part[:, None] * block_rows + offsets[None, :]).reshape(-1)


def sequence_place(packed, seq_lengths):
    seq_ends = jnp.cumsum(seq_lengths)
    seq_starts = seq_ends - seq_lengths
    seq_ids = jnp.sum((packed[:, None] >= seq_ends[None, :]).astype(jnp.int32), axis=1)
    onehot_seq = (
        seq_ids[:, None] == jnp.arange(seq_lengths.shape[0], dtype=jnp.int32)[None, :]
    ).astype(jnp.int32)
    return (seq_ids, packed - jnp.sum(onehot_seq * seq_starts[None, :], axis=1))


def rms_scale(value_rows):
    return lax.rsqrt(jnp.mean(value_rows * value_rows, axis=-1, keepdims=True) + NORM_EPS)


def norm_back(grad_normed, normed, inverse):
    return inverse * (grad_normed - normed * jnp.mean(grad_normed * normed, axis=-1, keepdims=True))


def mm(left_in, right_in):
    return jnp.dot(left_in, right_in, preferred_element_type=F32)


def mm_nt(left_in, right_in):
    return lax.dot_general(left_in, right_in, (((1,), (1,)), ((), ())), preferred_element_type=F32)


def mm_tn(left_in, right_in):
    return lax.dot_general(left_in, right_in, (((0,), (0,)), ((), ())), preferred_element_type=F32)


def swap_fsdp(value, d):
    return lax.ppermute(value, "fsdp", [(i, i ^ d) for i in range(4)])


def gather_fsdp(shard):
    across = swap_fsdp(shard, 2)
    return [shard, swap_fsdp(shard, 1), across, swap_fsdp(across, 1)]


def xor_blocks(value, f, axis):
    size = value.shape[axis] // 4
    return jnp.concatenate(
        [lax.dynamic_slice_in_dim(value, (f ^ d) * size, size, axis) for d in range(4)], axis=axis
    )


def swap_cols(value, d, parts):
    width = value.shape[1] // (4 * parts)
    return jnp.concatenate(
        [
            value[:, (p * 4 + (e ^ d)) * width : (p * 4 + (e ^ d) + 1) * width]
            for p in range(parts)
            for e in range(4)
        ],
        axis=1,
    )


def scatter_fsdp(term, fix):
    size = term.shape[0] // 4
    blocks = [term[d * size : (d + 1) * size] for d in range(4)]
    got = swap_fsdp(jnp.concatenate([blocks[1], blocks[3]], axis=0).astype(BF), 1)
    own = blocks[0] + fix(got[:size], 1).astype(F32)
    other = blocks[2] + fix(got[size:], 1).astype(F32)
    return own + fix(swap_fsdp(other.astype(BF), 2), 2).astype(F32)


def ring_index(place, n):
    place = place % n
    return jnp.where(place < n // 2, 2 * place, 2 * (n - 1 - place) + 1)


def ring_shift(value, step, n):
    order = list(range(0, n, 2)) + list(range(n - 1, 0, -2))
    return lax.ppermute(value, "ctx", [(order[i], order[(i + step) % n]) for i in range(n)])


def ring_gather(own, n):
    half, width = n // 2, own.shape[1] // 2
    chunks = {0: own}
    right = left = own
    for step in range(1, half):
        right = ring_shift(right, 1, n)
        left = ring_shift(left, -1, n)
        chunks[-step], chunks[step] = right, left
    chunks[half] = jnp.concatenate(
        [ring_shift(right[:, :width], 1, n), ring_shift(left[:, width:], -1, n)], axis=1
    )
    return chunks


def ring_scatter(contrib, n):
    half = n // 2
    far = contrib(half)
    width = far.shape[1] // 2
    from_left = ring_shift(far[:, :width].astype(BF), 1, n)
    from_right = ring_shift(far[:, width:].astype(BF), -1, n)
    pad = ((0, 0), (0, width))
    from_left = jnp.pad(from_left, pad)
    from_right = jnp.pad(from_right, pad[:1] + (pad[1][::-1],))
    for step in range(half - 1, 0, -1):
        from_left = ring_shift((contrib(step) + from_left.astype(F32)).astype(BF), 1, n)
        from_right = ring_shift((contrib(-step) + from_right.astype(F32)).astype(BF), -1, n)
    return contrib(0) + from_left.astype(F32) + from_right.astype(F32)


def reduce_gain(term):
    within = lax.psum_scatter(term.astype(BF), "fsdp", scatter_dimension=0, tiled=True)
    return lax.psum_scatter(within, "ctx", scatter_dimension=0, tiled=True).astype(F32)


def body(
    n,
    tokens,
    first_gain,
    query_weight,
    key_matrix,
    value_matrix,
    out_weight,
    second_gain,
    gate_weight,
    up_weight,
    down_weight,
    lengths,
    block_order,
    cotangent,
):
    token_rows, model = tokens.shape
    block_rows = token_rows // 2
    kv_width = key_matrix.shape[1]
    heads_per_group = QUERY_HEADS // KEY_VALUE_HEADS
    score_scale = 1.0 / math.sqrt(HEAD_SIZE)
    c = lax.axis_index("ctx")
    f = lax.axis_index("fsdp")
    place = jnp.where(c % 2 == 0, c // 2, n - 1 - c // 2)
    rel = list(range(-(n // 2 - 1), n // 2 + 1))
    owners = ring_index(place + jnp.asarray(rel, jnp.int32), n)

    own_blocks = lax.dynamic_slice_in_dim(block_order, 2 * c, 2)
    key_blocks = jnp.take(block_order.reshape(n, 2), owners, axis=0).reshape(-1)
    packed_query = packed_rows(own_blocks, block_rows)
    packed_key = packed_rows(key_blocks, block_rows)
    seq_query, position = sequence_place(packed_query, lengths[0])
    seq_key = sequence_place(packed_key, lengths[0])[0]
    allowed = (seq_query[:, None] == seq_key[None, :]) & (
        packed_key[None, :] <= packed_query[:, None]
    )
    cosine_table, sine_values = rope_tables(position)

    kv_rows = gather_fsdp(jnp.concatenate([key_matrix, value_matrix], axis=1))
    query_rows_w = gather_fsdp(query_weight)
    gains = jnp.stack([first_gain, second_gain])
    gains_x = jnp.concatenate(gather_fsdp(gains), axis=1).astype(F32)
    gain_one, gain_two = gains_x[0], gains_x[1]
    weight_kv = jnp.concatenate(kv_rows, axis=0)
    weight_q = jnp.concatenate(query_rows_w, axis=0)
    weight_o = jnp.concatenate(gather_fsdp(out_weight), axis=0)

    units = gate_weight.shape[1] // (4 * n)
    span = gate_weight.shape[1] // 4

    def own_units(weight):
        return [
            lax.dynamic_slice_in_dim(weight, (f ^ e) * span + c * units, units, 1)
            for e in range(4)
        ]

    gate_up_own = jnp.concatenate(own_units(gate_weight) + own_units(up_weight), axis=1)
    gate_up = jnp.concatenate(
        [swap_cols(part, d, 2) for d, part in enumerate(gather_fsdp(gate_up_own))], axis=0
    )
    down = jnp.concatenate(
        gather_fsdp(lax.dynamic_slice_in_dim(down_weight, c * units, units, 0)), axis=0
    )
    grad_out_all = ring_gather(cotangent, n)

    inputs_f = tokens.astype(F32)
    inverse_one = rms_scale(inputs_f)
    normed_one = xor_blocks(inputs_f * inverse_one, f, 1)
    first_hidden = (normed_one * gain_one).astype(BF)
    kv_pre = mm(first_hidden, weight_kv)
    key_before_rotary = kv_pre[:, :kv_width].reshape(token_rows, KEY_VALUE_HEADS, HEAD_SIZE)
    key_row_matrix = (
        apply_rotary(key_before_rotary, cosine_table, sine_values)
        .astype(BF)
        .reshape(token_rows, kv_width)
    )
    value_rows = kv_pre[:, kv_width:].astype(BF)
    kv_all = ring_gather(jnp.concatenate([key_row_matrix, value_rows], axis=1), n)
    kv_all = jnp.concatenate([kv_all[r] for r in rel], axis=0)
    query_pre = mm(first_hidden, weight_q).reshape(token_rows, QUERY_HEADS, HEAD_SIZE)
    query_rows = apply_rotary(query_pre, cosine_table, sine_values).astype(BF)
    key_total_count = kv_all.shape[0]
    query_head_rows = query_rows.reshape(
        token_rows, KEY_VALUE_HEADS, heads_per_group, HEAD_SIZE
    ).transpose(1, 0, 2, 3)
    key_head_rows = (
        kv_all[:, :kv_width]
        .reshape(key_total_count, KEY_VALUE_HEADS, HEAD_SIZE)
        .transpose(1, 0, 2)
    )
    value_head_rows = (
        kv_all[:, kv_width:]
        .reshape(key_total_count, KEY_VALUE_HEADS, HEAD_SIZE)
        .transpose(1, 0, 2)
    )

    def head_forward(head_args):
        head_query, head_key, head_value = head_args
        raw_scores = jnp.einsum("qrd,td->qrt", head_query, head_key, preferred_element_type=F32)
        scores = jnp.where(allowed[:, None, :], raw_scores * score_scale, MASKED_SCORE)
        row_peak = jnp.max(scores, axis=-1, keepdims=True)
        expd_rows = jnp.exp(scores - row_peak)
        row_total = jnp.sum(expd_rows, axis=-1, keepdims=True)
        weights = (expd_rows / row_total).astype(BF)
        mixed_rows = jnp.einsum("qrt,td->qrd", weights, head_value, preferred_element_type=F32)
        return (mixed_rows, (row_peak + jnp.log(row_total))[..., 0])

    head_out, head_lse = lax.map(head_forward, (query_head_rows, key_head_rows, value_head_rows))
    attended = (
        head_out.transpose(1, 0, 2, 3).reshape(token_rows, QUERY_HEADS * HEAD_SIZE).astype(BF)
    )
    attended = xor_blocks(attended, f, 1)
    residual = inputs_f + mm(attended, weight_o)
    inverse_two = rms_scale(residual)
    normed_two = xor_blocks(residual * inverse_two, f, 1)
    hidden_two = (normed_two * gain_two).astype(BF)

    hidden_all = ring_gather(hidden_two, n)
    width = 4 * units
    activated, grad_gate_up = {}, {}
    for r in sorted(rel, key=abs):
        gate_up_proj = mm(hidden_all[r], gate_up)
        gate_proj, up_proj = gate_up_proj[:, :width], gate_up_proj[:, width:]
        gate_sig = jax.nn.sigmoid(gate_proj)
        activated[r] = (gate_proj * gate_sig * up_proj).astype(BF)
        grad_act = mm_nt(grad_out_all[r], down)
        grad_gate = grad_act * up_proj * gate_sig * (1.0 + gate_proj * (1.0 - gate_sig))
        grad_up = grad_act * gate_proj * gate_sig
        grad_gate_up[r] = jnp.concatenate([grad_gate, grad_up], axis=1).astype(BF)
    grad_hidden_two = ring_scatter(lambda r: mm_nt(grad_gate_up[r], gate_up), n)
    layer_out = (residual + ring_scatter(lambda r: mm(activated[r], down), n)).astype(BF)

    activated_rows = jnp.concatenate([activated[r] for r in rel], axis=0)
    grad_out_rows = jnp.concatenate([grad_out_all[r] for r in rel], axis=0)
    hidden_rows = jnp.concatenate([hidden_all[r] for r in rel], axis=0)
    grad_gate_up_rows = jnp.concatenate([grad_gate_up[r] for r in rel], axis=0)
    down_grad = scatter_fsdp(mm_tn(activated_rows, grad_out_rows), lambda value, d: value)
    down_grad = down_grad.astype(BF).astype(F32)
    gate_up_grad = scatter_fsdp(
        mm_tn(hidden_rows, grad_gate_up_rows), lambda value, d: swap_cols(value, d, 2)
    ).astype(BF)
    own_rows = gate_up_grad.shape[0] // n
    gate_up_grad = lax.all_to_all(
        gate_up_grad.reshape(n, own_rows, 2 * width), "ctx", 0, 0, tiled=False
    )
    gate_up_grad = gate_up_grad.reshape(n, own_rows, 2, 4, units).transpose(2, 1, 3, 0, 4)
    gate_up_grad = xor_blocks(gate_up_grad, f, 2).reshape(2, own_rows, 4 * n * units).astype(F32)
    gate_grad, up_grad = gate_up_grad[0], gate_up_grad[1]

    grad_normed_two = grad_hidden_two * gain_two
    gain_two_term = jnp.sum(grad_hidden_two * normed_two, axis=0)
    grad_residual = cotangent.astype(F32) + xor_blocks(
        norm_back(grad_normed_two, normed_two, inverse_two), f, 1
    )
    grad_branch = grad_residual.astype(BF)

    def reduce_rows(term):
        within = scatter_fsdp(term, lambda value, d: value)
        rows = within.shape[0] // n

        def contrib(r):
            start = ring_index(place + r, n) * rows
            return lax.dynamic_slice_in_dim(within, start, rows, 0)

        return ring_scatter(contrib, n)

    out_grad = reduce_rows(mm_tn(attended, grad_branch))
    second_gain_grad = reduce_gain(xor_blocks(gain_two_term, f, 0))
    attended_gradient = xor_blocks(mm_nt(grad_branch, weight_o), f, 1).astype(BF)
    head_gradients = attended_gradient.reshape(
        token_rows, KEY_VALUE_HEADS, heads_per_group, HEAD_SIZE
    ).transpose(1, 0, 2, 3)

    def head_backward(head_args):
        head_query, head_key, head_value, head_grad, head_logsum = head_args
        raw_scores = jnp.einsum("qrd,td->qrt", head_query, head_key, preferred_element_type=F32)
        scores = jnp.where(allowed[:, None, :], raw_scores * score_scale, MASKED_SCORE)
        prob_rows = jnp.exp(scores - head_logsum[..., None])
        grad_probs = jnp.einsum("qrd,td->qrt", head_grad, head_value, preferred_element_type=F32)
        row_dot = jnp.sum(prob_rows * grad_probs, axis=-1, keepdims=True)
        grad_scores = (prob_rows * (grad_probs - row_dot) * score_scale).astype(BF)
        grad_query_head = jnp.einsum(
            "qrt,td->qrd", grad_scores, head_key, preferred_element_type=F32
        )
        grad_key_head = jnp.einsum(
            "qrt,qrd->td", grad_scores, head_query, preferred_element_type=F32
        )
        grad_value_head = jnp.einsum(
            "qrt,qrd->td", prob_rows.astype(BF), head_grad, preferred_element_type=F32
        )
        return (grad_query_head, grad_key_head, grad_value_head)

    grad_q_heads, grad_k_heads, grad_v_heads = lax.map(
        head_backward, (query_head_rows, key_head_rows, value_head_rows, head_gradients, head_lse)
    )
    grad_key_part = grad_k_heads.transpose(1, 0, 2).reshape(key_total_count, kv_width)
    grad_value_part = grad_v_heads.transpose(1, 0, 2).reshape(key_total_count, kv_width)
    grad_kv_part = jnp.concatenate([grad_key_part, grad_value_part], axis=1)
    grad_query_rows = grad_q_heads.transpose(1, 0, 2, 3).reshape(token_rows, QUERY_HEADS, HEAD_SIZE)
    grad_query = (
        apply_rotary(grad_query_rows, cosine_table, -sine_values)
        .astype(BF)
        .reshape(token_rows, QUERY_HEADS * HEAD_SIZE)
    )
    query_grad = reduce_rows(mm_tn(first_hidden, grad_query))

    def kv_contrib(r):
        start = rel.index(r) * token_rows
        return grad_kv_part[start : start + token_rows]

    grad_kv = ring_scatter(kv_contrib, n)
    grad_key = (
        apply_rotary(
            grad_kv[:, :kv_width].reshape(token_rows, KEY_VALUE_HEADS, HEAD_SIZE),
            cosine_table,
            -sine_values,
        )
        .astype(BF)
        .reshape(token_rows, kv_width)
    )
    grad_kv_pre = jnp.concatenate([grad_key, grad_kv[:, kv_width:].astype(BF)], axis=1)
    kv_grad = reduce_rows(mm_tn(first_hidden, grad_kv_pre))
    grad_hidden_one = mm_nt(grad_query, weight_q) + mm_nt(grad_kv_pre, weight_kv)
    gain_one_term = jnp.sum(grad_hidden_one * normed_one, axis=0)
    first_gain_grad = reduce_gain(xor_blocks(gain_one_term, f, 0))
    tokens_grad = grad_residual + xor_blocks(
        norm_back(grad_hidden_one * gain_one, normed_one, inverse_one), f, 1
    )
    return (
        layer_out,
        tokens_grad,
        first_gain_grad,
        query_grad,
        kv_grad[:, :kv_width],
        kv_grad[:, kv_width:],
        out_grad,
        second_gain_grad,
        gate_grad,
        up_grad,
        down_grad,
    )


def solution(mesh):
    rows, vector = P(("fsdp", "ctx"), None), P(("fsdp", "ctx"))
    weight = P("fsdp", None)

    def layer(*arrays):
        return body(mesh.shape["ctx"], *arrays)

    return jax.shard_map(
        layer,
        mesh=mesh,
        in_specs=(
            rows, P("fsdp"), weight, weight, weight, weight, P("fsdp"), weight, weight, weight,
            weight, P(), rows,
        ),
        out_specs=(rows, rows, vector, rows, rows, rows, rows, vector, rows, rows, rows),
        check_vma=False,
    )
```

```python
import functools

import jax
import jax.numpy as jnp
from jax import lax
from jax.experimental import pallas as pl
from jax.experimental.pallas import tpu as pltpu
from jax.sharding import PartitionSpec as P

HEAD = 64
NORM_EPS = 1e-05
ROPE_BASE = 500000.0
MASKED = -1e30
VARIANTS = 5
BF = jnp.bfloat16
F32 = jnp.float32
MIB = 2**20


def dot(a, b):
    return jnp.dot(a, b, preferred_element_type=F32)


def dot_nt(a, b):
    return lax.dot_general(a, b, (((1,), (1,)), ((), ())), preferred_element_type=F32)


def fill_bias(sc, bias, own, block, ends_at, ends):
    for j in range(2):
        place = sc[own + j] * block + lax.broadcasted_iota(jnp.int32, bias.shape[1:], 0)
        key = lax.broadcasted_iota(jnp.int32, bias.shape[1:], 1)
        start = jnp.zeros_like(place)
        for s in range(ends):
            end = sc[ends_at + s]
            start = jnp.where(place >= end, end, start)
        bias[j] = jnp.where((key >= start) & (key <= place), 0.0, MASKED)


def fill_keys(sc, chunks, keys, values, block, blocks_at):
    for r, chunk in enumerate(chunks):
        for j in range(2):
            at = pl.multiple_of(sc[blocks_at + 2 * r + j] * block, 16)
            part = chunk[j * block : (j + 1) * block, :]
            for g in range(2):
                keys[g, pl.ds(at, block), :] = part[:, g * HEAD : (g + 1) * HEAD]
                values[g, pl.ds(at, block), :] = part[:, 2 * HEAD + g * HEAD : 2 * HEAD + (g + 1) * HEAD]


def split_heads(ref, out, block, group):
    for g in range(2):
        for j in range(2):
            for h in range(group):
                lane = (g * group + h) * HEAD
                out[g, j, h * block : (h + 1) * block, :] = ref[
                    j * block : (j + 1) * block, lane : lane + HEAD
                ]


def join_heads(out, block, group):
    rows = []
    for j in range(2):
        rows.append(
            jnp.concatenate(
                [out[g, j, h * block : (h + 1) * block, :] for g in range(2) for h in range(group)],
                axis=1,
            )
        )
    return jnp.concatenate(rows, axis=0)


def visible(sc, own, j, block, step):
    return (sc[own + j] * block + block - 1) // step + 1


def forward_kernel(n, group, ends, sc, q_ref, *rest):
    chunks, (o_ref, lse_ref), (bias, keys, values, queries, outs) = (
        rest[:n],
        rest[n : n + 2],
        rest[n + 2 :],
    )
    block = q_ref.shape[0] // 2
    total = keys.shape[1]
    step = total // VARIANTS
    pair = pl.program_id(0)

    @pl.when(pair == 0)
    def _():
        fill_bias(sc, bias, 1, block, 3 + 2 * n, ends)
        lse_ref[...] = jnp.zeros_like(lse_ref)

    fill_keys(sc, chunks, keys, values, block, 3)
    split_heads(q_ref, queries, block, group)

    def one(g, j, length):
        scores = dot_nt(queries[g, j], keys[g, :length, :])
        scores = (scores.reshape(group, block, length) + bias[j, :, :length][None]).reshape(
            group * block, length
        )
        peak = jnp.max(scores, axis=-1, keepdims=True)
        expd = jnp.exp(scores - peak)
        row_total = jnp.sum(expd, axis=-1, keepdims=True)
        mixed = dot(expd.astype(BF), values[g, :length, :])
        outs[g, j] = mixed / row_total
        lse = peak + jnp.log(row_total)
        lane = lax.broadcasted_iota(jnp.int32, (block, lse_ref.shape[1]), 1)
        rows = pl.ds(pl.multiple_of(j * block, 16), block)
        kept = lse_ref[rows, :]
        for h in range(group):
            kept = jnp.where(
                lane == (pair * 2 + g) * group + h, lse[h * block : (h + 1) * block], kept
            )
        lse_ref[rows, :] = kept

    def both(at, carry):
        g, j = at // 2, at % 2
        count = visible(sc, 1, j, block, step)
        for v in range(1, VARIANTS + 1):
            pl.when(count == v)(functools.partial(one, g, j, v * step))
        return carry

    lax.fori_loop(0, 4, both, 0)
    o_ref[...] = join_heads(outs, block, group).astype(o_ref.dtype)


def attention_forward(scalars, queries, chunks, ends):
    n = len(chunks)
    rows, width = queries.shape
    group = width // HEAD // 8
    block, total = rows // 2, rows * n
    pairs = 4
    return pl.pallas_call(
        functools.partial(forward_kernel, n, group, ends),
        grid_spec=pltpu.PrefetchScalarGridSpec(
            num_scalar_prefetch=1,
            grid=(pairs,),
            in_specs=[pl.BlockSpec((rows, width // pairs), lambda p, sc: (0, p))]
            + [pl.BlockSpec((rows, 4 * HEAD), lambda p, sc: (0, p))] * n,
            out_specs=[
                pl.BlockSpec((rows, width // pairs), lambda p, sc: (0, p ^ sc[0])),
                pl.BlockSpec((rows, 128), lambda p, sc: (0, 0)),
            ],
            scratch_shapes=[
                pltpu.VMEM((2, block, total), F32),
                pltpu.VMEM((2, total, HEAD), BF),
                pltpu.VMEM((2, total, HEAD), BF),
                pltpu.VMEM((2, 2, group * block, HEAD), BF),
                pltpu.VMEM((2, 2, group * block, HEAD), F32),
            ],
        ),
        out_shape=[
            jax.ShapeDtypeStruct((rows, width), BF),
            jax.ShapeDtypeStruct((rows, 128), F32),
        ],
        compiler_params=pltpu.CompilerParams(vmem_limit_bytes=48 * 2**20),
        cost_estimate=cost(18),
        name="attention_forward",
    )(scalars, queries, *chunks)


def backward_kernel(n, group, ends, first, sc, q_ref, do_ref, lse_ref, cos_ref, sin_ref, *rest):
    chunks, (dq_ref, dkv_ref), scratch = rest[:n], rest[n : n + 2], rest[n + 2 :]
    bias, keys, values, queries, grads, outs, dkeys, dvalues, flat = scratch
    block = q_ref.shape[0] // 2
    total = keys.shape[1]
    step = total // VARIANTS
    pair = pl.program_id(0) + first

    @pl.when(pair == first)
    def _():
        fill_bias(sc, bias, 1, block, 3 + 2 * n, ends)

    fill_keys(sc, chunks, keys, values, block, 3)
    split_heads(q_ref, queries, block, group)
    split_heads(do_ref, grads, block, group)
    dkeys[...] = jnp.zeros_like(dkeys)
    dvalues[...] = jnp.zeros_like(dvalues)

    def one(g, j, length):
        query, grad = queries[g, j], grads[g, j]
        key, value = keys[g, :length, :], values[g, :length, :]
        rows = pl.ds(pl.multiple_of(j * block, 16), block)
        kept = lse_ref[rows, :]
        lane = lax.broadcasted_iota(jnp.int32, kept.shape, 1)
        lse = jnp.concatenate(
            [
                jnp.sum(
                    jnp.where(lane == (pair * 2 + g) * group + h, kept, 0.0), axis=1, keepdims=True
                )
                for h in range(group)
            ],
            axis=0,
        )
        scores = dot_nt(query, key)
        scores = (scores.reshape(group, block, length) + bias[j, :, :length][None]).reshape(
            group * block, length
        )
        prob = jnp.exp(scores - lse)
        dprob = dot_nt(grad, value)
        weighted = prob * dprob
        row_dot = jnp.sum(weighted, axis=-1, keepdims=True)
        dscore = (weighted - prob * row_dot).astype(BF)
        outs[g, j] = dot(dscore, key)
        dkeys[g, :, :length] += dot(query.T, dscore)
        dvalues[g, :, :length] += dot(grad.T, prob.astype(BF))

    def both(at, carry):
        g, j = at // 2, at % 2
        count = visible(sc, 1, j, block, step)
        for v in range(1, VARIANTS + 1):
            pl.when(count == v)(functools.partial(one, g, j, v * step))
        return carry

    lax.fori_loop(0, 4, both, 0)
    dq = join_heads(outs, block, group) * (1.0 / 8.0)
    cosine, sine = cos_ref[...], sin_ref[...]
    low = lax.broadcasted_iota(jnp.int32, cosine.shape, 1) % HEAD < HEAD // 2
    for t in range(dq.shape[1] // 128):
        part = dq[:, t * 128 : (t + 1) * 128]
        turned = jnp.where(low, pltpu.roll(part, 96, 1), pltpu.roll(part, 32, 1))
        dq_ref[:, t * 128 : (t + 1) * 128] = (part * cosine - turned * sine).astype(dq_ref.dtype)
    flat[:, : 2 * HEAD] = jnp.concatenate([dkeys[0], dkeys[1]], axis=0).T
    flat[:, 2 * HEAD :] = jnp.concatenate([dvalues[0], dvalues[1]], axis=0).T
    for r in range(2 * n):
        at = pl.multiple_of(sc[3 + r] * block, 16)
        dkv_ref[r * block : (r + 1) * block, :] = flat[pl.ds(at, block), :].astype(dkv_ref.dtype)


def attention_backward(scalars, queries, grads, lse, cosine, sine, chunks, ends, pairs):
    n = len(chunks)
    rows, width = queries.shape
    group = width // HEAD // 8
    block, total = rows // 2, rows * n
    first, steps = pairs
    whole = pl.BlockSpec((rows, 128), lambda p, sc: (0, 0))
    wide = pl.BlockSpec((rows, width // 4), lambda p, sc: (0, p + first))
    return pl.pallas_call(
        functools.partial(backward_kernel, n, group, ends, first),
        grid_spec=pltpu.PrefetchScalarGridSpec(
            num_scalar_prefetch=1,
            grid=(steps,),
            in_specs=[
                wide,
                pl.BlockSpec((rows, width // 4), lambda p, sc: (0, (p + first) ^ sc[0])),
                whole,
                whole,
                whole,
            ]
            + [pl.BlockSpec((rows, 4 * HEAD), lambda p, sc: (0, p + first))] * n,
            out_specs=[
                pl.BlockSpec((rows, width // 4), lambda p, sc: (0, p)),
                pl.BlockSpec((total, 4 * HEAD), lambda p, sc: (0, p)),
            ],
            scratch_shapes=[
                pltpu.VMEM((2, block, total), F32),
                pltpu.VMEM((2, total, HEAD), BF),
                pltpu.VMEM((2, total, HEAD), BF),
                pltpu.VMEM((2, 2, group * block, HEAD), BF),
                pltpu.VMEM((2, 2, group * block, HEAD), BF),
                pltpu.VMEM((2, 2, group * block, HEAD), F32),
                pltpu.VMEM((2, HEAD, total), F32),
                pltpu.VMEM((2, HEAD, total), F32),
                pltpu.VMEM((total, 4 * HEAD), F32),
            ],
        ),
        out_shape=[
            jax.ShapeDtypeStruct((rows, steps * width // 4), BF),
            jax.ShapeDtypeStruct((total, steps * 4 * HEAD), BF),
        ],
        compiler_params=pltpu.CompilerParams(vmem_limit_bytes=56 * 2**20),
        cost_estimate=cost(26),
        name="attention_backward",
    )(scalars, queries, grads, lse, cosine, sine, *chunks)


def params(mib):
    return pltpu.CompilerParams(vmem_limit_bytes=mib * MIB)


def cost(micros):
    return pl.CostEstimate(flops=int(micros * 1e7), bytes_accessed=0, transcendentals=0)


def row_scale(values):
    return lax.rsqrt(jnp.mean(values * values, axis=-1, keepdims=True) + NORM_EPS)


def quarter(f, d, size):
    return pl.ds(pl.multiple_of((f ^ d) * size, size), size)


def norm_kernel(f_ref, x_ref, gain_ref, h_ref):
    inverse = row_scale(x_ref[...].astype(F32))
    size = x_ref.shape[1] // 4
    for d in range(4):
        part = x_ref[:, quarter(f_ref[0], d, size)].astype(F32) * inverse
        h_ref[:, d * size : (d + 1) * size] = (
            part * gain_ref[:, d * size : (d + 1) * size]
        ).astype(BF)


def smem():
    return pl.BlockSpec(memory_space=pltpu.SMEM)


def vmem():
    return pl.BlockSpec(memory_space=pltpu.VMEM)


def norm_rows(scalars, rows, gain):
    return pl.pallas_call(
        norm_kernel,
        in_specs=[smem(), vmem(), vmem()],
        out_specs=vmem(),
        out_shape=jax.ShapeDtypeStruct(rows.shape, BF),
        compiler_params=params(32),
        cost_estimate=cost(1),
        name="norm_rows",
    )(scalars, rows, gain)


def project_kernel(scale, turned_tiles, x_ref, cos_ref, sin_ref, *refs):
    weights, out_ref = refs[:-1], refs[-1]
    size = x_ref.shape[1] // 4
    parts = []
    for at in range(0, len(weights), 4):
        parts.append(
            sum(
                dot(x_ref[:, d * size : (d + 1) * size], w[...])
                for d, w in enumerate(weights[at : at + 4])
            )
        )
    cosine, sine = cos_ref[...], sin_ref[...]
    low = lax.broadcasted_iota(jnp.int32, cosine.shape, 1) % HEAD < HEAD // 2
    tiles = [p[:, t * 128 : (t + 1) * 128] for p in parts for t in range(p.shape[1] // 128)]
    for t, part in enumerate(tiles):
        if t < turned_tiles:
            turned = jnp.where(low, pltpu.roll(part, 96, 1), pltpu.roll(part, 32, 1))
            part = part * cosine + turned * sine
        part = part.astype(BF)
        if scale != 1.0:
            part = (part.astype(F32) * scale).astype(BF)
        out_ref[:, t * 128 : (t + 1) * 128] = part


def project(rows, cosine, sine, weights, turned_tiles, scale, micros):
    count, depth = rows.shape
    size, width = weights[0][0].shape
    part = 256 // len(weights)
    whole = lambda a: pl.BlockSpec(a.shape, lambda j: (0, 0))
    return pl.pallas_call(
        functools.partial(project_kernel, scale, turned_tiles),
        grid=(width // part,),
        in_specs=[whole(rows), whole(cosine), whole(sine)]
        + [pl.BlockSpec((size, part), lambda j: (0, j))] * (4 * len(weights)),
        out_specs=pl.BlockSpec((count, 256), lambda j: (0, j)),
        out_shape=jax.ShapeDtypeStruct((count, width * len(weights)), BF),
        compiler_params=params(32),
        cost_estimate=cost(micros),
        name="project",
    )(rows, cosine, sine, *[w for shards in weights for w in shards])


def out_kernel(f_ref, o_ref, x_ref, gain_ref, w0, w1, w2, w3, r_ref, h_ref):
    size = o_ref.shape[1] // 4
    tile = w0.shape[1]
    total = sum(
        dot(o_ref[:, d * size : (d + 1) * size], w[...]) for d, w in enumerate((w0, w1, w2, w3))
    )
    at = pl.ds(pl.multiple_of(pl.program_id(0) * tile, tile), tile)
    r_ref[:, at] = x_ref[:, at].astype(F32) + total

    @pl.when(pl.program_id(0) == pl.num_programs(0) - 1)
    def _():
        norm_kernel(f_ref, r_ref, gain_ref, h_ref)


def out_project(scalars, mixed, tokens, gain, weights):
    count, depth = mixed.shape
    size, width = weights[0].shape
    whole = lambda a: pl.BlockSpec(a.shape, lambda j: (0, 0))
    return pl.pallas_call(
        out_kernel,
        grid=(width // 256,),
        in_specs=[smem(), whole(mixed), whole(tokens), whole(gain)]
        + [pl.BlockSpec((size, 256), lambda j: (0, j))] * 4,
        out_specs=[whole(tokens), whole(tokens)],
        out_shape=[
            jax.ShapeDtypeStruct((count, width), F32),
            jax.ShapeDtypeStruct((count, width), BF),
        ],
        compiler_params=params(32),
        cost_estimate=cost(6),
        name="out_project",
    )(scalars, mixed, tokens, gain, *weights)


def norm_back_kernel(wide, f_ref, x_ref, gain_ref, base_ref, *rest):
    terms, outs = rest[:-wide], rest[-wide:]
    x = x_ref[...].astype(F32)
    inverse = row_scale(x)
    size = x_ref.shape[1] // 4
    f = f_ref[0]
    grads, normed = [], []
    dot_sum = 0.0
    for d in range(4):
        cols = slice(d * size, (d + 1) * size)
        grad = sum(t[:, cols].astype(F32) for t in terms)
        part = x_ref[:, quarter(f, d, size)].astype(F32) * inverse
        outs[1][:, cols] = jnp.sum(grad * part, axis=0, keepdims=True)
        grad = grad * gain_ref[:, cols]
        dot_sum += jnp.sum(grad * part, axis=-1, keepdims=True)
        grads.append(grad)
        normed.append(part)
    mean = dot_sum / x_ref.shape[1]
    for d in range(4):
        at = quarter(f, d, size)
        value = base_ref[:, at].astype(F32) + inverse * (grads[d] - normed[d] * mean)
        outs[0][:, at] = value
        if wide == 3:
            outs[2][:, at] = value.astype(BF)


def norm_back(scalars, rows, gain, base, terms, rounded):
    wide = 3 if rounded else 2
    shapes = [
        jax.ShapeDtypeStruct(rows.shape, F32),
        jax.ShapeDtypeStruct((1, rows.shape[1]), F32),
        jax.ShapeDtypeStruct(rows.shape, BF),
    ][:wide]
    return pl.pallas_call(
        functools.partial(norm_back_kernel, wide),
        in_specs=[smem()] + [vmem()] * (3 + len(terms)),
        out_specs=[vmem()] * wide,
        out_shape=shapes,
        compiler_params=params(40),
        cost_estimate=cost(2),
        name="norm_back",
    )(scalars, rows, gain, base, *terms)


def back_kernel(pairs, based, *refs):
    out_ref = refs[-1]
    step = pl.program_id(0)
    tile = refs[pairs].shape[0]
    size = tile * pl.num_programs(0)
    for d in range(4):
        at = pl.ds(pl.multiple_of(d * size + step * tile, tile), tile)
        total = sum(dot_nt(refs[i][...], refs[pairs + 4 * i + d][...]) for i in range(pairs))
        if based:
            total += refs[5 * pairs][:, at]
        out_ref[:, at] = total.astype(out_ref.dtype)


def back_project(rows, weights, kind, micros, base=None):
    count = rows[0].shape[0]
    size = weights[0][0].shape[0]
    whole = pl.BlockSpec((count, 4 * size), lambda j: (0, 0))
    extra = [] if base is None else [base]
    return pl.pallas_call(
        functools.partial(back_kernel, len(rows), base is not None),
        grid=(2,),
        in_specs=[pl.BlockSpec(r.shape, lambda j: (0, 0)) for r in rows]
        + [pl.BlockSpec((size // 2, w.shape[1]), lambda j: (j, 0)) for ws in weights for w in ws]
        + [whole] * len(extra),
        out_specs=whole,
        out_shape=jax.ShapeDtypeStruct((count, 4 * size), kind),
        compiler_params=params(40),
        cost_estimate=cost(micros),
        name="back_project",
    )(*rows, *[w for ws in weights for w in ws], *extra)


def cross(value):
    half = value.shape[1] // 2
    return jnp.concatenate([value[:, half:], value[:, :half]], axis=1)


def feed_kernel(m, kept, crossed, *refs):
    hidden, grads = refs[:m], refs[m : 2 * m]
    gates, ups = refs[2 * m : 2 * m + 4], refs[2 * m + 4 : 2 * m + 8]
    down_ref = refs[2 * m + 8]
    outs = refs[2 * m + 9 + kept :]
    rows_h, rows_dy, act_ref, dgu_ref, dh_ref, h_s, dy_s, dh_s = outs
    step = pl.program_id(0)
    count = hidden[0].shape[0]
    size = gates[0].shape[0]
    tile = gates[0].shape[1]

    @pl.when(step == 0)
    def _():
        for i in range(m):
            at = slice(i * count, (i + 1) * count)
            h_s[at], dy_s[at] = hidden[i][...], grads[i][...]
            rows_h[at], rows_dy[at] = hidden[i][...], grads[i][...]

    def ahead(weights):
        parts = [dot(h_s[:, d * size : (d + 1) * size], w[...]) for d, w in enumerate(weights)]
        if not crossed:
            return sum(parts)
        return parts[0] + parts[2] + cross(parts[1] + parts[3])

    gate, up = ahead(gates), ahead(ups)
    sig = jax.nn.sigmoid(gate)
    silu = gate * sig
    act_ref[...] = (silu * up).astype(BF)
    grad_act = dot_nt(dy_s[...], down_ref[...])
    grad_gate = (grad_act * up * sig * (1.0 + gate * (1.0 - sig))).astype(BF)
    grad_up = (grad_act * silu).astype(BF)
    dgu_ref[:, :tile] = grad_gate
    dgu_ref[:, tile:] = grad_up
    pairs = [(grad_gate, grad_up)] * 4
    if crossed:
        pairs[1] = pairs[3] = (cross(grad_gate), cross(grad_up))
    last = pl.num_programs(0) - 1
    for d in range(4):
        cols = slice(d * size, (d + 1) * size)
        dh = dot_nt(pairs[d][0], gates[d][...]) + dot_nt(pairs[d][1], ups[d][...])

        @pl.when(step == 0)
        def _():
            dh_s[:, cols] = dh

        @pl.when(step > 0)
        def _():
            dh_s[:, cols] += dh

    @pl.when(step == last)
    def _():
        dh_ref[...] = dh_s[...].astype(BF)


def feed_tile(units):
    crossed = units >= 128
    return (2 * units if crossed else 4 * units), crossed


def feed(hidden, grads, gate_up, down, slot, kept, n):
    m = len(hidden)
    count, depth = hidden[0].shape
    width = down.shape[0]
    tile, crossed = feed_tile(width // 4)
    steps = width // tile
    rows = m * count
    size = depth // 4

    def shard(d, part):
        flip = d >> 1 if crossed else 0
        return pl.BlockSpec((size, tile), lambda e: (0, part * steps + (e ^ flip)))

    chunk = pl.BlockSpec((count, depth), lambda e: (0, 0))
    block = pl.BlockSpec((rows, depth), lambda e: (slot, 0))
    shapes = [
        jax.ShapeDtypeStruct((n * count, depth), BF),
        jax.ShapeDtypeStruct((n * count, depth), BF),
        jax.ShapeDtypeStruct((n * count, width), BF),
        jax.ShapeDtypeStruct((n * count, 2 * width), BF),
        jax.ShapeDtypeStruct((rows, depth), BF),
    ]
    first = 2 * m + 9
    *kept, dh = pl.pallas_call(
        functools.partial(feed_kernel, m, len(kept), crossed),
        grid=(steps,),
        in_specs=[chunk] * (2 * m)
        + [shard(d, 0) for d in range(4)]
        + [shard(d, 1) for d in range(4)]
        + [pl.BlockSpec((tile, depth), lambda e: (e, 0))]
        + [pl.BlockSpec(memory_space=pl.ANY)] * len(kept),
        out_specs=[
            block,
            block,
            pl.BlockSpec((rows, tile), lambda e: (slot, e)),
            pl.BlockSpec((rows, 2 * tile), lambda e: (slot, e)),
            pl.BlockSpec((rows, depth), lambda e: (0, 0)),
        ],
        scratch_shapes=[pltpu.VMEM((rows, depth), BF)] * 2 + [pltpu.VMEM((rows, depth), F32)],
        out_shape=shapes,
        input_output_aliases={first + i: i for i in range(len(kept))},
        compiler_params=params(48),
        cost_estimate=cost(8 + 4 * m),
        name="feed",
    )(*hidden, *grads, *gate_up, *gate_up, down, *kept)
    return kept, [dh[i * count : (i + 1) * count] for i in range(m)]


def down_kernel(sc, act_ref, down_ref, y_ref):
    y_ref[...] = dot(act_ref[...], down_ref[...]).astype(BF)


def down_rows(scalars, act, down, n):
    count = act.shape[0] // n
    at = scalars.shape[0] - n
    return pl.pallas_call(
        down_kernel,
        grid_spec=pltpu.PrefetchScalarGridSpec(
            num_scalar_prefetch=1,
            grid=(n,),
            in_specs=[
                pl.BlockSpec((count, act.shape[1]), lambda i, sc: (i, 0)),
                pl.BlockSpec(down.shape, lambda i, sc: (0, 0)),
            ],
            out_specs=pl.BlockSpec((count, down.shape[1]), lambda i, sc: (sc[at + i], 0)),
        ),
        out_shape=jax.ShapeDtypeStruct((n * count, down.shape[1]), BF),
        compiler_params=params(32),
        cost_estimate=cost(12),
        name="down_rows",
    )(scalars, act, down)


def place_kernel(sc, *refs):
    out = refs[-1]
    count = refs[0].shape[0]
    for i, part in enumerate(refs[:-1]):
        out[pl.ds(pl.multiple_of(sc[i] * count, count), count), :] = part[...]


def place_rows(places, parts):
    count, width = parts[0].shape
    return pl.pallas_call(
        place_kernel,
        in_specs=[smem()] + [vmem()] * len(parts),
        out_specs=vmem(),
        out_shape=jax.ShapeDtypeStruct((count * len(parts), width), parts[0].dtype),
        compiler_params=params(24),
        cost_estimate=cost(2),
        name="place_rows",
    )(places, *parts)


def tn_kernel(adds, outs, left_ref, right_ref, *refs):
    turned = refs[-1]
    i, j = pl.program_id(0), pl.program_id(1)

    @pl.when(j == 0)
    def _():
        turned[...] = left_ref[...].T

    total = dot(turned[...], right_ref[...])
    for (low, high, crossed), extra in zip(adds, refs):
        extra = extra[...].astype(F32)
        if crossed:
            extra = cross(extra)
        if low is not None:
            extra = jnp.where((j >= low) & (j < high), extra, 0.0)
        total += extra
    for (row, low, high), out in zip(outs, refs[len(adds) :]):

        @pl.when((i == row) & (j >= low) & (j < high))
        def _():
            out[...] = total.astype(out.dtype)


def tn_blocks(left, right, blocks, kind, micros, adds=(), pieces=1):
    rows, depth = left.shape
    size, width = depth // 4, right.shape[1]
    tile = min(width, 512)
    steps = width // tile
    pieces = min(pieces, steps)
    if size % 128:
        result = []
        for block in blocks:
            total = lax.dot_general(
                left[:, block * size : (block + 1) * size],
                right,
                (((0,), (0,)), ((), ())),
                preferred_element_type=F32,
            )
            for array, part, parts, _ in adds:
                at = part * (width // parts)
                total = total.at[:, at : at + width // parts].add(array.astype(F32))
            result.append(jnp.split(total.astype(kind), pieces, axis=1))
        return result
    first = blocks[0]
    stride = blocks[1] - first if len(blocks) > 1 else 0

    def window(part, parts):
        count = max(1, steps // parts)
        return part * count, (part + 1) * count

    def added_spec(part, parts):
        low, high = window(part, parts)
        return pl.BlockSpec((size, tile), lambda i, j: (0, jnp.clip(j - low, 0, high - low - 1)))

    def out_spec(row, low, high):
        def index(i, j):
            at = jnp.clip(j - low, 0, high - low - 1)
            return (0, jnp.where(i < row, 0, jnp.where(i > row, high - low - 1, at)))

        return pl.BlockSpec((size, tile), index)

    windows = [
        (*(window(part, parts) if parts > 1 and steps > 1 else (None, None)), crossed)
        for _, part, parts, crossed in adds
    ]
    outs = [(row, *window(piece, pieces)) for row in range(len(blocks)) for piece in range(pieces)]
    result = pl.pallas_call(
        functools.partial(tn_kernel, windows, outs),
        grid=(len(blocks), steps),
        in_specs=[
            pl.BlockSpec((rows, size), lambda i, j: (0, first + stride * i)),
            pl.BlockSpec((rows, tile), lambda i, j: (0, j)),
        ]
        + [added_spec(part, parts) for _, part, parts, _ in adds],
        out_specs=[out_spec(*out) for out in outs],
        out_shape=[jax.ShapeDtypeStruct((size, width // pieces), kind)] * len(outs),
        scratch_shapes=[pltpu.VMEM((size, rows), BF)],
        compiler_params=params(32),
        cost_estimate=cost(micros),
        name="tn_blocks",
    )(left, right, *[a[0] for a in adds])
    return [list(result[row * pieces : (row + 1) * pieces]) for row in range(len(blocks))]


def spread_kernel(n, units, f_ref, *refs):
    arrays, outs = refs[:-2], refs[-2:]
    tile = arrays[0].shape[2] // 2
    span = outs[0].shape[1] // 4
    c = pl.program_id(0)
    e = 0
    for array in arrays:
        for at in range(0, tile, units):
            start = (f_ref[0] ^ e) * span + c * units
            e += 1
            for part in range(2):
                value = array[0, :, part * tile + at : part * tile + at + units].astype(F32)
                outs[part][:, pl.ds(pl.multiple_of(start, units), units)] = value


def spread(scalars, arrays, units):
    n, rows, _ = arrays[0].shape
    width = 4 * n * units
    return pl.pallas_call(
        functools.partial(spread_kernel, n, units),
        grid=(n,),
        in_specs=[smem()] + [pl.BlockSpec((1, *a.shape[1:]), lambda i: (i, 0, 0)) for a in arrays],
        out_specs=[pl.BlockSpec((rows, width), lambda i: (0, 0))] * 2,
        out_shape=[jax.ShapeDtypeStruct((rows, width), F32)] * 2,
        compiler_params=params(32),
        cost_estimate=cost(4),
        name="spread",
    )(scalars, *arrays)


def swap_fsdp(value, d):
    return lax.ppermute(value, "fsdp", [(i, i ^ d) for i in range(4)])


def after(value, *others):
    return lax.optimization_barrier((value, others))[0] if others else value


def gather_fsdp(shard):
    across = swap_fsdp(shard, 2)
    return [shard, swap_fsdp(shard, 1), across, swap_fsdp(across, 1)]


def xor_blocks(value, f, axis):
    size = value.shape[axis] // 4
    return jnp.concatenate(
        [lax.dynamic_slice_in_dim(value, (f ^ d) * size, size, axis) for d in range(4)], axis=axis
    )


def swap_cols(value, d, parts):
    width = value.shape[1] // (4 * parts)
    return jnp.concatenate(
        [
            value[:, (p * 4 + (e ^ d)) * width : (p * 4 + (e ^ d) + 1) * width]
            for p in range(parts)
            for e in range(4)
        ],
        axis=1,
    )


def ring_index(place, n):
    place = place % n
    return jnp.where(place < n // 2, 2 * place, 2 * (n - 1 - place) + 1)


def ring_shift(value, step, n):
    order = list(range(0, n, 2)) + list(range(n - 1, 0, -2))
    return lax.ppermute(value, "ctx", [(order[i], order[(i + step) % n]) for i in range(n)])


class Order:
    def __init__(self):
        self.last = ()

    def at(self, value):
        return after(value, *self.last)

    def done(self, value):
        self.last = (value,)
        return value

    def take(self, value):
        return self.done(self.at(value))

    def run(self, function, *args, **kwargs):
        return self.done(function(*self.at(args), **kwargs))


class Gather:
    def __init__(self, order, own, n):
        self.order, self.n, self.half, self.step = order, n, n // 2, 0
        self.chunks = {0: own}
        self.now = (own, own)
        self.width = own.shape[1] // 2

    def send(self):
        self.step += 1
        right, left = self.now
        if self.step == self.half:
            right, left = right[:, : self.width], left[:, self.width :]
        self.now = (ring_shift(right, 1, self.n), ring_shift(left, -1, self.n))

    def take(self):
        self.now = right, left = self.order.take(self.now)
        if self.step == self.half:
            self.chunks[self.half] = jnp.concatenate([right, left], axis=1)
        else:
            self.chunks[-self.step], self.chunks[self.step] = right, left

    def rest(self, hops=None):
        while self.step < self.half and hops != 0:
            self.take()
            self.send()
            hops = hops and hops - 1
        return self


class Scatter:
    def __init__(self, order, contrib, n):
        self.order, self.n, self.half, self.step = order, n, n // 2, 0
        self.contrib = contrib
        far = contrib(self.half)
        self.width = far.shape[1] // 2
        self.now = (far[:, : self.width].astype(BF), far[:, self.width :].astype(BF))

    def send(self):
        self.step += 1
        right, left = self.now
        self.now = (ring_shift(right, 1, self.n), ring_shift(left, -1, self.n))

    def take(self):
        self.now = got = self.order.take(self.now)
        r = self.half - self.step
        if r == 0:
            return (self.contrib(0), *got)
        got = [v.astype(F32) for v in got]
        width = self.width
        ahead, behind = self.contrib(r).astype(F32), self.contrib(-r).astype(F32)
        if self.step == 1:
            ahead = jnp.concatenate([ahead[:, :width] + got[0], ahead[:, width:]], axis=1)
            behind = jnp.concatenate([behind[:, :width], behind[:, width:] + got[1]], axis=1)
        else:
            ahead, behind = ahead + got[0], behind + got[1]
        self.now = (ahead.astype(BF), behind.astype(BF))

    def rest(self, hops=None):
        while self.step < self.half and hops != 0:
            self.take()
            self.send()
            hops = hops and hops - 1
        return self


def added(terms):
    return sum(t.astype(F32) for t in terms)


def deinterleave(both):
    runs = range(both.shape[1] // 256)
    return tuple(
        jnp.concatenate([both[:, p * 256 + o : p * 256 + o + 128] for p in runs], axis=1)
        for o in (0, 128)
    )


def turn_tables(block_ids, block, ends, starts):
    place = (block_ids[:, None] * block + jnp.arange(block, dtype=jnp.int32)[None, :]).reshape(-1)
    begin = jnp.max(jnp.where(place[:, None] >= starts[None, :], starts[None, :], 0), axis=1)
    freqs = ROPE_BASE ** (-(jnp.arange(HEAD // 2, dtype=F32) * 2.0 / HEAD))
    angle = (place - begin).astype(F32)[:, None] * freqs[None, :]
    cosine, sine = jnp.cos(angle), jnp.sin(angle)
    return (
        jnp.concatenate([cosine] * 4, axis=1),
        jnp.concatenate([-sine, sine, -sine, sine], axis=1),
    )


def turn_back(values, cosine, sine):
    parts = []
    for p in range(values.shape[1] // 128):
        part = values[:, p * 128 : (p + 1) * 128]
        if p % 2 == 0:
            low = lax.broadcasted_iota(jnp.int32, part.shape, 1) % HEAD < HEAD // 2
            turned = jnp.where(low, jnp.roll(part, -32, axis=1), jnp.roll(part, 32, axis=1))
            part = part * cosine - turned * sine
        parts.append(part)
    return jnp.concatenate(parts, axis=1)


def body(
    n,
    tokens,
    first_gain,
    query_weight,
    key_matrix,
    value_matrix,
    out_weight,
    second_gain,
    gate_weight,
    up_weight,
    down_weight,
    lengths,
    block_order,
    cotangent,
):
    token_rows, model = tokens.shape
    block = token_rows // 2
    c = lax.axis_index("ctx")
    f = lax.axis_index("fsdp")
    place = jnp.where(c % 2 == 0, c // 2, n - 1 - c // 2)
    half = n // 2
    rel = list(range(-(half - 1), half + 1))
    owners = ring_index(place + jnp.asarray(rel, jnp.int32), n)

    own_blocks = lax.dynamic_slice_in_dim(block_order, 2 * c, 2)
    key_blocks = jnp.take(block_order.reshape(n, 2), owners, axis=0).reshape(-1)
    seq_ends = jnp.cumsum(lengths[0])
    count = lengths.shape[1]
    slot_rel = [r for step in range(1, half) for r in (-step, step)] + [0, half]
    slot_owners = ring_index(place + jnp.asarray(slot_rel, jnp.int32), n)
    scalars = jnp.concatenate([f[None], own_blocks, key_blocks, seq_ends, slot_owners])
    scalars = scalars.astype(jnp.int32)
    cosine, sine = turn_tables(own_blocks, block, seq_ends, seq_ends - lengths[0])
    order = Order()

    units = gate_weight.shape[1] // (4 * n)
    span = gate_weight.shape[1] // 4
    width = 4 * units

    def own_units(weight):
        return [
            lax.dynamic_slice_in_dim(weight, (f ^ e) * span + c * units, units, 1)
            for e in range(4)
        ]

    gains = gather_fsdp(jnp.stack([first_gain, second_gain]))
    gains = jnp.concatenate(gains, axis=1).astype(F32)
    gain_one, gain_two = gains[:1], gains[1:]
    out_part = out_weight.shape[0] // n
    out_across = swap_fsdp(lax.dynamic_slice_in_dim(out_weight, c * out_part, out_part, 0), 2)
    key_across, value_across = swap_fsdp(key_matrix, 2), swap_fsdp(value_matrix, 2)
    grad_out = Gather(order, cotangent, n)
    grad_out.send()
    key_core, value_core = swap_fsdp(key_matrix, 1), swap_fsdp(value_matrix, 1)
    out_core, query_core = swap_fsdp(out_weight, 1), swap_fsdp(query_weight, 1)
    down_own = lax.dynamic_slice_in_dim(down_weight, c * units, units, 0)
    down_core = swap_fsdp(down_own, 1)

    hidden_one = order.run(norm_rows, scalars, tokens, gain_one)
    out_across = order.take(out_across)
    out_parts = Gather(order, out_across, n)
    out_parts.send()
    key_across = order.take(key_across)
    key_far = swap_fsdp(key_across, 1)
    out_parts.rest(1)
    value_across = order.take(value_across)
    value_far = swap_fsdp(value_across, 1)
    query_across = swap_fsdp(order.at(query_weight), 2)
    gate_up_own = order.done(
        jnp.concatenate(own_units(order.at(gate_weight)) + own_units(up_weight), axis=1)
    )
    gate_up_core = swap_fsdp(gate_up_own, 1)
    out_parts.rest(1)
    grad_out.take()
    key_far, value_far = order.take((key_far, value_far))
    weight_k = [key_matrix, key_core, key_across, key_far]
    weight_v = [value_matrix, value_core, value_across, value_far]
    kv_own = order.run(project, hidden_one, cosine, sine, [weight_k, weight_v], turned_tiles=1, scale=1.0, micros=4)
    kv = Gather(order, kv_own, n)
    kv.send()
    kv.rest(1)
    out_parts.take()
    kv.rest(1)
    query_across = order.take(query_across)
    query_far = swap_fsdp(query_across, 1)
    gate_up_across = swap_fsdp(order.at(gate_up_own), 2)
    down_across = swap_fsdp(order.at(after(down_own, query_across)), 2)
    kv.rest()
    kv.take()
    kv_chunks = [kv.chunks[r] for r in rel]
    out_parts.send()
    query_far = order.take(query_far)
    weight_q = [query_weight, query_core, query_across, query_far]

    queries = order.run(project, hidden_one, cosine, sine, [weight_q], turned_tiles=2, scale=0.125, micros=7)
    out_parts.rest()
    out_parts.take()
    out_across = order.run(place_rows, owners.astype(jnp.int32), [out_parts.chunks[r] for r in rel])
    out_far = swap_fsdp(out_across, 1)
    grad_out.send()
    mixed, lse = order.run(attention_forward, scalars, queries, kv_chunks, ends=count)
    grad_out.rest(1)
    weight_o = [out_weight, out_core, out_across, out_far]
    residual, hidden_two = order.run(out_project, scalars, mixed, tokens, gain_two, weight_o)
    grad_out.rest()
    hidden = Gather(order, hidden_two, n)
    hidden.send()
    gate_up_across = order.take(gate_up_across)
    gate_up_far = swap_fsdp(gate_up_across, 1)
    grad_out.take()
    down_across = order.take(down_across)
    down_far = swap_fsdp(down_across, 1)
    gate_up = [gate_up_own, gate_up_core, gate_up_across, gate_up_far]
    if units < 128:
        gate_up = [swap_cols(part, d, 2) for d, part in enumerate(gate_up)]
    down = jnp.concatenate([down_own, down_core, down_across, down_far], axis=0)

    kept, grads_two = [], {}
    for near in range(half + 1):
        group = (0,) if near == 0 else (half,) if near == half else (-near, near)
        slot = n - 2 if near == 0 else n - 1 if near == half else near - 1
        kept, parts = order.run(
            feed,
            [hidden.chunks[r] for r in group],
            [grad_out.chunks[r] for r in group],
            gate_up,
            down,
            slot=slot,
            kept=kept,
            n=n,
        )
        grads_two.update(zip(group, parts))
        if near < half:
            hidden.take()
        if near < half - 1:
            hidden.send()

    rows_h, rows_dy, act, grads = kept
    tile, crossed = feed_tile(units)
    waiting, under_way = [], []

    def tick():
        while under_way:
            mid, h = under_way.pop()
            mid[h] = order.take(mid[h])
        if waiting:
            mid, h = waiting.pop(0)
            mid[h] = swap_fsdp(order.at(mid[h]), 2)
            under_way.append((mid, h))

    class Product:
        def __init__(self, left, right, micros, by_units=False):
            self.left, self.right, self.micros, self.by_units = left, right, micros, by_units

        def kernel(self, blocks, kind, adds=(), pieces=1):
            def run(left, right, *arrays):
                own = [(a, *rest) for a, (_, *rest) in zip(arrays, adds)]
                micros = self.micros * len(blocks)
                return tn_blocks(left, right, blocks, kind, micros, own, pieces)

            return order.run(run, self.left, self.right, *[a for a, *_ in adds])

        def from_partner(self, value, d):
            return swap_cols(value, d, 2) if self.by_units and not crossed else value

        def first(self):
            self.near = [
                [swap_fsdp(piece, 1) for piece in row] for row in self.kernel((1, 3), BF, (), 4)
            ]

        def pieces(self, row):
            turned = self.by_units and crossed
            got = [self.from_partner(v, 1) for v in order.take(self.near[row])]
            return [(v, p, len(got), turned) for p, v in enumerate(got)]

        def second(self, halves=2):
            (self.mid,) = self.kernel((2,), BF, self.pieces(1), halves)
            waiting.extend((self.mid, h) for h in range(len(self.mid)))

        def last(self, kind):
            over = [self.from_partner(v, 2) for v in self.mid]
            if self.by_units and crossed:
                over = over[::-1]
            adds = [(v, h, len(over), False) for h, v in enumerate(over)]
            ((whole,),) = self.kernel((0,), kind, self.pieces(0) + adds)
            return whole

    sums = Scatter(order, lambda r: grads_two[r], n)
    sums.send()
    of_down = Product(act, rows_dy, 3)
    of_gate_up = Product(rows_h, grads, 5, True)
    of_down.first()
    sums.rest(1)
    of_gate_up.first()
    of_down.second(1)
    tick()
    sums.rest(1)
    of_gate_up.second()
    y_rows = order.run(down_rows, scalars, act, down, n=n)
    sums.rest(1)
    tick()
    down_grad = of_down.last(F32)
    sums.rest()
    grad_hidden_two = sums.take()
    grad_residual, gain_two_term, grad_branch = order.run(
        norm_back, scalars, residual, gain_two, cotangent, grad_hidden_two, rounded=True
    )
    grad_mixed = order.run(back_project, [grad_branch], [weight_o], kind=BF, micros=5)
    tick()
    y_own = lax.psum_scatter(order.at(y_rows), "ctx", scatter_dimension=0, tiled=True)
    of_out = Product(mixed, grad_branch, 2)
    of_out.first()

    parts = []

    def attention_part(first):
        parts.append(
            order.run(
                attention_backward,
                scalars,
                queries,
                grad_mixed,
                lse,
                cosine,
                sine,
                kv_chunks,
                ends=count,
                pairs=(first, 2),
            )
        )

    attention_part(0)
    of_out.second()
    tick()
    attention_part(2)
    grad_query = jnp.concatenate([p[0] for p in parts], axis=1)

    def kv_contrib(r):
        start = rel.index(r) * token_rows
        return jnp.concatenate([p[1][start : start + token_rows] for p in parts], axis=1)

    grad_kv = Scatter(order, kv_contrib, n)
    grad_kv.send()
    of_query = Product(hidden_one, grad_query, 2)
    of_query.first()
    grad_kv.rest(1)
    tick()
    gate_up_grad = of_gate_up.last(BF)
    rows = gate_up_grad.shape[0] // n
    gate_up_all = lax.all_to_all(
        gate_up_grad.reshape(n, rows, 2 * width), "ctx", 0, 0, tiled=False
    )
    grad_kv.rest(1)
    of_query.second()
    grad_hidden_one = order.run(back_project, [grad_query], [weight_q], kind=F32, micros=5)
    grad_kv.rest(1)
    tick()

    def scatter_rows(within):
        rows = within.shape[0] // n

        def contrib(r):
            start = ring_index(place + r, n) * rows
            return lax.dynamic_slice_in_dim(within, start, rows, 0)

        return Scatter(order, contrib, n)

    out_sums = scatter_rows(of_out.last(BF))
    grad_kv.rest()
    grad_kv = added(grad_kv.take())
    out_sums.send()
    grad_kv = turn_back(grad_kv, cosine, sine).astype(BF)
    grad_key, grad_value = deinterleave(grad_kv)
    grad_kv = jnp.concatenate([grad_key, grad_value], axis=1)
    of_kv = Product(hidden_one, grad_kv, 1.5)
    of_kv.first()
    grad_hidden_one = order.run(
        back_project, [grad_key, grad_value], [weight_k, weight_v], base=grad_hidden_one, kind=F32, micros=3
    )
    out_sums.rest(1)
    of_kv.second(1)
    tick()
    tokens_grad, gain_one_term = order.run(
        norm_back, scalars, tokens, gain_one, grad_residual, [grad_hidden_one], rounded=False
    )
    out_sums.rest(1)
    gain_terms = xor_blocks(jnp.concatenate([gain_one_term, gain_two_term], axis=0), f, 1)
    gain_terms = gain_terms.astype(BF).reshape(2, 4 * n, model // (4 * n)).transpose(1, 0, 2)
    gain_terms = lax.all_to_all(order.at(gain_terms), ("fsdp", "ctx"), 0, 0, tiled=False)
    out_sums.rest()
    out_grad = order.done(added(out_sums.take()))
    tick()
    gate_up_all = order.take(gate_up_all)
    if crossed:
        gate_up_all = gate_up_all.reshape(n, rows, width // tile, 2 * tile)
        gate_grad, up_grad = order.run(
            spread, scalars, [gate_up_all[:, :, s] for s in range(width // tile)], units=units
        )
    else:
        gate_up_all = gate_up_all.reshape(n, rows, 2, 4, units).transpose(2, 1, 3, 0, 4)
        gate_up_all = xor_blocks(gate_up_all, f, 2).reshape(2, rows, n * width).astype(F32)
        gate_grad, up_grad = order.done((gate_up_all[0], gate_up_all[1]))
    query_sums = scatter_rows(of_query.last(BF))
    query_sums.send()
    query_sums.rest(1)
    layer_out = order.done((residual + order.at(y_own).astype(F32)).astype(BF))
    query_sums.rest(1)
    tick()
    kv_sums = scatter_rows(of_kv.last(BF))
    kv_sums.send()
    query_sums.rest(1)
    kv_sums.rest(1)
    query_sums.rest()
    kv_sums.rest(1)
    query_grad = order.done(added(query_sums.take()))
    kv_sums.rest()
    gain_grads = jnp.sum(order.at(gain_terms).astype(F32), axis=0)
    kv_grad = added(kv_sums.take())
    kv_width = key_matrix.shape[1]
    key_grad, value_grad = kv_grad[:, :kv_width], kv_grad[:, kv_width:]
    return (
        layer_out,
        tokens_grad,
        gain_grads[0],
        query_grad,
        key_grad,
        value_grad,
        out_grad,
        gain_grads[1],
        gate_grad,
        up_grad,
        down_grad,
    )


def solution(mesh):
    rows, vector = P(("fsdp", "ctx"), None), P(("fsdp", "ctx"))
    weight = P("fsdp", None)

    def layer(*arrays):
        return body(mesh.shape["ctx"], *arrays)

    return jax.shard_map(
        layer,
        mesh=mesh,
        in_specs=(
            rows, P("fsdp"), weight, weight, weight, weight, P("fsdp"), weight, weight, weight,
            weight, P(), rows,
        ),
        out_specs=(rows, rows, vector, rows, rows, rows, rows, vector, rows, rows, rows),
        check_vma=False,
    )
```

```python
import functools

import jax
import jax.numpy as jnp
from jax import lax
from jax.experimental import pallas as pl
from jax.experimental.pallas import tpu as pltpu
from jax.sharding import PartitionSpec as P

HEAD = 64
NORM_EPS = 1e-05
ROPE_BASE = 500000.0
MASKED = -1e30
VARIANTS = 5
BF = jnp.bfloat16
F32 = jnp.float32
MIB = 2**20


def dot(a, b):
    return jnp.dot(a, b, preferred_element_type=F32)


def dot_nt(a, b):
    return lax.dot_general(a, b, (((1,), (1,)), ((), ())), preferred_element_type=F32)


def fill_bias(sc, bias, own, block, ends_at, ends):
    for j in range(2):
        place = sc[own + j] * block + lax.broadcasted_iota(jnp.int32, bias.shape[1:], 0)
        key = lax.broadcasted_iota(jnp.int32, bias.shape[1:], 1)
        start = jnp.zeros_like(place)
        for s in range(ends):
            end = sc[ends_at + s]
            start = jnp.where(place >= end, end, start)
        bias[j] = jnp.where((key >= start) & (key <= place), 0.0, MASKED)


def fill_keys(sc, chunks, keys, values, block, blocks_at):
    for r, chunk in enumerate(chunks):
        for j in range(2):
            at = pl.multiple_of(sc[blocks_at + 2 * r + j] * block, 16)
            part = chunk[j * block : (j + 1) * block, :]
            for g in range(2):
                keys[g, pl.ds(at, block), :] = part[:, g * HEAD : (g + 1) * HEAD]
                values[g, pl.ds(at, block), :] = part[:, 2 * HEAD + g * HEAD : 2 * HEAD + (g + 1) * HEAD]


def split_heads(ref, out, block, group):
    for g in range(2):
        for j in range(2):
            for h in range(group):
                lane = (g * group + h) * HEAD
                out[g, j, h * block : (h + 1) * block, :] = ref[
                    j * block : (j + 1) * block, lane : lane + HEAD
                ]


def join_heads(out, block, group):
    rows = []
    for j in range(2):
        rows.append(
            jnp.concatenate(
                [out[g, j, h * block : (h + 1) * block, :] for g in range(2) for h in range(group)],
                axis=1,
            )
        )
    return jnp.concatenate(rows, axis=0)


def visible(sc, own, j, block, step):
    return (sc[own + j] * block + block - 1) // step + 1


def forward_kernel(n, group, ends, sc, q_ref, *rest):
    chunks, (o_ref, lse_ref), (bias, keys, values, queries, outs) = (
        rest[:n],
        rest[n : n + 2],
        rest[n + 2 :],
    )
    block = q_ref.shape[0] // 2
    total = keys.shape[1]
    step = total // VARIANTS
    pair = pl.program_id(0)

    @pl.when(pair == 0)
    def _():
        fill_bias(sc, bias, 1, block, 3 + 2 * n, ends)
        lse_ref[...] = jnp.zeros_like(lse_ref)

    fill_keys(sc, chunks, keys, values, block, 3)
    split_heads(q_ref, queries, block, group)

    def one(g, j, length):
        scores = dot_nt(queries[g, j], keys[g, :length, :])
        scores = (scores.reshape(group, block, length) + bias[j, :, :length][None]).reshape(
            group * block, length
        )
        peak = jnp.max(scores, axis=-1, keepdims=True)
        expd = jnp.exp(scores - peak)
        row_total = jnp.sum(expd, axis=-1, keepdims=True)
        mixed = dot(expd.astype(BF), values[g, :length, :])
        outs[g, j] = mixed / row_total
        lse = peak + jnp.log(row_total)
        lane = lax.broadcasted_iota(jnp.int32, (block, lse_ref.shape[1]), 1)
        rows = pl.ds(pl.multiple_of(j * block, 16), block)
        kept = lse_ref[rows, :]
        for h in range(group):
            kept = jnp.where(
                lane == (pair * 2 + g) * group + h, lse[h * block : (h + 1) * block], kept
            )
        lse_ref[rows, :] = kept

    def both(at, carry):
        g, j = at // 2, at % 2
        count = visible(sc, 1, j, block, step)
        for v in range(1, VARIANTS + 1):
            pl.when(count == v)(functools.partial(one, g, j, v * step))
        return carry

    lax.fori_loop(0, 4, both, 0)
    o_ref[...] = join_heads(outs, block, group).astype(o_ref.dtype)


def attention_forward(scalars, queries, chunks, ends):
    n = len(chunks)
    rows, width = queries.shape
    group = width // HEAD // 8
    block, total = rows // 2, rows * n
    pairs = 4
    return pl.pallas_call(
        functools.partial(forward_kernel, n, group, ends),
        grid_spec=pltpu.PrefetchScalarGridSpec(
            num_scalar_prefetch=1,
            grid=(pairs,),
            in_specs=[pl.BlockSpec((rows, width // pairs), lambda p, sc: (0, p))]
            + [pl.BlockSpec((rows, 4 * HEAD), lambda p, sc: (0, p))] * n,
            out_specs=[
                pl.BlockSpec((rows, width // pairs), lambda p, sc: (0, p ^ sc[0])),
                pl.BlockSpec((rows, 128), lambda p, sc: (0, 0)),
            ],
            scratch_shapes=[
                pltpu.VMEM((2, block, total), F32),
                pltpu.VMEM((2, total, HEAD), BF),
                pltpu.VMEM((2, total, HEAD), BF),
                pltpu.VMEM((2, 2, group * block, HEAD), BF),
                pltpu.VMEM((2, 2, group * block, HEAD), F32),
            ],
        ),
        out_shape=[
            jax.ShapeDtypeStruct((rows, width), BF),
            jax.ShapeDtypeStruct((rows, 128), F32),
        ],
        compiler_params=pltpu.CompilerParams(vmem_limit_bytes=48 * 2**20),
        cost_estimate=cost(18),
        name="attention_forward",
    )(scalars, queries, *chunks)


def backward_kernel(n, group, ends, first, sc, q_ref, do_ref, lse_ref, cos_ref, sin_ref, *rest):
    chunks, (dq_ref, dkv_ref), scratch = rest[:n], rest[n : n + 2], rest[n + 2 :]
    bias, keys, values, queries, grads, outs, dkeys, dvalues, flat = scratch
    block = q_ref.shape[0] // 2
    total = keys.shape[1]
    step = total // VARIANTS
    pair = pl.program_id(0) + first

    @pl.when(pair == first)
    def _():
        fill_bias(sc, bias, 1, block, 3 + 2 * n, ends)

    fill_keys(sc, chunks, keys, values, block, 3)
    split_heads(q_ref, queries, block, group)
    split_heads(do_ref, grads, block, group)
    dkeys[...] = jnp.zeros_like(dkeys)
    dvalues[...] = jnp.zeros_like(dvalues)

    def one(g, j, length):
        query, grad = queries[g, j], grads[g, j]
        key, value = keys[g, :length, :], values[g, :length, :]
        rows = pl.ds(pl.multiple_of(j * block, 16), block)
        kept = lse_ref[rows, :]
        lane = lax.broadcasted_iota(jnp.int32, kept.shape, 1)
        lse = jnp.concatenate(
            [
                jnp.sum(
                    jnp.where(lane == (pair * 2 + g) * group + h, kept, 0.0), axis=1, keepdims=True
                )
                for h in range(group)
            ],
            axis=0,
        )
        scores = dot_nt(query, key)
        scores = (scores.reshape(group, block, length) + bias[j, :, :length][None]).reshape(
            group * block, length
        )
        prob = jnp.exp(scores - lse)
        dprob = dot_nt(grad, value)
        weighted = prob * dprob
        row_dot = jnp.sum(weighted, axis=-1, keepdims=True)
        dscore = (weighted - prob * row_dot).astype(BF)
        outs[g, j] = dot(dscore, key)
        dkeys[g, :, :length] += dot(query.T, dscore)
        dvalues[g, :, :length] += dot(grad.T, prob.astype(BF))

    def both(at, carry):
        g, j = at // 2, at % 2
        count = visible(sc, 1, j, block, step)
        for v in range(1, VARIANTS + 1):
            pl.when(count == v)(functools.partial(one, g, j, v * step))
        return carry

    lax.fori_loop(0, 4, both, 0)
    dq = join_heads(outs, block, group) * (1.0 / 8.0)
    cosine, sine = cos_ref[...], sin_ref[...]
    low = lax.broadcasted_iota(jnp.int32, cosine.shape, 1) % HEAD < HEAD // 2
    for t in range(dq.shape[1] // 128):
        part = dq[:, t * 128 : (t + 1) * 128]
        turned = jnp.where(low, pltpu.roll(part, 96, 1), pltpu.roll(part, 32, 1))
        dq_ref[:, t * 128 : (t + 1) * 128] = (part * cosine - turned * sine).astype(dq_ref.dtype)
    flat[:, : 2 * HEAD] = jnp.concatenate([dkeys[0], dkeys[1]], axis=0).T
    flat[:, 2 * HEAD :] = jnp.concatenate([dvalues[0], dvalues[1]], axis=0).T
    for r in range(2 * n):
        at = pl.multiple_of(sc[3 + r] * block, 16)
        dkv_ref[r * block : (r + 1) * block, :] = flat[pl.ds(at, block), :].astype(dkv_ref.dtype)


def attention_backward(scalars, queries, grads, lse, cosine, sine, chunks, ends, pairs):
    n = len(chunks)
    rows, width = queries.shape
    group = width // HEAD // 8
    block, total = rows // 2, rows * n
    first, steps = pairs
    whole = pl.BlockSpec((rows, 128), lambda p, sc: (0, 0))
    wide = pl.BlockSpec((rows, width // 4), lambda p, sc: (0, p + first))
    return pl.pallas_call(
        functools.partial(backward_kernel, n, group, ends, first),
        grid_spec=pltpu.PrefetchScalarGridSpec(
            num_scalar_prefetch=1,
            grid=(steps,),
            in_specs=[
                wide,
                pl.BlockSpec((rows, width // 4), lambda p, sc: (0, (p + first) ^ sc[0])),
                whole,
                whole,
                whole,
            ]
            + [pl.BlockSpec((rows, 4 * HEAD), lambda p, sc: (0, p + first))] * n,
            out_specs=[
                pl.BlockSpec((rows, width // 4), lambda p, sc: (0, p)),
                pl.BlockSpec((total, 4 * HEAD), lambda p, sc: (0, p)),
            ],
            scratch_shapes=[
                pltpu.VMEM((2, block, total), F32),
                pltpu.VMEM((2, total, HEAD), BF),
                pltpu.VMEM((2, total, HEAD), BF),
                pltpu.VMEM((2, 2, group * block, HEAD), BF),
                pltpu.VMEM((2, 2, group * block, HEAD), BF),
                pltpu.VMEM((2, 2, group * block, HEAD), F32),
                pltpu.VMEM((2, HEAD, total), F32),
                pltpu.VMEM((2, HEAD, total), F32),
                pltpu.VMEM((total, 4 * HEAD), F32),
            ],
        ),
        out_shape=[
            jax.ShapeDtypeStruct((rows, steps * width // 4), BF),
            jax.ShapeDtypeStruct((total, steps * 4 * HEAD), BF),
        ],
        compiler_params=pltpu.CompilerParams(vmem_limit_bytes=56 * 2**20),
        cost_estimate=cost(26),
        name="attention_backward",
    )(scalars, queries, grads, lse, cosine, sine, *chunks)


def params(mib):
    return pltpu.CompilerParams(vmem_limit_bytes=mib * MIB)


def cost(micros):
    return pl.CostEstimate(flops=int(micros * 1e7), bytes_accessed=0, transcendentals=0)


def row_scale(values):
    return lax.rsqrt(jnp.mean(values * values, axis=-1, keepdims=True) + NORM_EPS)


def quarter(f, d, size):
    return pl.ds(pl.multiple_of((f ^ d) * size, size), size)


def norm_kernel(f_ref, x_ref, gain_ref, h_ref):
    inverse = row_scale(x_ref[...].astype(F32))
    size = x_ref.shape[1] // 4
    for d in range(4):
        part = x_ref[:, quarter(f_ref[0], d, size)].astype(F32) * inverse
        h_ref[:, d * size : (d + 1) * size] = (
            part * gain_ref[:, d * size : (d + 1) * size]
        ).astype(BF)


def smem():
    return pl.BlockSpec(memory_space=pltpu.SMEM)


def vmem():
    return pl.BlockSpec(memory_space=pltpu.VMEM)


def norm_rows(scalars, rows, gain):
    return pl.pallas_call(
        norm_kernel,
        in_specs=[smem(), vmem(), vmem()],
        out_specs=vmem(),
        out_shape=jax.ShapeDtypeStruct(rows.shape, BF),
        compiler_params=params(32),
        cost_estimate=cost(1),
        name="norm_rows",
    )(scalars, rows, gain)


def project_kernel(scale, turned_tiles, x_ref, cos_ref, sin_ref, *refs):
    weights, out_ref = refs[:-1], refs[-1]
    size = x_ref.shape[1] // 4
    parts = []
    for at in range(0, len(weights), 4):
        parts.append(
            sum(
                dot(x_ref[:, d * size : (d + 1) * size], w[...])
                for d, w in enumerate(weights[at : at + 4])
            )
        )
    cosine, sine = cos_ref[...], sin_ref[...]
    low = lax.broadcasted_iota(jnp.int32, cosine.shape, 1) % HEAD < HEAD // 2
    tiles = [p[:, t * 128 : (t + 1) * 128] for p in parts for t in range(p.shape[1] // 128)]
    for t, part in enumerate(tiles):
        if t < turned_tiles:
            turned = jnp.where(low, pltpu.roll(part, 96, 1), pltpu.roll(part, 32, 1))
            part = part * cosine + turned * sine
        part = part.astype(BF)
        if scale != 1.0:
            part = (part.astype(F32) * scale).astype(BF)
        out_ref[:, t * 128 : (t + 1) * 128] = part


def project(rows, cosine, sine, weights, turned_tiles, scale, micros):
    count, depth = rows.shape
    size, width = weights[0][0].shape
    part = 256 // len(weights)
    whole = lambda a: pl.BlockSpec(a.shape, lambda j: (0, 0))
    return pl.pallas_call(
        functools.partial(project_kernel, scale, turned_tiles),
        grid=(width // part,),
        in_specs=[whole(rows), whole(cosine), whole(sine)]
        + [pl.BlockSpec((size, part), lambda j: (0, j))] * (4 * len(weights)),
        out_specs=pl.BlockSpec((count, 256), lambda j: (0, j)),
        out_shape=jax.ShapeDtypeStruct((count, width * len(weights)), BF),
        compiler_params=params(32),
        cost_estimate=cost(micros),
        name="project",
    )(rows, cosine, sine, *[w for shards in weights for w in shards])


def out_kernel(f_ref, o_ref, x_ref, gain_ref, w0, w1, w2, w3, r_ref, h_ref):
    size = o_ref.shape[1] // 4
    tile = w0.shape[1]
    total = sum(
        dot(o_ref[:, d * size : (d + 1) * size], w[...]) for d, w in enumerate((w0, w1, w2, w3))
    )
    at = pl.ds(pl.multiple_of(pl.program_id(0) * tile, tile), tile)
    r_ref[:, at] = x_ref[:, at].astype(F32) + total

    @pl.when(pl.program_id(0) == pl.num_programs(0) - 1)
    def _():
        norm_kernel(f_ref, r_ref, gain_ref, h_ref)


def out_project(scalars, mixed, tokens, gain, weights):
    count, depth = mixed.shape
    size, width = weights[0].shape
    whole = lambda a: pl.BlockSpec(a.shape, lambda j: (0, 0))
    return pl.pallas_call(
        out_kernel,
        grid=(width // 256,),
        in_specs=[smem(), whole(mixed), whole(tokens), whole(gain)]
        + [pl.BlockSpec((size, 256), lambda j: (0, j))] * 4,
        out_specs=[whole(tokens), whole(tokens)],
        out_shape=[
            jax.ShapeDtypeStruct((count, width), F32),
            jax.ShapeDtypeStruct((count, width), BF),
        ],
        compiler_params=params(32),
        cost_estimate=cost(6),
        name="out_project",
    )(scalars, mixed, tokens, gain, *weights)


def norm_back_kernel(wide, f_ref, x_ref, gain_ref, base_ref, *rest):
    terms, outs = rest[:-wide], rest[-wide:]
    x = x_ref[...].astype(F32)
    inverse = row_scale(x)
    size = x_ref.shape[1] // 4
    f = f_ref[0]
    grads, normed = [], []
    dot_sum = 0.0
    for d in range(4):
        cols = slice(d * size, (d + 1) * size)
        grad = sum(t[:, cols].astype(F32) for t in terms)
        part = x_ref[:, quarter(f, d, size)].astype(F32) * inverse
        outs[1][:, cols] = jnp.sum(grad * part, axis=0, keepdims=True)
        grad = grad * gain_ref[:, cols]
        dot_sum += jnp.sum(grad * part, axis=-1, keepdims=True)
        grads.append(grad)
        normed.append(part)
    mean = dot_sum / x_ref.shape[1]
    for d in range(4):
        at = quarter(f, d, size)
        value = base_ref[:, at].astype(F32) + inverse * (grads[d] - normed[d] * mean)
        outs[0][:, at] = value
        if wide == 3:
            outs[2][:, at] = value.astype(BF)


def norm_back(scalars, rows, gain, base, terms, rounded):
    wide = 3 if rounded else 2
    shapes = [
        jax.ShapeDtypeStruct(rows.shape, F32),
        jax.ShapeDtypeStruct((1, rows.shape[1]), F32),
        jax.ShapeDtypeStruct(rows.shape, BF),
    ][:wide]
    return pl.pallas_call(
        functools.partial(norm_back_kernel, wide),
        in_specs=[smem()] + [vmem()] * (3 + len(terms)),
        out_specs=[vmem()] * wide,
        out_shape=shapes,
        compiler_params=params(40),
        cost_estimate=cost(2),
        name="norm_back",
    )(scalars, rows, gain, base, *terms)


def back_kernel(pairs, based, *refs):
    out_ref = refs[-1]
    step = pl.program_id(0)
    tile = refs[pairs].shape[0]
    size = tile * pl.num_programs(0)
    for d in range(4):
        at = pl.ds(pl.multiple_of(d * size + step * tile, tile), tile)
        total = sum(dot_nt(refs[i][...], refs[pairs + 4 * i + d][...]) for i in range(pairs))
        if based:
            total += refs[5 * pairs][:, at]
        out_ref[:, at] = total.astype(out_ref.dtype)


def back_project(rows, weights, kind, micros, base=None):
    count = rows[0].shape[0]
    size = weights[0][0].shape[0]
    whole = pl.BlockSpec((count, 4 * size), lambda j: (0, 0))
    extra = [] if base is None else [base]
    return pl.pallas_call(
        functools.partial(back_kernel, len(rows), base is not None),
        grid=(2,),
        in_specs=[pl.BlockSpec(r.shape, lambda j: (0, 0)) for r in rows]
        + [pl.BlockSpec((size // 2, w.shape[1]), lambda j: (j, 0)) for ws in weights for w in ws]
        + [whole] * len(extra),
        out_specs=whole,
        out_shape=jax.ShapeDtypeStruct((count, 4 * size), kind),
        compiler_params=params(40 if len(rows) == 1 else 60),
        cost_estimate=cost(micros),
        name="back_project",
    )(*rows, *[w for ws in weights for w in ws], *extra)


def cross(value):
    half = value.shape[1] // 2
    return jnp.concatenate([value[:, half:], value[:, :half]], axis=1)


def feed_kernel(m, kept, crossed, *refs):
    hidden, grads = refs[:m], refs[m : 2 * m]
    gates, ups = refs[2 * m : 2 * m + 4], refs[2 * m + 4 : 2 * m + 8]
    down_ref = refs[2 * m + 8]
    outs = refs[2 * m + 9 + kept :]
    rows_h, rows_dy, act_ref, dgu_ref, dh_ref, h_s, dy_s, dh_s = outs
    step = pl.program_id(0)
    count = hidden[0].shape[0]
    size = gates[0].shape[0]
    tile = gates[0].shape[1]

    @pl.when(step == 0)
    def _():
        for i in range(m):
            at = slice(i * count, (i + 1) * count)
            h_s[at], dy_s[at] = hidden[i][...], grads[i][...]
            rows_h[at], rows_dy[at] = hidden[i][...], grads[i][...]

    def ahead(weights):
        parts = [dot(h_s[:, d * size : (d + 1) * size], w[...]) for d, w in enumerate(weights)]
        if not crossed:
            return sum(parts)
        return parts[0] + parts[2] + cross(parts[1] + parts[3])

    gate, up = ahead(gates), ahead(ups)
    sig = jax.nn.sigmoid(gate)
    silu = gate * sig
    act_ref[...] = (silu * up).astype(BF)
    grad_act = dot_nt(dy_s[...], down_ref[...])
    grad_gate = (grad_act * up * sig * (1.0 + gate * (1.0 - sig))).astype(BF)
    grad_up = (grad_act * silu).astype(BF)
    dgu_ref[:, :tile] = grad_gate
    dgu_ref[:, tile:] = grad_up
    pairs = [(grad_gate, grad_up)] * 4
    if crossed:
        pairs[1] = pairs[3] = (cross(grad_gate), cross(grad_up))
    last = pl.num_programs(0) - 1
    for d in range(4):
        cols = slice(d * size, (d + 1) * size)
        dh = dot_nt(pairs[d][0], gates[d][...]) + dot_nt(pairs[d][1], ups[d][...])

        @pl.when(step == 0)
        def _():
            dh_s[:, cols] = dh

        @pl.when(step > 0)
        def _():
            dh_s[:, cols] += dh

    @pl.when(step == last)
    def _():
        dh_ref[...] = dh_s[...].astype(BF)


def feed_tile(units):
    crossed = units >= 128
    return (2 * units if crossed else 4 * units), crossed


def feed(hidden, grads, gate, up, down, slot, kept, n):
    m = len(hidden)
    count, depth = hidden[0].shape
    width = down.shape[0]
    tile, crossed = feed_tile(width // 4)
    steps = width // tile
    rows = m * count
    size = depth // 4

    def shard(d):
        flip = d >> 1 if crossed else 0
        return pl.BlockSpec((size, tile), lambda e: (0, e ^ flip))

    chunk = pl.BlockSpec((count, depth), lambda e: (0, 0))
    block = pl.BlockSpec((rows, depth), lambda e: (slot, 0))
    shapes = [
        jax.ShapeDtypeStruct((n * count, depth), BF),
        jax.ShapeDtypeStruct((n * count, depth), BF),
        jax.ShapeDtypeStruct((n * count, width), BF),
        jax.ShapeDtypeStruct((n * count, 2 * width), BF),
        jax.ShapeDtypeStruct((rows, depth), BF),
    ]
    first = 2 * m + 9
    *kept, dh = pl.pallas_call(
        functools.partial(feed_kernel, m, len(kept), crossed),
        grid=(steps,),
        in_specs=[chunk] * (2 * m)
        + [shard(d) for d in range(4)] * 2
        + [pl.BlockSpec((tile, depth), lambda e: (e, 0))]
        + [pl.BlockSpec(memory_space=pl.ANY)] * len(kept),
        out_specs=[
            block,
            block,
            pl.BlockSpec((rows, tile), lambda e: (slot, e)),
            pl.BlockSpec((rows, 2 * tile), lambda e: (slot, e)),
            pl.BlockSpec((rows, depth), lambda e: (0, 0)),
        ],
        scratch_shapes=[pltpu.VMEM((rows, depth), BF)] * 2 + [pltpu.VMEM((rows, depth), F32)],
        out_shape=shapes,
        input_output_aliases={first + i: i for i in range(len(kept))},
        compiler_params=params(48),
        cost_estimate=cost(8 + 4 * m),
        name="feed",
    )(*hidden, *grads, *gate, *up, down, *kept)
    return kept, [dh[i * count : (i + 1) * count] for i in range(m)]


def down_kernel(sc, act_ref, down_ref, y_ref):
    y_ref[...] = dot(act_ref[...], down_ref[...]).astype(BF)


def down_rows(scalars, act, down, n):
    count = act.shape[0] // n
    at = scalars.shape[0] - n
    return pl.pallas_call(
        down_kernel,
        grid_spec=pltpu.PrefetchScalarGridSpec(
            num_scalar_prefetch=1,
            grid=(n,),
            in_specs=[
                pl.BlockSpec((count, act.shape[1]), lambda i, sc: (i, 0)),
                pl.BlockSpec(down.shape, lambda i, sc: (0, 0)),
            ],
            out_specs=pl.BlockSpec((count, down.shape[1]), lambda i, sc: (sc[at + i], 0)),
        ),
        out_shape=jax.ShapeDtypeStruct((n * count, down.shape[1]), BF),
        compiler_params=params(32),
        cost_estimate=cost(12),
        name="down_rows",
    )(scalars, act, down)


def place_kernel(sc, *refs):
    out = refs[-1]
    count = refs[0].shape[0]
    for i, part in enumerate(refs[:-1]):
        out[pl.ds(pl.multiple_of(sc[i] * count, count), count), :] = part[...]


def place_rows(places, parts):
    count, width = parts[0].shape
    return pl.pallas_call(
        place_kernel,
        in_specs=[smem()] + [vmem()] * len(parts),
        out_specs=vmem(),
        out_shape=jax.ShapeDtypeStruct((count * len(parts), width), parts[0].dtype),
        compiler_params=params(24),
        cost_estimate=cost(2),
        name="place_rows",
    )(places, *parts)


def tn_kernel(adds, outs, left_ref, right_ref, *refs):
    turned = refs[-1]
    i, j = pl.program_id(0), pl.program_id(1)

    @pl.when(j == 0)
    def _():
        turned[...] = left_ref[...].T

    total = dot(turned[...], right_ref[...])
    for (low, high, crossed), extra in zip(adds, refs):
        extra = extra[...].astype(F32)
        if crossed:
            extra = cross(extra)
        if low is not None:
            extra = jnp.where((j >= low) & (j < high), extra, 0.0)
        total += extra
    for (row, low, high), out in zip(outs, refs[len(adds) :]):

        @pl.when((i == row) & (j >= low) & (j < high))
        def _():
            out[...] = total.astype(out.dtype)


def tn_blocks(left, right, blocks, kind, micros, adds=(), pieces=1):
    rows, depth = left.shape
    size, width = depth // 4, right.shape[1]
    tile = min(width, 512)
    steps = width // tile
    pieces = min(pieces, steps)
    if size % 128:
        result = []
        for block in blocks:
            total = lax.dot_general(
                left[:, block * size : (block + 1) * size],
                right,
                (((0,), (0,)), ((), ())),
                preferred_element_type=F32,
            )
            for array, part, parts, _, _ in adds:
                at = part * (width // parts)
                total = total.at[:, at : at + width // parts].add(array.astype(F32))
            result.append(jnp.split(total.astype(kind), pieces, axis=1))
        return result
    first = blocks[0]
    stride = blocks[1] - first if len(blocks) > 1 else 0

    def window(part, parts):
        count = max(1, steps // parts)
        return part * count, (part + 1) * count

    def added_spec(part, parts, flip):
        low, high = window(part, parts)
        if parts == 1:
            return pl.BlockSpec((size, tile), lambda i, j: (0, j ^ flip))
        return pl.BlockSpec((size, tile), lambda i, j: (0, jnp.clip(j - low, 0, high - low - 1)))

    def out_spec(row, low, high):
        def index(i, j):
            at = jnp.clip(j - low, 0, high - low - 1)
            return (0, jnp.where(i < row, 0, jnp.where(i > row, high - low - 1, at)))

        return pl.BlockSpec((size, tile), index)

    windows = [
        (*(window(part, parts) if parts > 1 and steps > 1 else (None, None)), crossed)
        for _, part, parts, _, crossed in adds
    ]
    outs = [(row, *window(piece, pieces)) for row in range(len(blocks)) for piece in range(pieces)]
    result = pl.pallas_call(
        functools.partial(tn_kernel, windows, outs),
        grid=(len(blocks), steps),
        in_specs=[
            pl.BlockSpec((rows, size), lambda i, j: (0, first + stride * i)),
            pl.BlockSpec((rows, tile), lambda i, j: (0, j)),
        ]
        + [added_spec(part, parts, flip) for _, part, parts, flip, _ in adds],
        out_specs=[out_spec(*out) for out in outs],
        out_shape=[jax.ShapeDtypeStruct((size, width // pieces), kind)] * len(outs),
        scratch_shapes=[pltpu.VMEM((size, rows), BF)],
        compiler_params=params(32),
        cost_estimate=cost(micros),
        name="tn_blocks",
    )(left, right, *[a[0] for a in adds])
    return [list(result[row * pieces : (row + 1) * pieces]) for row in range(len(blocks))]


def spread_kernel(units, tile, f_ref, all_ref, *outs):
    span = outs[0].shape[1] // 4
    c = pl.program_id(0)
    for e in range(4):
        step, at = divmod(e * units, tile)
        start = (f_ref[0] ^ e) * span + c * units
        for part in range(2):
            low = (2 * step + part) * tile + at
            value = all_ref[0, :, low : low + units].astype(F32)
            outs[part][:, pl.ds(pl.multiple_of(start, units), units)] = value


def spread(scalars, gathered, units, tile):
    n, rows, _ = gathered.shape
    width = 4 * n * units
    return pl.pallas_call(
        functools.partial(spread_kernel, units, tile),
        grid=(n,),
        in_specs=[smem(), pl.BlockSpec((1, *gathered.shape[1:]), lambda i: (i, 0, 0))],
        out_specs=[pl.BlockSpec((rows, width), lambda i: (0, 0))] * 2,
        out_shape=[jax.ShapeDtypeStruct((rows, width), F32)] * 2,
        compiler_params=params(32),
        cost_estimate=cost(4),
        name="spread",
    )(scalars, gathered)


def swap_fsdp(value, d):
    return lax.ppermute(value, "fsdp", [(i, i ^ d) for i in range(4)])


def after(value, *others):
    return lax.optimization_barrier((value, others))[0] if others else value


def gather_fsdp(shard):
    across = swap_fsdp(shard, 2)
    return [shard, swap_fsdp(shard, 1), across, swap_fsdp(across, 1)]


def xor_blocks(value, f, axis):
    size = value.shape[axis] // 4
    return jnp.concatenate(
        [lax.dynamic_slice_in_dim(value, (f ^ d) * size, size, axis) for d in range(4)], axis=axis
    )


def swap_cols(value, d, parts):
    width = value.shape[1] // (4 * parts)
    return jnp.concatenate(
        [
            value[:, (p * 4 + (e ^ d)) * width : (p * 4 + (e ^ d) + 1) * width]
            for p in range(parts)
            for e in range(4)
        ],
        axis=1,
    )


def ring_index(place, n):
    place = place % n
    return jnp.where(place < n // 2, 2 * place, 2 * (n - 1 - place) + 1)


def ring_shift(value, step, n):
    order = list(range(0, n, 2)) + list(range(n - 1, 0, -2))
    return lax.ppermute(value, "ctx", [(order[i], order[(i + step) % n]) for i in range(n)])


class Order:
    def __init__(self):
        self.last = ()

    def at(self, value):
        return after(value, *self.last)

    def done(self, value):
        self.last = (value,)
        return value

    def take(self, value):
        return self.done(self.at(value))

    def run(self, function, *args, **kwargs):
        return self.done(function(*self.at(args), **kwargs))


class Gather:
    def __init__(self, order, own, n):
        self.order, self.n, self.half, self.step = order, n, n // 2, 0
        self.chunks = {0: own}
        self.now = (own, own)
        self.width = own.shape[1] // 2

    def send(self):
        if self.step == self.half:
            return
        self.step += 1
        right, left = self.now
        if self.step == self.half:
            right, left = right[:, : self.width], left[:, self.width :]
        self.now = (ring_shift(right, 1, self.n), ring_shift(left, -1, self.n))

    def take(self):
        if self.half in self.chunks:
            return
        self.now = right, left = self.order.take(self.now)
        if self.step == self.half:
            self.chunks[self.half] = jnp.concatenate([right, left], axis=1)
        else:
            self.chunks[-self.step], self.chunks[self.step] = right, left

    def rest(self, hops=None):
        while self.step < self.half and hops != 0:
            self.take()
            self.send()
            hops = hops and hops - 1
        return self


class Scatter:
    def __init__(self, order, contrib, n):
        self.order, self.n, self.half, self.step = order, n, n // 2, 0
        self.contrib = contrib
        far = contrib(self.half)
        self.width = far.shape[1] // 2
        self.now = (far[:, : self.width].astype(BF), far[:, self.width :].astype(BF))

    def send(self):
        self.step += 1
        right, left = self.now
        self.now = (ring_shift(right, 1, self.n), ring_shift(left, -1, self.n))

    def take(self):
        self.now = got = self.order.take(self.now)
        r = self.half - self.step
        if r == 0:
            return (self.contrib(0), *got)
        got = [v.astype(F32) for v in got]
        width = self.width
        ahead, behind = self.contrib(r).astype(F32), self.contrib(-r).astype(F32)
        if self.step == 1:
            ahead = jnp.concatenate([ahead[:, :width] + got[0], ahead[:, width:]], axis=1)
            behind = jnp.concatenate([behind[:, :width], behind[:, width:] + got[1]], axis=1)
        else:
            ahead, behind = ahead + got[0], behind + got[1]
        self.now = self.order.done((ahead.astype(BF), behind.astype(BF)))

    def rest(self, hops=None):
        while self.step < self.half and hops != 0:
            self.take()
            self.send()
            hops = hops and hops - 1
        return self


def added(terms):
    return sum(t.astype(F32) for t in terms)


def deinterleave(both):
    runs = range(both.shape[1] // 256)
    return tuple(
        jnp.concatenate([both[:, p * 256 + o : p * 256 + o + 128] for p in runs], axis=1)
        for o in (0, 128)
    )


def turn_tables(block_ids, block, ends, starts):
    place = (block_ids[:, None] * block + jnp.arange(block, dtype=jnp.int32)[None, :]).reshape(-1)
    begin = jnp.max(jnp.where(place[:, None] >= starts[None, :], starts[None, :], 0), axis=1)
    freqs = ROPE_BASE ** (-(jnp.arange(HEAD // 2, dtype=F32) * 2.0 / HEAD))
    angle = (place - begin).astype(F32)[:, None] * freqs[None, :]
    cosine, sine = jnp.cos(angle), jnp.sin(angle)
    return (
        jnp.concatenate([cosine] * 4, axis=1),
        jnp.concatenate([-sine, sine, -sine, sine], axis=1),
    )


def turn_back(values, cosine, sine):
    parts = []
    for p in range(values.shape[1] // 128):
        part = values[:, p * 128 : (p + 1) * 128]
        if p % 2 == 0:
            low = lax.broadcasted_iota(jnp.int32, part.shape, 1) % HEAD < HEAD // 2
            turned = jnp.where(low, jnp.roll(part, -32, axis=1), jnp.roll(part, 32, axis=1))
            part = part * cosine - turned * sine
        parts.append(part)
    return jnp.concatenate(parts, axis=1)


def body(
    n,
    tokens,
    first_gain,
    query_weight,
    key_matrix,
    value_matrix,
    out_weight,
    second_gain,
    gate_weight,
    up_weight,
    down_weight,
    lengths,
    block_order,
    cotangent,
):
    token_rows, model = tokens.shape
    block = token_rows // 2
    c = lax.axis_index("ctx")
    f = lax.axis_index("fsdp")
    place = jnp.where(c % 2 == 0, c // 2, n - 1 - c // 2)
    half = n // 2
    rel = list(range(-(half - 1), half + 1))
    owners = ring_index(place + jnp.asarray(rel, jnp.int32), n)

    own_blocks = lax.dynamic_slice_in_dim(block_order, 2 * c, 2)
    key_blocks = jnp.take(block_order.reshape(n, 2), owners, axis=0).reshape(-1)
    seq_ends = jnp.cumsum(lengths[0])
    count = lengths.shape[1]
    groups = [(-1, 0, 1)] + [(-step, step) for step in range(2, half)] + [(half,)]
    slot_rel = [r for group in (groups[0], groups[-1], *groups[1:-1]) for r in group]
    slot_owners = ring_index(place + jnp.asarray(slot_rel, jnp.int32), n)
    scalars = jnp.concatenate([f[None], own_blocks, key_blocks, seq_ends, slot_owners])
    scalars = scalars.astype(jnp.int32)
    cosine, sine = turn_tables(own_blocks, block, seq_ends, seq_ends - lengths[0])
    order = Order()

    units = gate_weight.shape[1] // (4 * n)
    span = gate_weight.shape[1] // 4
    width = 4 * units

    def own_units(weight):
        return jnp.concatenate(
            [
                lax.dynamic_slice_in_dim(weight, (f ^ e) * span + c * units, units, 1)
                for e in range(4)
            ],
            axis=1,
        )

    gains = gather_fsdp(jnp.stack([first_gain, second_gain]))
    gains = jnp.concatenate(gains, axis=1).astype(F32)
    gain_one, gain_two = gains[:1], gains[1:]
    out_part = out_weight.shape[0] // n
    out_across = swap_fsdp(lax.dynamic_slice_in_dim(out_weight, c * out_part, out_part, 0), 2)
    key_across, value_across = swap_fsdp(key_matrix, 2), swap_fsdp(value_matrix, 2)
    grad_out = Gather(order, cotangent, n)
    grad_out.send()
    key_core, value_core = swap_fsdp(key_matrix, 1), swap_fsdp(value_matrix, 1)
    out_core, query_core = swap_fsdp(out_weight, 1), swap_fsdp(query_weight, 1)
    def across(value):
        return swap_fsdp(order.at(value), 2)

    def shards(own, core, over):
        return [own, core, over, swap_fsdp(over, 1)]

    hidden_one = order.run(norm_rows, scalars, tokens, gain_one)
    out_across = order.take(out_across)
    out_parts = Gather(order, out_across, n)
    out_parts.send()
    weight_k = shards(key_matrix, key_core, order.take(key_across))
    out_parts.rest(1)
    weight_v = shards(value_matrix, value_core, order.take(value_across))
    query_across = across(query_weight)
    gate_own = order.run(own_units, gate_weight)
    up_own = order.run(own_units, up_weight)
    gate_core, up_core = swap_fsdp(gate_own, 1), swap_fsdp(up_own, 1)
    down_own = order.done(lax.dynamic_slice_in_dim(order.at(down_weight), c * units, units, 0))
    down_core = swap_fsdp(down_own, 1)
    out_parts.rest(1)
    grad_out.take()
    kv_own = order.run(project, hidden_one, cosine, sine, [weight_k, weight_v], turned_tiles=1, scale=1.0, micros=4)
    kv = Gather(order, kv_own, n)
    kv.send()
    kv.rest(1)
    kv.rest(1)
    out_parts.take()
    weight_q = shards(query_weight, query_core, order.take(query_across))
    gate_across = across(gate_own)
    kv.rest()
    kv.take()
    out_parts.send()
    kv_chunks = [kv.chunks[r] for r in rel]

    queries = order.run(project, hidden_one, cosine, sine, [weight_q], turned_tiles=2, scale=0.125, micros=7)
    out_parts.rest()
    out_parts.take()
    gate = shards(gate_own, gate_core, order.take(gate_across))
    up_across = across(up_own)
    grad_out.send()
    out_across = order.run(place_rows, owners.astype(jnp.int32), [out_parts.chunks[r] for r in rel])
    weight_o = shards(out_weight, out_core, out_across)
    mixed, lse = order.run(attention_forward, scalars, queries, kv_chunks, ends=count)
    up = shards(up_own, up_core, order.take(up_across))
    down_across = across(down_own)
    grad_out.take()
    residual, hidden_two = order.run(out_project, scalars, mixed, tokens, gain_two, weight_o)
    hidden = Gather(order, hidden_two, n)
    hidden.send()
    hidden.rest(1)
    grad_out.send()
    down = shards(down_own, down_core, order.take(down_across))
    if units < 128:
        gate = [swap_cols(part, d, 1) for d, part in enumerate(gate)]
        up = [swap_cols(part, d, 1) for d, part in enumerate(up)]
    down = order.done(jnp.concatenate(down, axis=0))

    kept, grads_two = [], {}
    for at, group in enumerate(groups):
        slot = slot_rel.index(group[0]) // len(group)
        kept, parts = order.run(
            feed,
            [hidden.chunks[r] for r in group],
            [grad_out.chunks[r] for r in group],
            gate,
            up,
            down,
            slot=slot,
            kept=kept,
            n=n,
        )
        grads_two.update(zip(group, parts))
        if at < half - 1:
            hidden.take()
            hidden.send()
            grad_out.take()
            grad_out.send()

    rows_h, rows_dy, act, grads = kept
    tile, crossed = feed_tile(units)
    class Product:
        def __init__(self, left, right, micros, by_units=False):
            self.left, self.right, self.micros, self.by_units = left, right, micros, by_units

        def kernel(self, blocks, kind, adds=(), pieces=1):
            def run(left, right, *arrays):
                own = [(a, *rest) for a, (_, *rest) in zip(arrays, adds)]
                micros = self.micros * len(blocks)
                return tn_blocks(left, right, blocks, kind, micros, own, pieces)

            return order.run(run, self.left, self.right, *[a for a, *_ in adds])

        def from_partner(self, value, d):
            return swap_cols(value, d, 2) if self.by_units and not crossed else value

        def first(self):
            self.near = [
                [swap_fsdp(piece, 1) for piece in row] for row in self.kernel((1, 3), BF, (), 2)
            ]

        def pieces(self, row):
            turned = self.by_units and crossed
            got = [self.from_partner(v, 1) for v in order.take(self.near[row])]
            return [(v, p, len(got), 0, turned) for p, v in enumerate(got)]

        def second(self, halves=1):
            (mid,) = self.kernel((2,), BF, self.pieces(1), halves)
            self.mid = [swap_fsdp(v, 2) for v in mid]

        def settle(self):
            self.mid = order.take(self.mid)

        def last(self, kind):
            over = [self.from_partner(v, 2) for v in order.at(self.mid)]
            flip = 2 if self.by_units and crossed else 0
            adds = [(v, h, len(over), flip, False) for h, v in enumerate(over)]
            ((whole,),) = self.kernel((0,), kind, self.pieces(0) + adds)
            return whole

    sums = Scatter(order, lambda r: grads_two[r], n)
    sums.send()
    of_down = Product(act, rows_dy, 3)
    of_gate_up = Product(rows_h, grads, 5, True)
    of_gate_up.first()
    sums.rest(1)
    of_down.first()
    of_gate_up.second()
    sums.rest(1)
    y_rows = order.run(down_rows, scalars, act, down, n=n)
    of_down.second()
    sums.rest(1)
    sums.rest()
    grad_hidden_two = sums.take()
    grad_residual, gain_two_term, grad_branch = order.run(
        norm_back, scalars, residual, gain_two, cotangent, grad_hidden_two, rounded=True
    )
    grad_mixed = order.run(back_project, [grad_branch], [weight_o], kind=BF, micros=5)
    of_gate_up.settle()
    gate_up_grad = of_gate_up.last(BF)
    rows = gate_up_grad.shape[0] // n
    gate_up_all = lax.all_to_all(
        gate_up_grad.reshape(n, rows, 2 * width), "ctx", 0, 0, tiled=False
    )
    of_out = Product(mixed, grad_branch, 2)
    of_out.first()

    parts = []

    def attention_part(first):
        parts.append(
            order.run(
                attention_backward,
                scalars,
                queries,
                grad_mixed,
                lse,
                cosine,
                sine,
                kv_chunks,
                ends=count,
                pairs=(first, 2),
            )
        )

    attention_part(0)
    of_down.settle()
    of_out.second()
    attention_part(2)
    gate_up_all = order.take(gate_up_all)
    grad_query = jnp.concatenate([p[0] for p in parts], axis=1)

    def kv_contrib(r):
        start = rel.index(r) * token_rows
        return jnp.concatenate([p[1][start : start + token_rows] for p in parts], axis=1)

    def scatter_rows(within):
        rows = within.shape[0] // n

        def contrib(r):
            start = ring_index(place + r, n) * rows
            return lax.dynamic_slice_in_dim(within, start, rows, 0)

        return Scatter(order, contrib, n)

    grad_kv = Scatter(order, kv_contrib, n)
    grad_kv.send()
    of_query = Product(hidden_one, grad_query, 2)
    of_query.first()
    grad_kv.rest(1)
    grad_hidden_one = order.run(back_project, [grad_query], [weight_q], kind=F32, micros=5)
    of_out.settle()
    grad_kv.rest(1)
    of_query.second()
    grad_kv.rest(1)
    out_within = of_out.last(BF)
    grad_kv.rest()
    grad_kv = added(grad_kv.take())
    y_own = lax.psum_scatter(order.at(y_rows), "ctx", scatter_dimension=0, tiled=True)
    out_sums = scatter_rows(out_within)
    out_sums.send()
    grad_kv = turn_back(grad_kv, cosine, sine).astype(BF)
    grad_key, grad_value = deinterleave(grad_kv)
    grad_kv = jnp.concatenate([grad_key, grad_value], axis=1)
    of_kv = Product(hidden_one, grad_kv, 1.5)
    of_kv.first()
    out_sums.rest(1)
    grad_hidden_one = order.run(
        back_project, [grad_key, grad_value], [weight_k, weight_v], base=grad_hidden_one, kind=F32, micros=3
    )
    out_sums.rest(1)
    tokens_grad, gain_one_term = order.run(
        norm_back, scalars, tokens, gain_one, grad_residual, [grad_hidden_one], rounded=False
    )
    out_sums.rest(1)
    gain_terms = xor_blocks(jnp.concatenate([gain_one_term, gain_two_term], axis=0), f, 1)
    gain_terms = gain_terms.astype(BF).reshape(2, 4 * n, model // (4 * n)).transpose(1, 0, 2)
    gain_terms = lax.all_to_all(gain_terms, ("fsdp", "ctx"), 0, 0, tiled=False)
    of_query.settle()
    of_kv.second()
    query_sums = scatter_rows(of_query.last(BF))
    query_sums.send()
    out_sums.rest()
    out_grad = order.done(added(out_sums.take()))
    query_sums.rest(1)
    if crossed:
        gate_grad, up_grad = order.run(spread, scalars, gate_up_all, units=units, tile=tile)
    else:
        gate_up_all = gate_up_all.reshape(n, rows, 2, 4, units).transpose(2, 1, 3, 0, 4)
        gate_up_all = xor_blocks(gate_up_all, f, 2).reshape(2, rows, n * width).astype(F32)
        gate_grad, up_grad = order.done((gate_up_all[0], gate_up_all[1]))
    gain_terms = order.take(gain_terms)
    of_kv.settle()
    kv_sums = scatter_rows(of_kv.last(BF))
    kv_sums.send()
    query_sums.rest(1)
    down_grad = of_down.last(F32)
    kv_sums.rest(1)
    query_sums.rest()
    kv_sums.rest(1)
    query_grad = order.done(added(query_sums.take()))
    kv_sums.rest()
    layer_out = order.done((residual + order.at(y_own).astype(F32)).astype(BF))
    kv_grad = order.done(added(kv_sums.take()))
    gain_grads = jnp.sum(gain_terms.astype(F32), axis=0)
    kv_width = key_matrix.shape[1]
    key_grad, value_grad = kv_grad[:, :kv_width], kv_grad[:, kv_width:]
    return (
        layer_out,
        tokens_grad,
        gain_grads[0],
        query_grad,
        key_grad,
        value_grad,
        out_grad,
        gain_grads[1],
        gate_grad,
        up_grad,
        down_grad,
    )


def solution(mesh):
    rows, vector = P(("fsdp", "ctx"), None), P(("fsdp", "ctx"))
    weight = P("fsdp", None)

    def layer(*arrays):
        return body(mesh.shape["ctx"], *arrays)

    return jax.shard_map(
        layer,
        mesh=mesh,
        in_specs=(
            rows, P("fsdp"), weight, weight, weight, weight, P("fsdp"), weight, weight, weight,
            weight, P(), rows,
        ),
        out_specs=(rows, rows, vector, rows, rows, rows, rows, vector, rows, rows, rows),
        check_vma=False,
    )
```

```python
import functools

import jax
import jax.numpy as jnp
from jax import lax
from jax.experimental import pallas as pl
from jax.experimental.pallas import tpu as pltpu
from jax.sharding import PartitionSpec as P

HEAD = 64
NORM_EPS = 1e-05
ROPE_BASE = 500000.0
MASKED = -1e30
VARIANTS = 10
BF = jnp.bfloat16
F32 = jnp.float32
MIB = 2**20


def dot(a, b):
    return jnp.dot(a, b, preferred_element_type=F32)


def dot_nt(a, b):
    return lax.dot_general(a, b, (((1,), (1,)), ((), ())), preferred_element_type=F32)


def fill_bias(sc, bias, own, block, ends_at, ends):
    for j in range(2):
        place = sc[own + j] * block + lax.broadcasted_iota(jnp.int32, bias.shape[1:], 0)
        key = lax.broadcasted_iota(jnp.int32, bias.shape[1:], 1)
        start = jnp.zeros_like(place)
        for s in range(ends):
            end = sc[ends_at + s]
            start = jnp.where(place >= end, end, start)
        bias[j] = jnp.where((key >= start) & (key <= place), 0.0, MASKED)


def fill_keys(sc, chunks, keys, values, block, blocks_at):
    for r, chunk in enumerate(chunks):
        for j in range(2):
            at = pl.multiple_of(sc[blocks_at + 2 * r + j] * block, 16)
            part = chunk[j * block : (j + 1) * block, :]
            for g in range(2):
                keys[g, pl.ds(at, block), :] = part[:, g * HEAD : (g + 1) * HEAD]
                values[g, pl.ds(at, block), :] = part[:, 2 * HEAD + g * HEAD : 2 * HEAD + (g + 1) * HEAD]


def split_heads(ref, out, block, group):
    for g in range(2):
        for j in range(2):
            for h in range(group):
                lane = (g * group + h) * HEAD
                out[g, j, h * block : (h + 1) * block, :] = ref[
                    j * block : (j + 1) * block, lane : lane + HEAD
                ]


def join_heads(out, block, group):
    rows = []
    for j in range(2):
        rows.append(
            jnp.concatenate(
                [out[g, j, h * block : (h + 1) * block, :] for g in range(2) for h in range(group)],
                axis=1,
            )
        )
    return jnp.concatenate(rows, axis=0)


def visible(sc, own, j, block, step):
    return (sc[own + j] * block + block - 1) // step + 1


def forward_kernel(n, group, ends, sc, q_ref, *rest):
    chunks, (o_ref, lse_ref), (bias, keys, values, queries, outs) = (
        rest[:n],
        rest[n : n + 2],
        rest[n + 2 :],
    )
    block = q_ref.shape[0] // 2
    total = keys.shape[1]
    step = total // VARIANTS
    pair = pl.program_id(0)

    @pl.when(pair == 0)
    def _():
        fill_bias(sc, bias, 1, block, 3 + 2 * n, ends)
        lse_ref[...] = jnp.zeros_like(lse_ref)

    fill_keys(sc, chunks, keys, values, block, 3)
    split_heads(q_ref, queries, block, group)

    def one(g, j, length):
        scores = dot_nt(queries[g, j], keys[g, :length, :])
        scores = (scores.reshape(group, block, length) + bias[j, :, :length][None]).reshape(
            group * block, length
        )
        peak = jnp.max(scores, axis=-1, keepdims=True)
        expd = jnp.exp(scores - peak)
        row_total = jnp.sum(expd, axis=-1, keepdims=True)
        mixed = dot(expd.astype(BF), values[g, :length, :])
        outs[g, j] = mixed / row_total
        lse = peak + jnp.log(row_total)
        lane = lax.broadcasted_iota(jnp.int32, (block, lse_ref.shape[1]), 1)
        rows = pl.ds(pl.multiple_of(j * block, 16), block)
        kept = lse_ref[rows, :]
        for h in range(group):
            kept = jnp.where(
                lane == (pair * 2 + g) * group + h, lse[h * block : (h + 1) * block], kept
            )
        lse_ref[rows, :] = kept

    def both(at, carry):
        g, j = at // 2, at % 2
        count = visible(sc, 1, j, block, step)
        for v in range(1, VARIANTS + 1):
            pl.when(count == v)(functools.partial(one, g, j, v * step))
        return carry

    lax.fori_loop(0, 4, both, 0)
    o_ref[...] = join_heads(outs, block, group).astype(o_ref.dtype)


def attention_forward(scalars, queries, chunks, ends):
    n = len(chunks)
    rows, width = queries.shape
    group = width // HEAD // 8
    block, total = rows // 2, rows * n
    pairs = 4
    return pl.pallas_call(
        functools.partial(forward_kernel, n, group, ends),
        grid_spec=pltpu.PrefetchScalarGridSpec(
            num_scalar_prefetch=1,
            grid=(pairs,),
            in_specs=[pl.BlockSpec((rows, width // pairs), lambda p, sc: (0, p))]
            + [pl.BlockSpec((rows, 4 * HEAD), lambda p, sc: (0, p))] * n,
            out_specs=[
                pl.BlockSpec((rows, width // pairs), lambda p, sc: (0, p ^ sc[0])),
                pl.BlockSpec((rows, 128), lambda p, sc: (0, 0)),
            ],
            scratch_shapes=[
                pltpu.VMEM((2, block, total), F32),
                pltpu.VMEM((2, total, HEAD), BF),
                pltpu.VMEM((2, total, HEAD), BF),
                pltpu.VMEM((2, 2, group * block, HEAD), BF),
                pltpu.VMEM((2, 2, group * block, HEAD), F32),
            ],
        ),
        out_shape=[
            jax.ShapeDtypeStruct((rows, width), BF),
            jax.ShapeDtypeStruct((rows, 128), F32),
        ],
        compiler_params=pltpu.CompilerParams(vmem_limit_bytes=48 * 2**20),
        cost_estimate=cost(18),
        name="attention_forward",
    )(scalars, queries, *chunks)


def backward_kernel(n, group, ends, first, sc, q_ref, do_ref, lse_ref, cos_ref, sin_ref, *rest):
    chunks, (dq_ref, dkv_ref), scratch = rest[:n], rest[n : n + 2], rest[n + 2 :]
    bias, keys, values, queries, grads, outs, dkeys, dvalues, flat = scratch
    block = q_ref.shape[0] // 2
    total = keys.shape[1]
    step = total // VARIANTS
    pair = pl.program_id(0) + first

    @pl.when(pair == first)
    def _():
        fill_bias(sc, bias, 1, block, 3 + 2 * n, ends)

    fill_keys(sc, chunks, keys, values, block, 3)
    split_heads(q_ref, queries, block, group)
    split_heads(do_ref, grads, block, group)
    dkeys[...] = jnp.zeros_like(dkeys)
    dvalues[...] = jnp.zeros_like(dvalues)

    def one(g, j, length):
        query, grad = queries[g, j], grads[g, j]
        key, value = keys[g, :length, :], values[g, :length, :]
        rows = pl.ds(pl.multiple_of(j * block, 16), block)
        kept = lse_ref[rows, :]
        lane = lax.broadcasted_iota(jnp.int32, kept.shape, 1)
        lse = jnp.concatenate(
            [
                jnp.sum(
                    jnp.where(lane == (pair * 2 + g) * group + h, kept, 0.0), axis=1, keepdims=True
                )
                for h in range(group)
            ],
            axis=0,
        )
        scores = dot_nt(query, key)
        scores = (scores.reshape(group, block, length) + bias[j, :, :length][None]).reshape(
            group * block, length
        )
        prob = jnp.exp(scores - lse)
        dprob = dot_nt(grad, value)
        weighted = prob * dprob
        row_dot = jnp.sum(weighted, axis=-1, keepdims=True)
        dscore = (weighted - prob * row_dot).astype(BF)
        outs[g, j] = dot(dscore, key)
        dkeys[g, :, :length] += dot(query.T, dscore)
        dvalues[g, :, :length] += dot(grad.T, prob.astype(BF))

    def both(at, carry):
        g, j = at // 2, at % 2
        count = visible(sc, 1, j, block, step)
        for v in range(1, VARIANTS + 1):
            pl.when(count == v)(functools.partial(one, g, j, v * step))
        return carry

    lax.fori_loop(0, 4, both, 0)
    dq = join_heads(outs, block, group) * (1.0 / 8.0)
    cosine, sine = cos_ref[...], sin_ref[...]
    low = lax.broadcasted_iota(jnp.int32, cosine.shape, 1) % HEAD < HEAD // 2
    for t in range(dq.shape[1] // 128):
        part = dq[:, t * 128 : (t + 1) * 128]
        turned = jnp.where(low, pltpu.roll(part, 96, 1), pltpu.roll(part, 32, 1))
        dq_ref[:, t * 128 : (t + 1) * 128] = (part * cosine - turned * sine).astype(dq_ref.dtype)
    flat[:, : 2 * HEAD] = jnp.concatenate([dkeys[0], dkeys[1]], axis=0).T
    flat[:, 2 * HEAD :] = jnp.concatenate([dvalues[0], dvalues[1]], axis=0).T
    for r in range(2 * n):
        at = pl.multiple_of(sc[3 + r] * block, 16)
        dkv_ref[r * block : (r + 1) * block, :] = flat[pl.ds(at, block), :].astype(dkv_ref.dtype)


def attention_backward(scalars, queries, grads, lse, cosine, sine, chunks, ends, pairs):
    n = len(chunks)
    rows, width = queries.shape
    group = width // HEAD // 8
    block, total = rows // 2, rows * n
    first, steps = pairs
    whole = pl.BlockSpec((rows, 128), lambda p, sc: (0, 0))
    wide = pl.BlockSpec((rows, width // 4), lambda p, sc: (0, p + first))
    return pl.pallas_call(
        functools.partial(backward_kernel, n, group, ends, first),
        grid_spec=pltpu.PrefetchScalarGridSpec(
            num_scalar_prefetch=1,
            grid=(steps,),
            in_specs=[
                wide,
                pl.BlockSpec((rows, width // 4), lambda p, sc: (0, (p + first) ^ sc[0])),
                whole,
                whole,
                whole,
            ]
            + [pl.BlockSpec((rows, 4 * HEAD), lambda p, sc: (0, p + first))] * n,
            out_specs=[
                pl.BlockSpec((rows, width // 4), lambda p, sc: (0, p)),
                pl.BlockSpec((total, 4 * HEAD), lambda p, sc: (0, p)),
            ],
            scratch_shapes=[
                pltpu.VMEM((2, block, total), F32),
                pltpu.VMEM((2, total, HEAD), BF),
                pltpu.VMEM((2, total, HEAD), BF),
                pltpu.VMEM((2, 2, group * block, HEAD), BF),
                pltpu.VMEM((2, 2, group * block, HEAD), BF),
                pltpu.VMEM((2, 2, group * block, HEAD), F32),
                pltpu.VMEM((2, HEAD, total), F32),
                pltpu.VMEM((2, HEAD, total), F32),
                pltpu.VMEM((total, 4 * HEAD), F32),
            ],
        ),
        out_shape=[
            jax.ShapeDtypeStruct((rows, steps * width // 4), BF),
            jax.ShapeDtypeStruct((total, steps * 4 * HEAD), BF),
        ],
        compiler_params=pltpu.CompilerParams(vmem_limit_bytes=56 * 2**20),
        cost_estimate=cost(26),
        name="attention_backward",
    )(scalars, queries, grads, lse, cosine, sine, *chunks)


def params(mib):
    return pltpu.CompilerParams(vmem_limit_bytes=mib * MIB)


def cost(micros):
    return pl.CostEstimate(flops=int(micros * 1e7), bytes_accessed=0, transcendentals=0)


def row_scale(values):
    return lax.rsqrt(jnp.mean(values * values, axis=-1, keepdims=True) + NORM_EPS)


def quarter(f, d, size):
    return pl.ds(pl.multiple_of((f ^ d) * size, size), size)


def norm_kernel(f_ref, x_ref, gain_ref, h_ref):
    inverse = row_scale(x_ref[...].astype(F32))
    size = x_ref.shape[1] // 4
    for d in range(4):
        part = x_ref[:, quarter(f_ref[0], d, size)].astype(F32) * inverse
        h_ref[:, d * size : (d + 1) * size] = (
            part * gain_ref[:, d * size : (d + 1) * size]
        ).astype(BF)


def smem():
    return pl.BlockSpec(memory_space=pltpu.SMEM)


def vmem():
    return pl.BlockSpec(memory_space=pltpu.VMEM)


def norm_rows(scalars, rows, gain):
    return pl.pallas_call(
        norm_kernel,
        in_specs=[smem(), vmem(), vmem()],
        out_specs=vmem(),
        out_shape=jax.ShapeDtypeStruct(rows.shape, BF),
        compiler_params=params(32),
        cost_estimate=cost(1),
        name="norm_rows",
    )(scalars, rows, gain)


def project_kernel(scale, turned_tiles, x_ref, cos_ref, sin_ref, *refs):
    weights, out_ref = refs[:-1], refs[-1]
    size = x_ref.shape[1] // 4
    parts = []
    for at in range(0, len(weights), 4):
        parts.append(
            sum(
                dot(x_ref[:, d * size : (d + 1) * size], w[...])
                for d, w in enumerate(weights[at : at + 4])
            )
        )
    cosine, sine = cos_ref[...], sin_ref[...]
    low = lax.broadcasted_iota(jnp.int32, cosine.shape, 1) % HEAD < HEAD // 2
    tiles = [p[:, t * 128 : (t + 1) * 128] for p in parts for t in range(p.shape[1] // 128)]
    for t, part in enumerate(tiles):
        if t < turned_tiles:
            turned = jnp.where(low, pltpu.roll(part, 96, 1), pltpu.roll(part, 32, 1))
            part = part * cosine + turned * sine
        part = part.astype(BF)
        if scale != 1.0:
            part = (part.astype(F32) * scale).astype(BF)
        out_ref[:, t * 128 : (t + 1) * 128] = part


def project(rows, cosine, sine, weights, turned_tiles, scale, micros):
    count, depth = rows.shape
    size, width = weights[0][0].shape
    part = 256 // len(weights)
    whole = lambda a: pl.BlockSpec(a.shape, lambda j: (0, 0))
    return pl.pallas_call(
        functools.partial(project_kernel, scale, turned_tiles),
        grid=(width // part,),
        in_specs=[whole(rows), whole(cosine), whole(sine)]
        + [pl.BlockSpec((size, part), lambda j: (0, j))] * (4 * len(weights)),
        out_specs=pl.BlockSpec((count, 256), lambda j: (0, j)),
        out_shape=jax.ShapeDtypeStruct((count, width * len(weights)), BF),
        compiler_params=params(32),
        cost_estimate=cost(micros),
        name="project",
    )(rows, cosine, sine, *[w for shards in weights for w in shards])


def out_kernel(f_ref, o_ref, x_ref, gain_ref, w0, w1, w2, w3, r_ref, h_ref):
    size = o_ref.shape[1] // 4
    tile = w0.shape[1]
    total = sum(
        dot(o_ref[:, d * size : (d + 1) * size], w[...]) for d, w in enumerate((w0, w1, w2, w3))
    )
    at = pl.ds(pl.multiple_of(pl.program_id(0) * tile, tile), tile)
    r_ref[:, at] = x_ref[:, at].astype(F32) + total

    @pl.when(pl.program_id(0) == pl.num_programs(0) - 1)
    def _():
        norm_kernel(f_ref, r_ref, gain_ref, h_ref)


def out_project(scalars, mixed, tokens, gain, weights):
    count, depth = mixed.shape
    size, width = weights[0].shape
    whole = lambda a: pl.BlockSpec(a.shape, lambda j: (0, 0))
    return pl.pallas_call(
        out_kernel,
        grid=(width // 256,),
        in_specs=[smem(), whole(mixed), whole(tokens), whole(gain)]
        + [pl.BlockSpec((size, 256), lambda j: (0, j))] * 4,
        out_specs=[whole(tokens), whole(tokens)],
        out_shape=[
            jax.ShapeDtypeStruct((count, width), F32),
            jax.ShapeDtypeStruct((count, width), BF),
        ],
        compiler_params=params(32),
        cost_estimate=cost(6),
        name="out_project",
    )(scalars, mixed, tokens, gain, *weights)


def norm_back_kernel(wide, f_ref, x_ref, gain_ref, base_ref, *rest):
    terms, outs = rest[:-wide], rest[-wide:]
    x = x_ref[...].astype(F32)
    inverse = row_scale(x)
    size = x_ref.shape[1] // 4
    f = f_ref[0]
    grads, normed = [], []
    dot_sum = 0.0
    for d in range(4):
        cols = slice(d * size, (d + 1) * size)
        grad = sum(t[:, cols].astype(F32) for t in terms)
        part = x_ref[:, quarter(f, d, size)].astype(F32) * inverse
        outs[1][:, cols] = jnp.sum(grad * part, axis=0, keepdims=True)
        grad = grad * gain_ref[:, cols]
        dot_sum += jnp.sum(grad * part, axis=-1, keepdims=True)
        grads.append(grad)
        normed.append(part)
    mean = dot_sum / x_ref.shape[1]
    for d in range(4):
        at = quarter(f, d, size)
        value = base_ref[:, at].astype(F32) + inverse * (grads[d] - normed[d] * mean)
        outs[0][:, at] = value
        if wide == 3:
            outs[2][:, at] = value.astype(BF)


def norm_back(scalars, rows, gain, base, terms, rounded):
    wide = 3 if rounded else 2
    shapes = [
        jax.ShapeDtypeStruct(rows.shape, F32),
        jax.ShapeDtypeStruct((1, rows.shape[1]), F32),
        jax.ShapeDtypeStruct(rows.shape, BF),
    ][:wide]
    return pl.pallas_call(
        functools.partial(norm_back_kernel, wide),
        in_specs=[smem()] + [vmem()] * (3 + len(terms)),
        out_specs=[vmem()] * wide,
        out_shape=shapes,
        compiler_params=params(40),
        cost_estimate=cost(2),
        name="norm_back",
    )(scalars, rows, gain, base, *terms)


def back_kernel(pairs, based, *refs):
    out_ref = refs[-1]
    step = pl.program_id(0)
    tile = refs[pairs].shape[0]
    size = tile * pl.num_programs(0)
    for d in range(4):
        at = pl.ds(pl.multiple_of(d * size + step * tile, tile), tile)
        total = sum(dot_nt(refs[i][...], refs[pairs + 4 * i + d][...]) for i in range(pairs))
        if based:
            total += refs[5 * pairs][:, at]
        out_ref[:, at] = total.astype(out_ref.dtype)


def back_project(rows, weights, kind, micros, base=None):
    count = rows[0].shape[0]
    size = weights[0][0].shape[0]
    whole = pl.BlockSpec((count, 4 * size), lambda j: (0, 0))
    extra = [] if base is None else [base]
    return pl.pallas_call(
        functools.partial(back_kernel, len(rows), base is not None),
        grid=(2,),
        in_specs=[pl.BlockSpec(r.shape, lambda j: (0, 0)) for r in rows]
        + [pl.BlockSpec((size // 2, w.shape[1]), lambda j: (j, 0)) for ws in weights for w in ws]
        + [whole] * len(extra),
        out_specs=whole,
        out_shape=jax.ShapeDtypeStruct((count, 4 * size), kind),
        compiler_params=params(40 if len(rows) == 1 else 60),
        cost_estimate=cost(micros),
        name="back_project",
    )(*rows, *[w for ws in weights for w in ws], *extra)


def cross(value):
    half = value.shape[1] // 2
    return jnp.concatenate([value[:, half:], value[:, :half]], axis=1)


def feed_kernel(m, kept, crossed, *refs):
    hidden, grads = refs[:m], refs[m : 2 * m]
    gates, ups = refs[2 * m : 2 * m + 4], refs[2 * m + 4 : 2 * m + 8]
    down_ref = refs[2 * m + 8]
    outs = refs[2 * m + 9 + kept :]
    rows_h, rows_dy, act_ref, dgu_ref, dh_ref, h_s, dy_s, dh_s = outs
    step = pl.program_id(0)
    count = hidden[0].shape[0]
    size = gates[0].shape[0]
    tile = gates[0].shape[1]

    @pl.when(step == 0)
    def _():
        for i in range(m):
            at = slice(i * count, (i + 1) * count)
            h_s[at], dy_s[at] = hidden[i][...], grads[i][...]
            rows_h[at], rows_dy[at] = hidden[i][...], grads[i][...]

    def ahead(weights):
        parts = [dot(h_s[:, d * size : (d + 1) * size], w[...]) for d, w in enumerate(weights)]
        if not crossed:
            return sum(parts)
        return parts[0] + parts[2] + cross(parts[1] + parts[3])

    gate, up = ahead(gates), ahead(ups)
    sig = jax.nn.sigmoid(gate)
    silu = gate * sig
    act_ref[...] = (silu * up).astype(BF)
    grad_act = dot_nt(dy_s[...], down_ref[...])
    grad_gate = (grad_act * up * sig * (1.0 + gate * (1.0 - sig))).astype(BF)
    grad_up = (grad_act * silu).astype(BF)
    dgu_ref[:, :tile] = grad_gate
    dgu_ref[:, tile:] = grad_up
    pairs = [(grad_gate, grad_up)] * 4
    if crossed:
        pairs[1] = pairs[3] = (cross(grad_gate), cross(grad_up))
    last = pl.num_programs(0) - 1
    for d in range(4):
        cols = slice(d * size, (d + 1) * size)
        dh = dot_nt(pairs[d][0], gates[d][...]) + dot_nt(pairs[d][1], ups[d][...])

        @pl.when(step == 0)
        def _():
            dh_s[:, cols] = dh

        @pl.when(step > 0)
        def _():
            dh_s[:, cols] += dh

    @pl.when(step == last)
    def _():
        dh_ref[...] = dh_s[...].astype(BF)


def feed_tile(units):
    crossed = units >= 128
    return (2 * units if crossed else 4 * units), crossed


def feed(hidden, grads, gate, up, down, slot, kept, n):
    m = len(hidden)
    count, depth = hidden[0].shape
    width = down.shape[0]
    tile, crossed = feed_tile(width // 4)
    steps = width // tile
    rows = m * count
    size = depth // 4

    def shard(d):
        flip = d >> 1 if crossed else 0
        return pl.BlockSpec((size, tile), lambda e: (0, e ^ flip))

    chunk = pl.BlockSpec((count, depth), lambda e: (0, 0))
    block = pl.BlockSpec((rows, depth), lambda e: (slot, 0))
    shapes = [
        jax.ShapeDtypeStruct((n * count, depth), BF),
        jax.ShapeDtypeStruct((n * count, depth), BF),
        jax.ShapeDtypeStruct((n * count, width), BF),
        jax.ShapeDtypeStruct((n * count, 2 * width), BF),
        jax.ShapeDtypeStruct((rows, depth), BF),
    ]
    first = 2 * m + 9
    *kept, dh = pl.pallas_call(
        functools.partial(feed_kernel, m, len(kept), crossed),
        grid=(steps,),
        in_specs=[chunk] * (2 * m)
        + [shard(d) for d in range(4)] * 2
        + [pl.BlockSpec((tile, depth), lambda e: (e, 0))]
        + [pl.BlockSpec(memory_space=pl.ANY)] * len(kept),
        out_specs=[
            block,
            block,
            pl.BlockSpec((rows, tile), lambda e: (slot, e)),
            pl.BlockSpec((rows, 2 * tile), lambda e: (slot, e)),
            pl.BlockSpec((rows, depth), lambda e: (0, 0)),
        ],
        scratch_shapes=[pltpu.VMEM((rows, depth), BF)] * 2 + [pltpu.VMEM((rows, depth), F32)],
        out_shape=shapes,
        input_output_aliases={first + i: i for i in range(len(kept))},
        compiler_params=params(48),
        cost_estimate=cost(8 + 4 * m),
        name="feed",
    )(*hidden, *grads, *gate, *up, down, *kept)
    return kept, dh


def down_kernel(act_ref, down_ref, y_ref):
    y_ref[...] = dot(act_ref[...], down_ref[...]).astype(BF)


def down_rows(act, down, n):
    count = act.shape[0] // n
    return pl.pallas_call(
        down_kernel,
        grid=(n // 2,),
        in_specs=[
            pl.BlockSpec((2 * count, act.shape[1]), lambda i: (i, 0)),
            pl.BlockSpec(down.shape, lambda i: (0, 0)),
        ],
        out_specs=pl.BlockSpec((2 * count, down.shape[1]), lambda i: (i, 0)),
        out_shape=jax.ShapeDtypeStruct((n * count, down.shape[1]), BF),
        compiler_params=params(32),
        cost_estimate=cost(8),
        name="down_rows",
    )(act, down)


def place_kernel(sc, *refs):
    out = refs[-1]
    count = refs[0].shape[0]
    for i, part in enumerate(refs[:-1]):
        out[pl.ds(pl.multiple_of(sc[i] * count, count), count), :] = part[...]


def place_rows(places, parts):
    count, width = parts[0].shape
    return pl.pallas_call(
        place_kernel,
        in_specs=[smem()] + [vmem()] * len(parts),
        out_specs=vmem(),
        out_shape=jax.ShapeDtypeStruct((count * len(parts), width), parts[0].dtype),
        compiler_params=params(24),
        cost_estimate=cost(2),
        name="place_rows",
    )(places, *parts)


def tn_kernel(adds, outs, left_ref, right_ref, *refs):
    turned = refs[-1]
    i, j = pl.program_id(0), pl.program_id(1)

    @pl.when(j == 0)
    def _():
        turned[...] = left_ref[...].T

    total = dot(turned[...], right_ref[...])
    for (low, high, crossed), extra in zip(adds, refs):
        extra = extra[...].astype(F32)
        if crossed:
            extra = cross(extra)
        if low is not None:
            extra = jnp.where((j >= low) & (j < high), extra, 0.0)
        total += extra
    for (row, low, high), out in zip(outs, refs[len(adds) :]):

        @pl.when((i == row) & (j >= low) & (j < high))
        def _():
            out[...] = total.astype(out.dtype)


def tn_blocks(left, right, blocks, kind, micros, adds=(), pieces=1):
    rows, depth = left.shape
    size, width = depth // 4, right.shape[1]
    tile = min(width, 512)
    steps = width // tile
    pieces = min(pieces, steps)
    if size % 128:
        result = []
        for block in blocks:
            total = lax.dot_general(
                left[:, block * size : (block + 1) * size],
                right,
                (((0,), (0,)), ((), ())),
                preferred_element_type=F32,
            )
            for array, part, parts, _, _ in adds:
                at = part * (width // parts)
                total = total.at[:, at : at + width // parts].add(array.astype(F32))
            result.append(jnp.split(total.astype(kind), pieces, axis=1))
        return result
    first = blocks[0]
    stride = blocks[1] - first if len(blocks) > 1 else 0

    def window(part, parts):
        count = max(1, steps // parts)
        return part * count, (part + 1) * count

    def added_spec(part, parts, flip):
        low, high = window(part, parts)
        if parts == 1:
            return pl.BlockSpec((size, tile), lambda i, j: (0, j ^ flip))
        return pl.BlockSpec((size, tile), lambda i, j: (0, jnp.clip(j - low, 0, high - low - 1)))

    def out_spec(row, low, high):
        def index(i, j):
            at = jnp.clip(j - low, 0, high - low - 1)
            return (0, jnp.where(i < row, 0, jnp.where(i > row, high - low - 1, at)))

        return pl.BlockSpec((size, tile), index)

    windows = [
        (*(window(part, parts) if parts > 1 and steps > 1 else (None, None)), crossed)
        for _, part, parts, _, crossed in adds
    ]
    outs = [(row, *window(piece, pieces)) for row in range(len(blocks)) for piece in range(pieces)]
    result = pl.pallas_call(
        functools.partial(tn_kernel, windows, outs),
        grid=(len(blocks), steps),
        in_specs=[
            pl.BlockSpec((rows, size), lambda i, j: (0, first + stride * i)),
            pl.BlockSpec((rows, tile), lambda i, j: (0, j)),
        ]
        + [added_spec(part, parts, flip) for _, part, parts, flip, _ in adds],
        out_specs=[out_spec(*out) for out in outs],
        out_shape=[jax.ShapeDtypeStruct((size, width // pieces), kind)] * len(outs),
        scratch_shapes=[pltpu.VMEM((size, rows), BF)],
        compiler_params=params(32),
        cost_estimate=cost(micros),
        name="tn_blocks",
    )(left, right, *[a[0] for a in adds])
    return [list(result[row * pieces : (row + 1) * pieces]) for row in range(len(blocks))]


def spread_kernel(units, tile, f_ref, all_ref, *outs):
    span = outs[0].shape[1] // 4
    c = pl.program_id(0)
    for e in range(4):
        step, at = divmod(e * units, tile)
        start = (f_ref[0] ^ e) * span + c * units
        for part in range(2):
            low = (2 * step + part) * tile + at
            value = all_ref[0, :, low : low + units].astype(F32)
            outs[part][:, pl.ds(pl.multiple_of(start, units), units)] = value


def spread(scalars, gathered, units, tile):
    n, rows, _ = gathered.shape
    width = 4 * n * units
    return pl.pallas_call(
        functools.partial(spread_kernel, units, tile),
        grid=(n,),
        in_specs=[smem(), pl.BlockSpec((1, *gathered.shape[1:]), lambda i: (i, 0, 0))],
        out_specs=[pl.BlockSpec((rows, width), lambda i: (0, 0))] * 2,
        out_shape=[jax.ShapeDtypeStruct((rows, width), F32)] * 2,
        compiler_params=params(32),
        cost_estimate=cost(4),
        name="spread",
    )(scalars, gathered)


def swap_fsdp(value, d):
    return lax.ppermute(value, "fsdp", [(i, i ^ d) for i in range(4)])


def after(value, *others):
    return lax.optimization_barrier((value, others))[0] if others else value


def gather_fsdp(shard):
    across = swap_fsdp(shard, 2)
    return [shard, swap_fsdp(shard, 1), across, swap_fsdp(across, 1)]


def xor_blocks(value, f, axis):
    size = value.shape[axis] // 4
    return jnp.concatenate(
        [lax.dynamic_slice_in_dim(value, (f ^ d) * size, size, axis) for d in range(4)], axis=axis
    )


def swap_cols(value, d, parts):
    width = value.shape[1] // (4 * parts)
    return jnp.concatenate(
        [
            value[:, (p * 4 + (e ^ d)) * width : (p * 4 + (e ^ d) + 1) * width]
            for p in range(parts)
            for e in range(4)
        ],
        axis=1,
    )


def ring_index(place, n):
    place = place % n
    return jnp.where(place < n // 2, 2 * place, 2 * (n - 1 - place) + 1)


def ring_shift(value, step, n):
    order = list(range(0, n, 2)) + list(range(n - 1, 0, -2))
    return lax.ppermute(value, "ctx", [(order[i], order[(i + step) % n]) for i in range(n)])


class Order:
    def __init__(self):
        self.last = ()

    def at(self, value):
        return after(value, *self.last)

    def done(self, value):
        self.last = (value,)
        return value

    def take(self, value):
        return self.done(self.at(value))

    def run(self, function, *args, **kwargs):
        return self.done(function(*self.at(args), **kwargs))


class Gather:
    def __init__(self, order, own, n):
        self.order, self.n, self.half, self.step = order, n, n // 2, 0
        self.chunks = {0: own}
        self.now = (own, own)
        self.width = own.shape[1] // 2

    def send(self):
        if self.step == self.half:
            return
        self.step += 1
        right, left = self.now
        if self.step == self.half:
            right, left = right[:, : self.width], left[:, self.width :]
        self.now = (ring_shift(right, 1, self.n), ring_shift(left, -1, self.n))

    def take(self):
        if self.half in self.chunks:
            return
        self.now = right, left = self.order.take(self.now)
        if self.step == self.half:
            self.chunks[self.half] = jnp.concatenate([right, left], axis=1)
        else:
            self.chunks[-self.step], self.chunks[self.step] = right, left

    def rest(self, hops=None):
        while self.step < self.half and hops != 0:
            self.take()
            self.send()
            hops = hops and hops - 1
        return self


class Scatter:
    def __init__(self, order, contrib, n):
        self.order, self.n, self.half, self.step = order, n, n // 2, 0
        self.contrib = contrib
        far = contrib(self.half)
        self.width = far.shape[1] // 2
        self.now = (far[:, : self.width].astype(BF), far[:, self.width :].astype(BF))

    def send(self):
        self.step += 1
        right, left = self.now
        self.now = (ring_shift(right, 1, self.n), ring_shift(left, -1, self.n))

    def take(self):
        self.now = got = self.order.take(self.now)
        r = self.half - self.step
        if r == 0:
            return (self.contrib(0), *got)
        got = [v.astype(F32) for v in got]
        width = self.width
        ahead, behind = self.contrib(r).astype(F32), self.contrib(-r).astype(F32)
        if self.step == 1:
            ahead = jnp.concatenate([ahead[:, :width] + got[0], ahead[:, width:]], axis=1)
            behind = jnp.concatenate([behind[:, :width], behind[:, width:] + got[1]], axis=1)
        else:
            ahead, behind = ahead + got[0], behind + got[1]
        self.now = self.order.done((ahead.astype(BF), behind.astype(BF)))

    def rest(self, hops=None):
        while self.step < self.half and hops != 0:
            self.take()
            self.send()
            hops = hops and hops - 1
        return self


def added(terms):
    return sum(t.astype(F32) for t in terms)


def deinterleave(both):
    runs = range(both.shape[1] // 256)
    return tuple(
        jnp.concatenate([both[:, p * 256 + o : p * 256 + o + 128] for p in runs], axis=1)
        for o in (0, 128)
    )


def turn_tables(block_ids, block, ends, starts):
    place = (block_ids[:, None] * block + jnp.arange(block, dtype=jnp.int32)[None, :]).reshape(-1)
    begin = jnp.max(jnp.where(place[:, None] >= starts[None, :], starts[None, :], 0), axis=1)
    freqs = ROPE_BASE ** (-(jnp.arange(HEAD // 2, dtype=F32) * 2.0 / HEAD))
    angle = (place - begin).astype(F32)[:, None] * freqs[None, :]
    cosine, sine = jnp.cos(angle), jnp.sin(angle)
    return (
        jnp.concatenate([cosine] * 4, axis=1),
        jnp.concatenate([-sine, sine, -sine, sine], axis=1),
    )


def turn_back(values, cosine, sine):
    parts = []
    for p in range(values.shape[1] // 128):
        part = values[:, p * 128 : (p + 1) * 128]
        if p % 2 == 0:
            low = lax.broadcasted_iota(jnp.int32, part.shape, 1) % HEAD < HEAD // 2
            turned = jnp.where(low, jnp.roll(part, -32, axis=1), jnp.roll(part, 32, axis=1))
            part = part * cosine - turned * sine
        parts.append(part)
    return jnp.concatenate(parts, axis=1)


def body(
    n,
    tokens,
    first_gain,
    query_weight,
    key_matrix,
    value_matrix,
    out_weight,
    second_gain,
    gate_weight,
    up_weight,
    down_weight,
    lengths,
    block_order,
    cotangent,
):
    token_rows, model = tokens.shape
    block = token_rows // 2
    c = lax.axis_index("ctx")
    f = lax.axis_index("fsdp")
    place = jnp.where(c % 2 == 0, c // 2, n - 1 - c // 2)
    half = n // 2
    rel = list(range(-(half - 1), half + 1))
    owners = ring_index(place + jnp.asarray(rel, jnp.int32), n)

    own_blocks = lax.dynamic_slice_in_dim(block_order, 2 * c, 2)
    key_blocks = jnp.take(block_order.reshape(n, 2), owners, axis=0).reshape(-1)
    seq_ends = jnp.cumsum(lengths[0])
    count = lengths.shape[1]
    groups = [(-1, 0, 1)] + [(-step, step) for step in range(2, half)] + [(half,)]
    slot_rel = [r for group in (groups[0], groups[-1], *groups[1:-1]) for r in group]
    scalars = jnp.concatenate([f[None], own_blocks, key_blocks, seq_ends]).astype(jnp.int32)
    cosine, sine = turn_tables(own_blocks, block, seq_ends, seq_ends - lengths[0])
    order = Order()

    units = gate_weight.shape[1] // (4 * n)
    span = gate_weight.shape[1] // 4
    width = 4 * units

    def own_units(weight):
        return jnp.concatenate(
            [
                lax.dynamic_slice_in_dim(weight, (f ^ e) * span + c * units, units, 1)
                for e in range(4)
            ],
            axis=1,
        )

    gains = gather_fsdp(jnp.stack([first_gain, second_gain]))
    gains = jnp.concatenate(gains, axis=1).astype(F32)
    gain_one, gain_two = gains[:1], gains[1:]
    out_part = out_weight.shape[0] // n
    out_across = swap_fsdp(lax.dynamic_slice_in_dim(out_weight, c * out_part, out_part, 0), 2)
    key_across, value_across = swap_fsdp(key_matrix, 2), swap_fsdp(value_matrix, 2)
    grad_out = Gather(order, cotangent, n)
    grad_out.send()
    key_core, value_core = swap_fsdp(key_matrix, 1), swap_fsdp(value_matrix, 1)
    out_core, query_core = swap_fsdp(out_weight, 1), swap_fsdp(query_weight, 1)
    def across(value):
        return swap_fsdp(order.at(value), 2)

    def shards(own, core, over):
        return [own, core, over, swap_fsdp(over, 1)]

    hidden_one = order.run(norm_rows, scalars, tokens, gain_one)
    out_across = order.take(out_across)
    out_parts = Gather(order, out_across, n)
    out_parts.send()
    weight_k = shards(key_matrix, key_core, order.take(key_across))
    out_parts.rest(1)
    weight_v = shards(value_matrix, value_core, order.take(value_across))
    query_across = across(query_weight)
    gate_own = order.run(own_units, gate_weight)
    up_own = order.run(own_units, up_weight)
    gate_core, up_core = swap_fsdp(gate_own, 1), swap_fsdp(up_own, 1)
    down_own = order.done(lax.dynamic_slice_in_dim(order.at(down_weight), c * units, units, 0))
    down_core = swap_fsdp(down_own, 1)
    out_parts.rest(1)
    grad_out.take()
    kv_own = order.run(project, hidden_one, cosine, sine, [weight_k, weight_v], turned_tiles=1, scale=1.0, micros=4)
    kv = Gather(order, kv_own, n)
    kv.send()
    kv.rest(1)
    kv.rest(1)
    out_parts.take()
    weight_q = shards(query_weight, query_core, order.take(query_across))
    gate_across = across(gate_own)
    kv.rest()
    kv.take()
    out_parts.send()
    kv_chunks = [kv.chunks[r] for r in rel]

    queries = order.run(project, hidden_one, cosine, sine, [weight_q], turned_tiles=2, scale=0.125, micros=7)
    out_parts.rest()
    out_parts.take()
    gate = shards(gate_own, gate_core, order.take(gate_across))
    up_across = across(up_own)
    grad_out.send()
    out_across = order.run(place_rows, owners.astype(jnp.int32), [out_parts.chunks[r] for r in rel])
    weight_o = shards(out_weight, out_core, out_across)
    mixed, lse = order.run(attention_forward, scalars, queries, kv_chunks, ends=count)
    up = shards(up_own, up_core, order.take(up_across))
    down_across = across(down_own)
    grad_out.take()
    residual, hidden_two = order.run(out_project, scalars, mixed, tokens, gain_two, weight_o)
    hidden = Gather(order, hidden_two, n)
    hidden.send()
    hidden.rest(1)
    grad_out.send()
    down = shards(down_own, down_core, order.take(down_across))
    if units < 128:
        gate = [swap_cols(part, d, 1) for d, part in enumerate(gate)]
        up = [swap_cols(part, d, 1) for d, part in enumerate(up)]
    down = order.done(jnp.concatenate(down, axis=0))

    kept, grads_two = [], {}
    for at, group in enumerate(groups):
        slot = slot_rel.index(group[0]) // len(group)
        kept, sums = order.run(
            feed,
            [hidden.chunks[r] for r in group],
            [grad_out.chunks[r] for r in group],
            gate,
            up,
            down,
            slot=slot,
            kept=kept,
            n=n,
        )
        grads_two.update((r, (sums, i)) for i, r in enumerate(group))
        if at < half - 1:
            hidden.take()
            hidden.send()
            grad_out.take()
            grad_out.send()

    rows_h, rows_dy, act, grads = kept
    tile, crossed = feed_tile(units)
    class Product:
        def __init__(self, left, right, micros, by_units=False):
            self.left, self.right, self.micros, self.by_units = left, right, micros, by_units

        def kernel(self, blocks, kind, adds=(), pieces=1):
            def run(left, right, *arrays):
                own = [(a, *rest) for a, (_, *rest) in zip(arrays, adds)]
                micros = self.micros * len(blocks)
                return tn_blocks(left, right, blocks, kind, micros, own, pieces)

            return order.run(run, self.left, self.right, *[a for a, *_ in adds])

        def from_partner(self, value, d):
            return swap_cols(value, d, 2) if self.by_units and not crossed else value

        def first(self):
            self.near = [
                [swap_fsdp(piece, 1) for piece in row] for row in self.kernel((1, 3), BF, (), 2)
            ]

        def pieces(self, row):
            turned = self.by_units and crossed
            got = [self.from_partner(v, 1) for v in order.take(self.near[row])]
            return [(v, p, len(got), 0, turned) for p, v in enumerate(got)]

        def second(self, halves=1):
            (mid,) = self.kernel((2,), BF, self.pieces(1), halves)
            self.mid = [swap_fsdp(v, 2) for v in mid]

        def settle(self):
            self.mid = order.take(self.mid)

        def last(self, kind):
            over = [self.from_partner(v, 2) for v in order.at(self.mid)]
            flip = 2 if self.by_units and crossed else 0
            adds = [(v, h, len(over), flip, False) for h, v in enumerate(over)]
            ((whole,),) = self.kernel((0,), kind, self.pieces(0) + adds)
            return whole

    def feed_contrib(r):
        value, i = grads_two[r]
        return value[i * token_rows : (i + 1) * token_rows]

    sums = Scatter(order, feed_contrib, n)
    sums.send()
    of_down = Product(act, rows_dy, 3)
    of_gate_up = Product(rows_h, grads, 5, True)
    of_gate_up.first()
    sums.rest(1)
    of_down.first()
    of_gate_up.second()
    sums.rest(1)
    y_rows = order.run(down_rows, act, down, n=n)
    of_down.second()
    sums.rest(1)
    sums.rest()
    grad_hidden_two = sums.take()
    grad_residual, gain_two_term, grad_branch = order.run(
        norm_back, scalars, residual, gain_two, cotangent, grad_hidden_two, rounded=True
    )
    grad_mixed = order.run(back_project, [grad_branch], [weight_o], kind=BF, micros=5)
    of_gate_up.settle()
    gate_up_grad = of_gate_up.last(BF)
    rows = gate_up_grad.shape[0] // n
    gate_up_all = lax.all_to_all(
        gate_up_grad.reshape(n, rows, 2 * width), "ctx", 0, 0, tiled=False
    )
    of_out = Product(mixed, grad_branch, 2)
    of_out.first()

    parts = []

    def attention_part(first):
        parts.append(
            order.run(
                attention_backward,
                scalars,
                queries,
                grad_mixed,
                lse,
                cosine,
                sine,
                kv_chunks,
                ends=count,
                pairs=(first, 2),
            )
        )

    attention_part(0)
    of_down.settle()
    attention_part(2)
    grad_query = jnp.concatenate([p[0] for p in parts], axis=1)

    def kv_contrib(r):
        start = rel.index(r) * token_rows
        return jnp.concatenate([p[1][start : start + token_rows] for p in parts], axis=1)

    def scatter_rows(within):
        rows = within.shape[0] // n

        def contrib(r):
            start = ring_index(place + r, n) * rows
            return lax.dynamic_slice_in_dim(within, start, rows, 0)

        return Scatter(order, contrib, n)

    grad_kv = Scatter(order, kv_contrib, n)
    grad_kv.send()
    of_out.second()
    of_query = Product(hidden_one, grad_query, 2)
    of_query.first()
    gate_up_all = order.take(gate_up_all)
    grad_kv.rest(1)
    grad_hidden_one = order.run(back_project, [grad_query], [weight_q], kind=F32, micros=5)
    grad_kv.rest(1)
    of_query.second()
    grad_kv.rest(1)
    of_out.settle()
    out_within = of_out.last(BF)
    grad_kv.rest()
    grad_kv = added(grad_kv.take())
    out_sums = scatter_rows(out_within)
    out_sums.send()

    def y_contrib(r):
        start = slot_rel.index(r) * token_rows
        return y_rows[start : start + token_rows]

    y_sums = Scatter(order, y_contrib, n)
    y_sums.send()
    grad_kv = turn_back(grad_kv, cosine, sine).astype(BF)
    grad_key, grad_value = deinterleave(grad_kv)
    grad_kv = jnp.concatenate([grad_key, grad_value], axis=1)
    of_kv = Product(hidden_one, grad_kv, 1.5)
    of_kv.first()
    out_sums.rest(1)
    grad_hidden_one = order.run(
        back_project, [grad_key, grad_value], [weight_k, weight_v], base=grad_hidden_one, kind=F32, micros=3
    )
    of_kv.second()
    y_sums.rest(1)
    out_sums.rest(1)
    tokens_grad, gain_one_term = order.run(
        norm_back, scalars, tokens, gain_one, grad_residual, [grad_hidden_one], rounded=False
    )
    y_sums.rest(1)
    out_sums.rest(1)
    gain_terms = xor_blocks(jnp.concatenate([gain_one_term, gain_two_term], axis=0), f, 1)
    gain_terms = gain_terms.astype(BF).reshape(2, 4 * n, model // (4 * n)).transpose(1, 0, 2)
    gain_terms = lax.all_to_all(gain_terms, ("fsdp", "ctx"), 0, 0, tiled=False)
    out_sums.rest()
    out_grad = order.done(added(out_sums.take()))
    y_sums.rest(1)
    of_query.settle()
    query_sums = scatter_rows(of_query.last(BF))
    query_sums.send()
    y_sums.rest()
    layer_out = order.done((residual + added(y_sums.take())).astype(BF))
    query_sums.rest(1)
    if crossed:
        gate_grad, up_grad = order.run(spread, scalars, gate_up_all, units=units, tile=tile)
    else:
        gate_up_all = gate_up_all.reshape(n, rows, 2, 4, units).transpose(2, 1, 3, 0, 4)
        gate_up_all = xor_blocks(gate_up_all, f, 2).reshape(2, rows, n * width).astype(F32)
        gate_grad, up_grad = order.done((gate_up_all[0], gate_up_all[1]))
    of_kv.settle()
    kv_sums = scatter_rows(of_kv.last(BF))
    kv_sums.send()
    query_sums.rest(1)
    down_grad = of_down.last(F32)
    kv_sums.rest(1)
    query_sums.rest()
    gain_terms = order.take(gain_terms)
    kv_sums.rest(1)
    query_grad = order.done(added(query_sums.take()))
    kv_sums.rest()
    kv_grad = order.done(added(kv_sums.take()))
    gain_grads = jnp.sum(gain_terms.astype(F32), axis=0)
    kv_width = key_matrix.shape[1]
    key_grad, value_grad = kv_grad[:, :kv_width], kv_grad[:, kv_width:]
    return (
        layer_out,
        tokens_grad,
        gain_grads[0],
        query_grad,
        key_grad,
        value_grad,
        out_grad,
        gain_grads[1],
        gate_grad,
        up_grad,
        down_grad,
    )


def solution(mesh):
    rows, vector = P(("fsdp", "ctx"), None), P(("fsdp", "ctx"))
    weight = P("fsdp", None)

    def layer(*arrays):
        return body(mesh.shape["ctx"], *arrays)

    return jax.shard_map(
        layer,
        mesh=mesh,
        in_specs=(
            rows, P("fsdp"), weight, weight, weight, weight, P("fsdp"), weight, weight, weight,
            weight, P(), rows,
        ),
        out_specs=(rows, rows, vector, rows, rows, rows, rows, vector, rows, rows, rows),
        check_vma=False,
    )
```

```python
import functools

import jax
import jax.numpy as jnp
from jax import lax
from jax.experimental import pallas as pl
from jax.experimental.pallas import tpu as pltpu
from jax.sharding import PartitionSpec as P

HEAD = 64
NORM_EPS = 1e-05
ROPE_BASE = 500000.0
MASKED = -1e30
VARIANTS = 10
BF = jnp.bfloat16
F32 = jnp.float32
MIB = 2**20


def dot(a, b):
    return jnp.dot(a, b, preferred_element_type=F32)


def dot_nt(a, b):
    return lax.dot_general(a, b, (((1,), (1,)), ((), ())), preferred_element_type=F32)


def fill_bias(sc, bias, own, block, ends_at, ends):
    for j in range(2):
        place = sc[own + j] * block + lax.broadcasted_iota(jnp.int32, bias.shape[1:], 0)
        key = lax.broadcasted_iota(jnp.int32, bias.shape[1:], 1)
        start = jnp.zeros_like(place)
        for s in range(ends):
            end = sc[ends_at + s]
            start = jnp.where(place >= end, end, start)
        bias[j] = jnp.where((key >= start) & (key <= place), 0.0, MASKED)


def fill_keys(sc, chunks, keys, values, block, blocks_at):
    for r, chunk in enumerate(chunks):
        for j in range(2):
            at = pl.multiple_of(sc[blocks_at + 2 * r + j] * block, 16)
            part = chunk[j * block : (j + 1) * block, :]
            for g in range(2):
                keys[g, pl.ds(at, block), :] = part[:, g * HEAD : (g + 1) * HEAD]
                values[g, pl.ds(at, block), :] = part[:, 2 * HEAD + g * HEAD : 2 * HEAD + (g + 1) * HEAD]


def split_heads(ref, out, block, group):
    for g in range(2):
        for j in range(2):
            for h in range(group):
                lane = (g * group + h) * HEAD
                out[g, j, h * block : (h + 1) * block, :] = ref[
                    j * block : (j + 1) * block, lane : lane + HEAD
                ]


def join_heads(out, block, group):
    rows = []
    for j in range(2):
        rows.append(
            jnp.concatenate(
                [out[g, j, h * block : (h + 1) * block, :] for g in range(2) for h in range(group)],
                axis=1,
            )
        )
    return jnp.concatenate(rows, axis=0)


def visible(sc, own, j, block, step):
    return (sc[own + j] * block + block - 1) // step + 1


def forward_kernel(n, group, ends, sc, q_ref, *rest):
    chunks, (o_ref, lse_ref), (bias, keys, values, queries, outs) = (
        rest[:n],
        rest[n : n + 2],
        rest[n + 2 :],
    )
    block = q_ref.shape[0] // 2
    total = keys.shape[1]
    step = total // VARIANTS
    pair = pl.program_id(0)

    @pl.when(pair == 0)
    def _():
        fill_bias(sc, bias, 1, block, 3 + 2 * n, ends)
        lse_ref[...] = jnp.zeros_like(lse_ref)

    fill_keys(sc, chunks, keys, values, block, 3)
    split_heads(q_ref, queries, block, group)

    def one(g, j, length):
        scores = dot_nt(queries[g, j], keys[g, :length, :])
        scores = (scores.reshape(group, block, length) + bias[j, :, :length][None]).reshape(
            group * block, length
        )
        peak = jnp.max(scores, axis=-1, keepdims=True)
        expd = jnp.exp(scores - peak)
        row_total = jnp.sum(expd, axis=-1, keepdims=True)
        mixed = dot(expd.astype(BF), values[g, :length, :])
        outs[g, j] = mixed / row_total
        lse = peak + jnp.log(row_total)
        lane = lax.broadcasted_iota(jnp.int32, (block, lse_ref.shape[1]), 1)
        rows = pl.ds(pl.multiple_of(j * block, 16), block)
        kept = lse_ref[rows, :]
        for h in range(group):
            kept = jnp.where(
                lane == (pair * 2 + g) * group + h, lse[h * block : (h + 1) * block], kept
            )
        lse_ref[rows, :] = kept

    def both(at, carry):
        g, j = at // 2, at % 2
        count = visible(sc, 1, j, block, step)
        for v in range(1, VARIANTS + 1):
            pl.when(count == v)(functools.partial(one, g, j, v * step))
        return carry

    lax.fori_loop(0, 4, both, 0)
    o_ref[...] = join_heads(outs, block, group).astype(o_ref.dtype)


def attention_forward(scalars, queries, chunks, ends):
    n = len(chunks)
    rows, width = queries.shape
    group = width // HEAD // 8
    block, total = rows // 2, rows * n
    pairs = 4
    return pl.pallas_call(
        functools.partial(forward_kernel, n, group, ends),
        grid_spec=pltpu.PrefetchScalarGridSpec(
            num_scalar_prefetch=1,
            grid=(pairs,),
            in_specs=[pl.BlockSpec((rows, width // pairs), lambda p, sc: (0, p))]
            + [pl.BlockSpec((rows, 4 * HEAD), lambda p, sc: (0, p))] * n,
            out_specs=[
                pl.BlockSpec((rows, width // pairs), lambda p, sc: (0, p ^ sc[0])),
                pl.BlockSpec((rows, 128), lambda p, sc: (0, 0)),
            ],
            scratch_shapes=[
                pltpu.VMEM((2, block, total), F32),
                pltpu.VMEM((2, total, HEAD), BF),
                pltpu.VMEM((2, total, HEAD), BF),
                pltpu.VMEM((2, 2, group * block, HEAD), BF),
                pltpu.VMEM((2, 2, group * block, HEAD), F32),
            ],
        ),
        out_shape=[
            jax.ShapeDtypeStruct((rows, width), BF),
            jax.ShapeDtypeStruct((rows, 128), F32),
        ],
        compiler_params=pltpu.CompilerParams(vmem_limit_bytes=48 * 2**20),
        cost_estimate=cost(18),
        name="attention_forward",
    )(scalars, queries, *chunks)


def backward_kernel(n, group, ends, first, sc, q_ref, do_ref, lse_ref, cos_ref, sin_ref, *rest):
    chunks, (dq_ref, dkv_ref), scratch = rest[:n], rest[n : n + 2], rest[n + 2 :]
    bias, keys, values, queries, grads, outs, dkeys, dvalues, flat = scratch
    block = q_ref.shape[0] // 2
    total = keys.shape[1]
    step = total // VARIANTS
    pair = pl.program_id(0) + first

    @pl.when(pair == first)
    def _():
        fill_bias(sc, bias, 1, block, 3 + 2 * n, ends)

    fill_keys(sc, chunks, keys, values, block, 3)
    split_heads(q_ref, queries, block, group)
    split_heads(do_ref, grads, block, group)
    dkeys[...] = jnp.zeros_like(dkeys)
    dvalues[...] = jnp.zeros_like(dvalues)

    def one(g, j, length):
        query, grad = queries[g, j], grads[g, j]
        key, value = keys[g, :length, :], values[g, :length, :]
        rows = pl.ds(pl.multiple_of(j * block, 16), block)
        kept = lse_ref[rows, :]
        lane = lax.broadcasted_iota(jnp.int32, kept.shape, 1)
        lse = jnp.concatenate(
            [
                jnp.sum(
                    jnp.where(lane == (pair * 2 + g) * group + h, kept, 0.0), axis=1, keepdims=True
                )
                for h in range(group)
            ],
            axis=0,
        )
        scores = dot_nt(query, key)
        scores = (scores.reshape(group, block, length) + bias[j, :, :length][None]).reshape(
            group * block, length
        )
        prob = jnp.exp(scores - lse)
        dprob = dot_nt(grad, value)
        weighted = prob * dprob
        row_dot = jnp.sum(weighted, axis=-1, keepdims=True)
        dscore = (weighted - prob * row_dot).astype(BF)
        outs[g, j] = dot(dscore, key)
        dkeys[g, :, :length] += dot(query.T, dscore)
        dvalues[g, :, :length] += dot(grad.T, prob.astype(BF))

    def both(at, carry):
        g, j = at // 2, at % 2
        count = visible(sc, 1, j, block, step)
        for v in range(1, VARIANTS + 1):
            pl.when(count == v)(functools.partial(one, g, j, v * step))
        return carry

    lax.fori_loop(0, 4, both, 0)
    dq = join_heads(outs, block, group) * (1.0 / 8.0)
    cosine, sine = cos_ref[...], sin_ref[...]
    low = lax.broadcasted_iota(jnp.int32, cosine.shape, 1) % HEAD < HEAD // 2
    for t in range(dq.shape[1] // 128):
        part = dq[:, t * 128 : (t + 1) * 128]
        turned = jnp.where(low, pltpu.roll(part, 96, 1), pltpu.roll(part, 32, 1))
        dq_ref[:, t * 128 : (t + 1) * 128] = (part * cosine - turned * sine).astype(dq_ref.dtype)
    flat[:, : 2 * HEAD] = jnp.concatenate([dkeys[0], dkeys[1]], axis=0).T
    flat[:, 2 * HEAD :] = jnp.concatenate([dvalues[0], dvalues[1]], axis=0).T
    for r in range(2 * n):
        at = pl.multiple_of(sc[3 + r] * block, 16)
        dkv_ref[r * block : (r + 1) * block, :] = flat[pl.ds(at, block), :].astype(dkv_ref.dtype)


def attention_backward(scalars, queries, grads, lse, cosine, sine, chunks, ends, pairs):
    n = len(chunks)
    rows, width = queries.shape
    group = width // HEAD // 8
    block, total = rows // 2, rows * n
    first, steps = pairs
    whole = pl.BlockSpec((rows, 128), lambda p, sc: (0, 0))
    wide = pl.BlockSpec((rows, width // 4), lambda p, sc: (0, p + first))
    return pl.pallas_call(
        functools.partial(backward_kernel, n, group, ends, first),
        grid_spec=pltpu.PrefetchScalarGridSpec(
            num_scalar_prefetch=1,
            grid=(steps,),
            in_specs=[
                wide,
                pl.BlockSpec((rows, width // 4), lambda p, sc: (0, (p + first) ^ sc[0])),
                whole,
                whole,
                whole,
            ]
            + [pl.BlockSpec((rows, 4 * HEAD), lambda p, sc: (0, p + first))] * n,
            out_specs=[
                pl.BlockSpec((rows, width // 4), lambda p, sc: (0, p)),
                pl.BlockSpec((total, 4 * HEAD), lambda p, sc: (0, p)),
            ],
            scratch_shapes=[
                pltpu.VMEM((2, block, total), F32),
                pltpu.VMEM((2, total, HEAD), BF),
                pltpu.VMEM((2, total, HEAD), BF),
                pltpu.VMEM((2, 2, group * block, HEAD), BF),
                pltpu.VMEM((2, 2, group * block, HEAD), BF),
                pltpu.VMEM((2, 2, group * block, HEAD), F32),
                pltpu.VMEM((2, HEAD, total), F32),
                pltpu.VMEM((2, HEAD, total), F32),
                pltpu.VMEM((total, 4 * HEAD), F32),
            ],
        ),
        out_shape=[
            jax.ShapeDtypeStruct((rows, steps * width // 4), BF),
            jax.ShapeDtypeStruct((total, steps * 4 * HEAD), BF),
        ],
        compiler_params=pltpu.CompilerParams(vmem_limit_bytes=56 * 2**20),
        cost_estimate=cost(26),
        name="attention_backward",
    )(scalars, queries, grads, lse, cosine, sine, *chunks)


def params(mib):
    return pltpu.CompilerParams(vmem_limit_bytes=mib * MIB)


def cost(micros):
    return pl.CostEstimate(flops=int(micros * 1e7), bytes_accessed=0, transcendentals=0)


def row_scale(values):
    return lax.rsqrt(jnp.mean(values * values, axis=-1, keepdims=True) + NORM_EPS)


def quarter(f, d, size):
    return pl.ds(pl.multiple_of((f ^ d) * size, size), size)


def norm_kernel(f_ref, x_ref, gain_ref, h_ref):
    inverse = row_scale(x_ref[...].astype(F32))
    size = x_ref.shape[1] // 4
    for d in range(4):
        part = x_ref[:, quarter(f_ref[0], d, size)].astype(F32) * inverse
        h_ref[:, d * size : (d + 1) * size] = (
            part * gain_ref[:, d * size : (d + 1) * size]
        ).astype(BF)


def smem():
    return pl.BlockSpec(memory_space=pltpu.SMEM)


def vmem():
    return pl.BlockSpec(memory_space=pltpu.VMEM)


def norm_rows(scalars, rows, gain):
    return pl.pallas_call(
        norm_kernel,
        in_specs=[smem(), vmem(), vmem()],
        out_specs=vmem(),
        out_shape=jax.ShapeDtypeStruct(rows.shape, BF),
        compiler_params=params(32),
        cost_estimate=cost(1),
        name="norm_rows",
    )(scalars, rows, gain)


def project_kernel(scale, turned_tiles, x_ref, cos_ref, sin_ref, *refs):
    weights, out_ref = refs[:-1], refs[-1]
    size = x_ref.shape[1] // 4
    parts = []
    for at in range(0, len(weights), 4):
        parts.append(
            sum(
                dot(x_ref[:, d * size : (d + 1) * size], w[...])
                for d, w in enumerate(weights[at : at + 4])
            )
        )
    cosine, sine = cos_ref[...], sin_ref[...]
    low = lax.broadcasted_iota(jnp.int32, cosine.shape, 1) % HEAD < HEAD // 2
    tiles = [p[:, t * 128 : (t + 1) * 128] for p in parts for t in range(p.shape[1] // 128)]
    for t, part in enumerate(tiles):
        if t < turned_tiles:
            turned = jnp.where(low, pltpu.roll(part, 96, 1), pltpu.roll(part, 32, 1))
            part = part * cosine + turned * sine
        part = part.astype(BF)
        if scale != 1.0:
            part = (part.astype(F32) * scale).astype(BF)
        out_ref[:, t * 128 : (t + 1) * 128] = part


def project(rows, cosine, sine, weights, turned_tiles, scale, micros):
    count, depth = rows.shape
    size, width = weights[0][0].shape
    part = 256 // len(weights)
    whole = lambda a: pl.BlockSpec(a.shape, lambda j: (0, 0))
    return pl.pallas_call(
        functools.partial(project_kernel, scale, turned_tiles),
        grid=(width // part,),
        in_specs=[whole(rows), whole(cosine), whole(sine)]
        + [pl.BlockSpec((size, part), lambda j: (0, j))] * (4 * len(weights)),
        out_specs=pl.BlockSpec((count, 256), lambda j: (0, j)),
        out_shape=jax.ShapeDtypeStruct((count, width * len(weights)), BF),
        compiler_params=params(32),
        cost_estimate=cost(micros),
        name="project",
    )(rows, cosine, sine, *[w for shards in weights for w in shards])


def out_kernel(f_ref, o_ref, x_ref, gain_ref, w0, w1, w2, w3, r_ref, h_ref):
    size = o_ref.shape[1] // 4
    tile = w0.shape[1]
    total = sum(
        dot(o_ref[:, d * size : (d + 1) * size], w[...]) for d, w in enumerate((w0, w1, w2, w3))
    )
    at = pl.ds(pl.multiple_of(pl.program_id(0) * tile, tile), tile)
    r_ref[:, at] = x_ref[:, at].astype(F32) + total

    @pl.when(pl.program_id(0) == pl.num_programs(0) - 1)
    def _():
        norm_kernel(f_ref, r_ref, gain_ref, h_ref)


def out_project(scalars, mixed, tokens, gain, weights):
    count, depth = mixed.shape
    size, width = weights[0].shape
    whole = lambda a: pl.BlockSpec(a.shape, lambda j: (0, 0))
    return pl.pallas_call(
        out_kernel,
        grid=(width // 256,),
        in_specs=[smem(), whole(mixed), whole(tokens), whole(gain)]
        + [pl.BlockSpec((size, 256), lambda j: (0, j))] * 4,
        out_specs=[whole(tokens), whole(tokens)],
        out_shape=[
            jax.ShapeDtypeStruct((count, width), F32),
            jax.ShapeDtypeStruct((count, width), BF),
        ],
        compiler_params=params(32),
        cost_estimate=cost(6),
        name="out_project",
    )(scalars, mixed, tokens, gain, *weights)


def norm_back_kernel(wide, f_ref, x_ref, gain_ref, base_ref, *rest):
    terms, outs = rest[:-wide], rest[-wide:]
    x = x_ref[...].astype(F32)
    inverse = row_scale(x)
    size = x_ref.shape[1] // 4
    f = f_ref[0]
    grads, normed = [], []
    dot_sum = 0.0
    for d in range(4):
        cols = slice(d * size, (d + 1) * size)
        grad = sum(t[:, cols].astype(F32) for t in terms)
        part = x_ref[:, quarter(f, d, size)].astype(F32) * inverse
        outs[1][:, cols] = jnp.sum(grad * part, axis=0, keepdims=True)
        grad = grad * gain_ref[:, cols]
        dot_sum += jnp.sum(grad * part, axis=-1, keepdims=True)
        grads.append(grad)
        normed.append(part)
    mean = dot_sum / x_ref.shape[1]
    for d in range(4):
        at = quarter(f, d, size)
        value = base_ref[:, at].astype(F32) + inverse * (grads[d] - normed[d] * mean)
        outs[0][:, at] = value
        if wide == 3:
            outs[2][:, at] = value.astype(BF)


def norm_back(scalars, rows, gain, base, terms, rounded):
    wide = 3 if rounded else 2
    shapes = [
        jax.ShapeDtypeStruct(rows.shape, F32),
        jax.ShapeDtypeStruct((1, rows.shape[1]), F32),
        jax.ShapeDtypeStruct(rows.shape, BF),
    ][:wide]
    return pl.pallas_call(
        functools.partial(norm_back_kernel, wide),
        in_specs=[smem()] + [vmem()] * (3 + len(terms)),
        out_specs=[vmem()] * wide,
        out_shape=shapes,
        compiler_params=params(40),
        cost_estimate=cost(2),
        name="norm_back",
    )(scalars, rows, gain, base, *terms)


def back_kernel(pairs, based, *refs):
    out_ref = refs[-1]
    step = pl.program_id(0)
    tile = refs[pairs].shape[0]
    size = tile * pl.num_programs(0)
    for d in range(4):
        at = pl.ds(pl.multiple_of(d * size + step * tile, tile), tile)
        total = sum(dot_nt(refs[i][...], refs[pairs + 4 * i + d][...]) for i in range(pairs))
        if based:
            total += refs[5 * pairs][:, at]
        out_ref[:, at] = total.astype(out_ref.dtype)


def back_project(rows, weights, kind, micros, base=None):
    count = rows[0].shape[0]
    size = weights[0][0].shape[0]
    whole = pl.BlockSpec((count, 4 * size), lambda j: (0, 0))
    extra = [] if base is None else [base]
    return pl.pallas_call(
        functools.partial(back_kernel, len(rows), base is not None),
        grid=(2,),
        in_specs=[pl.BlockSpec(r.shape, lambda j: (0, 0)) for r in rows]
        + [pl.BlockSpec((size // 2, w.shape[1]), lambda j: (j, 0)) for ws in weights for w in ws]
        + [whole] * len(extra),
        out_specs=whole,
        out_shape=jax.ShapeDtypeStruct((count, 4 * size), kind),
        compiler_params=params(40 if len(rows) == 1 else 60),
        cost_estimate=cost(micros),
        name="back_project",
    )(*rows, *[w for ws in weights for w in ws], *extra)


def cross(value):
    half = value.shape[1] // 2
    return jnp.concatenate([value[:, half:], value[:, :half]], axis=1)


def feed_kernel(m, kept, crossed, *refs):
    hidden, grads = refs[:m], refs[m : 2 * m]
    gates, ups = refs[2 * m : 2 * m + 4], refs[2 * m + 4 : 2 * m + 8]
    down_ref = refs[2 * m + 8]
    outs = refs[2 * m + 9 + kept :]
    rows_h, rows_dy, act_ref, dgu_ref, dh_ref, h_s, dy_s, dh_s = outs
    step = pl.program_id(0)
    count = hidden[0].shape[0]
    size = gates[0].shape[0]
    tile = gates[0].shape[1]

    @pl.when(step == 0)
    def _():
        for i in range(m):
            at = slice(i * count, (i + 1) * count)
            h_s[at], dy_s[at] = hidden[i][...], grads[i][...]
            rows_h[at], rows_dy[at] = hidden[i][...], grads[i][...]

    def ahead(weights):
        parts = [dot(h_s[:, d * size : (d + 1) * size], w[...]) for d, w in enumerate(weights)]
        if not crossed:
            return sum(parts)
        return parts[0] + parts[2] + cross(parts[1] + parts[3])

    gate, up = ahead(gates), ahead(ups)
    sig = jax.nn.sigmoid(gate)
    silu = gate * sig
    act_ref[...] = (silu * up).astype(BF)
    grad_act = dot_nt(dy_s[...], down_ref[...])
    grad_gate = (grad_act * up * sig * (1.0 + gate * (1.0 - sig))).astype(BF)
    grad_up = (grad_act * silu).astype(BF)
    dgu_ref[:, :tile] = grad_gate
    dgu_ref[:, tile:] = grad_up
    pairs = [(grad_gate, grad_up)] * 4
    if crossed:
        pairs[1] = pairs[3] = (cross(grad_gate), cross(grad_up))
    last = pl.num_programs(0) - 1
    for d in range(4):
        cols = slice(d * size, (d + 1) * size)
        dh = dot_nt(pairs[d][0], gates[d][...]) + dot_nt(pairs[d][1], ups[d][...])

        @pl.when(step == 0)
        def _():
            dh_s[:, cols] = dh

        @pl.when(step > 0)
        def _():
            dh_s[:, cols] += dh

    @pl.when(step == last)
    def _():
        dh_ref[...] = dh_s[...].astype(BF)


def feed_tile(units):
    crossed = units >= 128
    return (2 * units if crossed else 4 * units), crossed


def feed(hidden, grads, gate, up, down, slot, kept, n):
    m = len(hidden)
    count, depth = hidden[0].shape
    width = down.shape[0]
    tile, crossed = feed_tile(width // 4)
    steps = width // tile
    rows = m * count
    size = depth // 4

    def shard(d):
        flip = d >> 1 if crossed else 0
        return pl.BlockSpec((size, tile), lambda e: (0, e ^ flip))

    chunk = pl.BlockSpec((count, depth), lambda e: (0, 0))
    block = pl.BlockSpec((rows, depth), lambda e: (slot, 0))
    shapes = [
        jax.ShapeDtypeStruct((n * count, depth), BF),
        jax.ShapeDtypeStruct((n * count, depth), BF),
        jax.ShapeDtypeStruct((n * count, width), BF),
        jax.ShapeDtypeStruct((n * count, 2 * width), BF),
        jax.ShapeDtypeStruct((rows, depth), BF),
    ]
    first = 2 * m + 9
    *kept, dh = pl.pallas_call(
        functools.partial(feed_kernel, m, len(kept), crossed),
        grid=(steps,),
        in_specs=[chunk] * (2 * m)
        + [shard(d) for d in range(4)] * 2
        + [pl.BlockSpec((tile, depth), lambda e: (e, 0))]
        + [pl.BlockSpec(memory_space=pl.ANY)] * len(kept),
        out_specs=[
            block,
            block,
            pl.BlockSpec((rows, tile), lambda e: (slot, e)),
            pl.BlockSpec((rows, 2 * tile), lambda e: (slot, e)),
            pl.BlockSpec((rows, depth), lambda e: (0, 0)),
        ],
        scratch_shapes=[pltpu.VMEM((rows, depth), BF)] * 2 + [pltpu.VMEM((rows, depth), F32)],
        out_shape=shapes,
        input_output_aliases={first + i: i for i in range(len(kept))},
        compiler_params=params(48),
        cost_estimate=cost(8 + 4 * m),
        name="feed",
    )(*hidden, *grads, *gate, *up, down, *kept)
    return kept, dh


def down_kernel(act_ref, down_ref, y_ref):
    y_ref[...] = dot(act_ref[...], down_ref[...]).astype(BF)


def down_rows(act, down, n):
    count = act.shape[0] // n
    return pl.pallas_call(
        down_kernel,
        grid=(n // 2,),
        in_specs=[
            pl.BlockSpec((2 * count, act.shape[1]), lambda i: (i, 0)),
            pl.BlockSpec(down.shape, lambda i: (0, 0)),
        ],
        out_specs=pl.BlockSpec((2 * count, down.shape[1]), lambda i: (i, 0)),
        out_shape=jax.ShapeDtypeStruct((n * count, down.shape[1]), BF),
        compiler_params=params(32),
        cost_estimate=cost(8),
        name="down_rows",
    )(act, down)


def place_kernel(sc, *refs):
    out = refs[-1]
    count = refs[0].shape[0]
    for i, part in enumerate(refs[:-1]):
        out[pl.ds(pl.multiple_of(sc[i] * count, count), count), :] = part[...]


def place_rows(places, parts):
    count, width = parts[0].shape
    return pl.pallas_call(
        place_kernel,
        in_specs=[smem()] + [vmem()] * len(parts),
        out_specs=vmem(),
        out_shape=jax.ShapeDtypeStruct((count * len(parts), width), parts[0].dtype),
        compiler_params=params(24),
        cost_estimate=cost(2),
        name="place_rows",
    )(places, *parts)


def tn_kernel(adds, outs, left_ref, right_ref, *refs):
    turned = refs[-1]
    i, j = pl.program_id(0), pl.program_id(1)

    @pl.when(j == 0)
    def _():
        turned[...] = left_ref[...].T

    total = dot(turned[...], right_ref[...])
    for (low, high, crossed), extra in zip(adds, refs):
        extra = extra[...].astype(F32)
        if crossed:
            extra = cross(extra)
        if low is not None:
            extra = jnp.where((j >= low) & (j < high), extra, 0.0)
        total += extra
    for (row, low, high), out in zip(outs, refs[len(adds) :]):

        @pl.when((i == row) & (j >= low) & (j < high))
        def _():
            out[...] = total.astype(out.dtype)


def tn_blocks(left, right, blocks, kind, micros, adds=(), pieces=1):
    rows, depth = left.shape
    size, width = depth // 4, right.shape[1]
    tile = min(width, 512)
    steps = width // tile
    pieces = min(pieces, steps)
    if size % 128:
        result = []
        for block in blocks:
            total = lax.dot_general(
                left[:, block * size : (block + 1) * size],
                right,
                (((0,), (0,)), ((), ())),
                preferred_element_type=F32,
            )
            for array, part, parts, _, _ in adds:
                at = part * (width // parts)
                total = total.at[:, at : at + width // parts].add(array.astype(F32))
            result.append(jnp.split(total.astype(kind), pieces, axis=1))
        return result
    first = blocks[0]
    stride = blocks[1] - first if len(blocks) > 1 else 0

    def window(part, parts):
        count = max(1, steps // parts)
        return part * count, (part + 1) * count

    def added_spec(part, parts, flip):
        low, high = window(part, parts)
        if parts == 1:
            return pl.BlockSpec((size, tile), lambda i, j: (0, j ^ flip))
        return pl.BlockSpec((size, tile), lambda i, j: (0, jnp.clip(j - low, 0, high - low - 1)))

    def out_spec(row, low, high):
        def index(i, j):
            at = jnp.clip(j - low, 0, high - low - 1)
            return (0, jnp.where(i < row, 0, jnp.where(i > row, high - low - 1, at)))

        return pl.BlockSpec((size, tile), index)

    windows = [
        (*(window(part, parts) if parts > 1 and steps > 1 else (None, None)), crossed)
        for _, part, parts, _, crossed in adds
    ]
    outs = [(row, *window(piece, pieces)) for row in range(len(blocks)) for piece in range(pieces)]
    result = pl.pallas_call(
        functools.partial(tn_kernel, windows, outs),
        grid=(len(blocks), steps),
        in_specs=[
            pl.BlockSpec((rows, size), lambda i, j: (0, first + stride * i)),
            pl.BlockSpec((rows, tile), lambda i, j: (0, j)),
        ]
        + [added_spec(part, parts, flip) for _, part, parts, flip, _ in adds],
        out_specs=[out_spec(*out) for out in outs],
        out_shape=[jax.ShapeDtypeStruct((size, width // pieces), kind)] * len(outs),
        scratch_shapes=[pltpu.VMEM((size, rows), BF)],
        compiler_params=params(32),
        cost_estimate=cost(micros),
        name="tn_blocks",
    )(left, right, *[a[0] for a in adds])
    return [list(result[row * pieces : (row + 1) * pieces]) for row in range(len(blocks))]


def spread_kernel(units, tile, f_ref, all_ref, *outs):
    span = outs[0].shape[1] // 4
    c = pl.program_id(0)
    for e in range(4):
        step, at = divmod(e * units, tile)
        start = (f_ref[0] ^ e) * span + c * units
        for part in range(2):
            low = (2 * step + part) * tile + at
            value = all_ref[0, :, low : low + units].astype(F32)
            outs[part][:, pl.ds(pl.multiple_of(start, units), units)] = value


def spread(scalars, gathered, units, tile):
    n, rows, _ = gathered.shape
    width = 4 * n * units
    return pl.pallas_call(
        functools.partial(spread_kernel, units, tile),
        grid=(n,),
        in_specs=[smem(), pl.BlockSpec((1, *gathered.shape[1:]), lambda i: (i, 0, 0))],
        out_specs=[pl.BlockSpec((rows, width), lambda i: (0, 0))] * 2,
        out_shape=[jax.ShapeDtypeStruct((rows, width), F32)] * 2,
        compiler_params=params(32),
        cost_estimate=cost(4),
        name="spread",
    )(scalars, gathered)


def swap_fsdp(value, d):
    return lax.ppermute(value, "fsdp", [(i, i ^ d) for i in range(4)])


def after(value, *others):
    return lax.optimization_barrier((value, others))[0] if others else value


def gather_fsdp(shard):
    across = swap_fsdp(shard, 2)
    return [shard, swap_fsdp(shard, 1), across, swap_fsdp(across, 1)]


def xor_blocks(value, f, axis):
    size = value.shape[axis] // 4
    return jnp.concatenate(
        [lax.dynamic_slice_in_dim(value, (f ^ d) * size, size, axis) for d in range(4)], axis=axis
    )


def swap_cols(value, d, parts):
    width = value.shape[1] // (4 * parts)
    return jnp.concatenate(
        [
            value[:, (p * 4 + (e ^ d)) * width : (p * 4 + (e ^ d) + 1) * width]
            for p in range(parts)
            for e in range(4)
        ],
        axis=1,
    )


def ring_index(place, n):
    place = place % n
    return jnp.where(place < n // 2, 2 * place, 2 * (n - 1 - place) + 1)


def ring_shift(value, step, n):
    order = list(range(0, n, 2)) + list(range(n - 1, 0, -2))
    return lax.ppermute(value, "ctx", [(order[i], order[(i + step) % n]) for i in range(n)])


class Order:
    def __init__(self):
        self.last = ()

    def at(self, value):
        return after(value, *self.last)

    def done(self, value):
        self.last = (value,)
        return value

    def take(self, value):
        return self.done(self.at(value))

    def run(self, function, *args, **kwargs):
        return self.done(function(*self.at(args), **kwargs))


class Gather:
    def __init__(self, order, own, n):
        self.order, self.n, self.half, self.step = order, n, n // 2, 0
        self.chunks = {0: own}
        self.now = (own, own)
        self.width = own.shape[1] // 2

    def send(self):
        if self.step == self.half:
            return
        self.step += 1
        right, left = self.now
        if self.step == self.half:
            right, left = right[:, : self.width], left[:, self.width :]
        self.now = (ring_shift(right, 1, self.n), ring_shift(left, -1, self.n))

    def take(self):
        if self.half in self.chunks:
            return
        self.now = right, left = self.order.take(self.now)
        if self.step == self.half:
            self.chunks[self.half] = jnp.concatenate([right, left], axis=1)
        else:
            self.chunks[-self.step], self.chunks[self.step] = right, left

    def rest(self, hops=None):
        while self.step < self.half and hops != 0:
            self.take()
            self.send()
            hops = hops and hops - 1
        return self


class Scatter:
    def __init__(self, order, contrib, n):
        self.order, self.n, self.half, self.step = order, n, n // 2, 0
        self.contrib = contrib
        far = contrib(self.half)
        self.width = far.shape[1] // 2
        self.now = (far[:, : self.width].astype(BF), far[:, self.width :].astype(BF))

    def send(self):
        self.step += 1
        right, left = self.now
        self.now = (ring_shift(right, 1, self.n), ring_shift(left, -1, self.n))

    def take(self):
        self.now = got = self.order.take(self.now)
        r = self.half - self.step
        if r == 0:
            return (self.contrib(0), *got)
        got = [v.astype(F32) for v in got]
        width = self.width
        ahead, behind = self.contrib(r).astype(F32), self.contrib(-r).astype(F32)
        if self.step == 1:
            ahead = jnp.concatenate([ahead[:, :width] + got[0], ahead[:, width:]], axis=1)
            behind = jnp.concatenate([behind[:, :width], behind[:, width:] + got[1]], axis=1)
        else:
            ahead, behind = ahead + got[0], behind + got[1]
        self.now = self.order.done((ahead.astype(BF), behind.astype(BF)))

    def rest(self, hops=None):
        while self.step < self.half and hops != 0:
            self.take()
            self.send()
            hops = hops and hops - 1
        return self


def added(terms):
    return sum(t.astype(F32) for t in terms)


def deinterleave(both):
    runs = range(both.shape[1] // 256)
    return tuple(
        jnp.concatenate([both[:, p * 256 + o : p * 256 + o + 128] for p in runs], axis=1)
        for o in (0, 128)
    )


def turn_tables(block_ids, block, ends, starts):
    place = (block_ids[:, None] * block + jnp.arange(block, dtype=jnp.int32)[None, :]).reshape(-1)
    begin = jnp.max(jnp.where(place[:, None] >= starts[None, :], starts[None, :], 0), axis=1)
    freqs = ROPE_BASE ** (-(jnp.arange(HEAD // 2, dtype=F32) * 2.0 / HEAD))
    angle = (place - begin).astype(F32)[:, None] * freqs[None, :]
    cosine, sine = jnp.cos(angle), jnp.sin(angle)
    return (
        jnp.concatenate([cosine] * 4, axis=1),
        jnp.concatenate([-sine, sine, -sine, sine], axis=1),
    )


def turn_back(values, cosine, sine):
    parts = []
    for p in range(values.shape[1] // 128):
        part = values[:, p * 128 : (p + 1) * 128]
        if p % 2 == 0:
            low = lax.broadcasted_iota(jnp.int32, part.shape, 1) % HEAD < HEAD // 2
            turned = jnp.where(low, jnp.roll(part, -32, axis=1), jnp.roll(part, 32, axis=1))
            part = part * cosine - turned * sine
        parts.append(part)
    return jnp.concatenate(parts, axis=1)


def body(
    n,
    tokens,
    first_gain,
    query_weight,
    key_matrix,
    value_matrix,
    out_weight,
    second_gain,
    gate_weight,
    up_weight,
    down_weight,
    lengths,
    block_order,
    cotangent,
):
    token_rows, model = tokens.shape
    block = token_rows // 2
    c = lax.axis_index("ctx")
    f = lax.axis_index("fsdp")
    place = jnp.where(c % 2 == 0, c // 2, n - 1 - c // 2)
    half = n // 2
    rel = list(range(-(half - 1), half + 1))
    owners = ring_index(place + jnp.asarray(rel, jnp.int32), n)

    own_blocks = lax.dynamic_slice_in_dim(block_order, 2 * c, 2)
    key_blocks = jnp.take(block_order.reshape(n, 2), owners, axis=0).reshape(-1)
    seq_ends = jnp.cumsum(lengths[0])
    count = lengths.shape[1]
    groups = [(-1, 0, 1)] + [(-step, step) for step in range(2, half)] + [(half,)]
    slot_rel = [r for group in (groups[0], groups[-1], *groups[1:-1]) for r in group]
    scalars = jnp.concatenate([f[None], own_blocks, key_blocks, seq_ends]).astype(jnp.int32)
    cosine, sine = turn_tables(own_blocks, block, seq_ends, seq_ends - lengths[0])
    order = Order()

    units = gate_weight.shape[1] // (4 * n)
    span = gate_weight.shape[1] // 4
    width = 4 * units

    def own_units(weight):
        return jnp.concatenate(
            [
                lax.dynamic_slice_in_dim(weight, (f ^ e) * span + c * units, units, 1)
                for e in range(4)
            ],
            axis=1,
        )

    gains = gather_fsdp(jnp.stack([first_gain, second_gain]))
    gains = jnp.concatenate(gains, axis=1).astype(F32)
    gain_one, gain_two = gains[:1], gains[1:]
    out_part = out_weight.shape[0] // n
    out_across = swap_fsdp(lax.dynamic_slice_in_dim(out_weight, c * out_part, out_part, 0), 2)
    key_across, value_across = swap_fsdp(key_matrix, 2), swap_fsdp(value_matrix, 2)
    grad_out = Gather(order, cotangent, n)
    grad_out.send()
    key_core, value_core = swap_fsdp(key_matrix, 1), swap_fsdp(value_matrix, 1)
    out_core, query_core = swap_fsdp(out_weight, 1), swap_fsdp(query_weight, 1)
    def across(value):
        return swap_fsdp(order.at(value), 2)

    def shards(own, core, over):
        return [own, core, over, swap_fsdp(over, 1)]

    hidden_one = order.run(norm_rows, scalars, tokens, gain_one)
    out_across = order.take(out_across)
    out_parts = Gather(order, out_across, n)
    out_parts.send()
    weight_k = shards(key_matrix, key_core, order.take(key_across))
    out_parts.rest(1)
    weight_v = shards(value_matrix, value_core, order.take(value_across))
    query_across = across(query_weight)
    gate_own = order.run(own_units, gate_weight)
    up_own = order.run(own_units, up_weight)
    gate_core, up_core = swap_fsdp(gate_own, 1), swap_fsdp(up_own, 1)
    down_own = order.done(lax.dynamic_slice_in_dim(order.at(down_weight), c * units, units, 0))
    down_core = swap_fsdp(down_own, 1)
    out_parts.rest(1)
    grad_out.take()
    kv_own = order.run(project, hidden_one, cosine, sine, [weight_k, weight_v], turned_tiles=1, scale=1.0, micros=4)
    kv = Gather(order, kv_own, n)
    kv.send()
    kv.rest(1)
    kv.rest(1)
    out_parts.take()
    weight_q = shards(query_weight, query_core, order.take(query_across))
    gate_across = across(gate_own)
    kv.rest()
    kv.take()
    out_parts.send()
    kv_chunks = [kv.chunks[r] for r in rel]

    queries = order.run(project, hidden_one, cosine, sine, [weight_q], turned_tiles=2, scale=0.125, micros=7)
    out_parts.rest()
    out_parts.take()
    gate = shards(gate_own, gate_core, order.take(gate_across))
    up_across = across(up_own)
    grad_out.send()
    out_across = order.run(place_rows, owners.astype(jnp.int32), [out_parts.chunks[r] for r in rel])
    weight_o = shards(out_weight, out_core, out_across)
    mixed, lse = order.run(attention_forward, scalars, queries, kv_chunks, ends=count)
    up = shards(up_own, up_core, order.take(up_across))
    down_across = across(down_own)
    grad_out.take()
    residual, hidden_two = order.run(out_project, scalars, mixed, tokens, gain_two, weight_o)
    hidden = Gather(order, hidden_two, n)
    hidden.send()
    hidden.rest(1)
    grad_out.send()
    down = shards(down_own, down_core, order.take(down_across))
    if units < 128:
        gate = [swap_cols(part, d, 1) for d, part in enumerate(gate)]
        up = [swap_cols(part, d, 1) for d, part in enumerate(up)]
    down = order.done(jnp.concatenate(down, axis=0))

    kept, grads_two = [], {}
    for at, group in enumerate(groups):
        slot = slot_rel.index(group[0]) // len(group)
        kept, sums = order.run(
            feed,
            [hidden.chunks[r] for r in group],
            [grad_out.chunks[r] for r in group],
            gate,
            up,
            down,
            slot=slot,
            kept=kept,
            n=n,
        )
        grads_two.update((r, (sums, i)) for i, r in enumerate(group))
        if at < half - 1:
            hidden.take()
            hidden.send()
            grad_out.take()
            grad_out.send()

    rows_h, rows_dy, act, grads = kept
    tile, crossed = feed_tile(units)
    class Product:
        def __init__(self, left, right, micros, by_units=False):
            self.left, self.right, self.micros, self.by_units = left, right, micros, by_units

        def kernel(self, blocks, kind, adds=(), pieces=1):
            def run(left, right, *arrays):
                own = [(a, *rest) for a, (_, *rest) in zip(arrays, adds)]
                micros = self.micros * len(blocks)
                return tn_blocks(left, right, blocks, kind, micros, own, pieces)

            return order.run(run, self.left, self.right, *[a for a, *_ in adds])

        def from_partner(self, value, d):
            return swap_cols(value, d, 2) if self.by_units and not crossed else value

        def first(self):
            self.near = [
                [swap_fsdp(piece, 1) for piece in row] for row in self.kernel((1, 3), BF, (), 2)
            ]

        def pieces(self, row):
            turned = self.by_units and crossed
            got = [self.from_partner(v, 1) for v in order.take(self.near[row])]
            return [(v, p, len(got), 0, turned) for p, v in enumerate(got)]

        def second(self, halves=1):
            (mid,) = self.kernel((2,), BF, self.pieces(1), halves)
            self.mid = [swap_fsdp(v, 2) for v in mid]

        def settle(self):
            self.mid = order.take(self.mid)

        def last(self, kind):
            over = [self.from_partner(v, 2) for v in order.at(self.mid)]
            flip = 2 if self.by_units and crossed else 0
            adds = [(v, h, len(over), flip, False) for h, v in enumerate(over)]
            ((whole,),) = self.kernel((0,), kind, self.pieces(0) + adds)
            return whole

    def feed_contrib(r):
        value, i = grads_two[r]
        return value[i * token_rows : (i + 1) * token_rows]

    sums = Scatter(order, feed_contrib, n)
    sums.send()
    of_down = Product(act, rows_dy, 3)
    of_gate_up = Product(rows_h, grads, 5, True)
    of_gate_up.first()
    sums.rest(1)
    of_down.first()
    of_gate_up.second()
    sums.rest(1)
    y_rows = order.run(down_rows, act, down, n=n)
    of_down.second()
    sums.rest(1)
    sums.rest()
    grad_hidden_two = sums.take()
    grad_residual, gain_two_term, grad_branch = order.run(
        norm_back, scalars, residual, gain_two, cotangent, grad_hidden_two, rounded=True
    )
    grad_mixed = order.run(back_project, [grad_branch], [weight_o], kind=BF, micros=5)
    of_gate_up.settle()
    gate_up_grad = of_gate_up.last(BF)
    rows = gate_up_grad.shape[0] // n
    gate_up_all = lax.all_to_all(
        gate_up_grad.reshape(n, rows, 2 * width), "ctx", 0, 0, tiled=False
    )
    of_out = Product(mixed, grad_branch, 2)
    of_out.first()

    parts = []

    def attention_part(first):
        parts.append(
            order.run(
                attention_backward,
                scalars,
                queries,
                grad_mixed,
                lse,
                cosine,
                sine,
                kv_chunks,
                ends=count,
                pairs=(first, 2),
            )
        )

    attention_part(0)
    of_down.settle()
    attention_part(2)
    grad_query = jnp.concatenate([p[0] for p in parts], axis=1)

    def kv_contrib(r):
        start = rel.index(r) * token_rows
        return jnp.concatenate([p[1][start : start + token_rows] for p in parts], axis=1)

    def scatter_rows(within):
        rows = within.shape[0] // n

        def contrib(r):
            start = ring_index(place + r, n) * rows
            return lax.dynamic_slice_in_dim(within, start, rows, 0)

        return Scatter(order, contrib, n)

    grad_kv = Scatter(order, kv_contrib, n)
    grad_kv.send()
    of_out.second()
    of_query = Product(hidden_one, grad_query, 2)
    of_query.first()
    gate_up_all = order.take(gate_up_all)
    grad_kv.rest(1)
    grad_hidden_one = order.run(back_project, [grad_query], [weight_q], kind=F32, micros=5)
    grad_kv.rest(1)
    of_query.second()
    grad_kv.rest(1)

    def y_contrib(r):
        start = slot_rel.index(r) * token_rows
        return y_rows[start : start + token_rows]

    def spread_out():
        if crossed:
            return order.run(spread, scalars, gate_up_all, units=units, tile=tile)
        both = gate_up_all.reshape(n, rows, 2, 4, units).transpose(2, 1, 3, 0, 4)
        both = xor_blocks(both, f, 2).reshape(2, rows, n * width).astype(F32)
        return order.done((both[0], both[1]))

    y_sums = Scatter(order, y_contrib, n)
    y_sums.send()
    down_grad = of_down.last(F32)
    of_out.settle()
    out_sums = scatter_rows(of_out.last(BF))
    grad_kv.rest()
    grad_kv = added(grad_kv.take())
    out_sums.send()
    y_sums.rest(1)
    grad_kv = turn_back(grad_kv, cosine, sine).astype(BF)
    grad_key, grad_value = deinterleave(grad_kv)
    grad_kv = jnp.concatenate([grad_key, grad_value], axis=1)
    of_kv = Product(hidden_one, grad_kv, 1.5)
    of_kv.first()
    gate_grad, up_grad = spread_out()
    out_sums.rest(1)
    y_sums.rest(1)
    grad_hidden_one = order.run(
        back_project, [grad_key, grad_value], [weight_k, weight_v], base=grad_hidden_one, kind=F32, micros=3
    )
    of_kv.second()
    out_sums.rest(1)
    tokens_grad, gain_one_term = order.run(
        norm_back, scalars, tokens, gain_one, grad_residual, [grad_hidden_one], rounded=False
    )
    y_sums.rest(1)
    out_sums.rest(1)
    gain_terms = xor_blocks(jnp.concatenate([gain_one_term, gain_two_term], axis=0), f, 1)
    gain_terms = gain_terms.astype(BF).reshape(2, 4 * n, model // (4 * n)).transpose(1, 0, 2)
    gain_terms = lax.all_to_all(gain_terms, ("fsdp", "ctx"), 0, 0, tiled=False)
    of_query.settle()
    query_sums = scatter_rows(of_query.last(BF))
    y_sums.rest()
    layer_out = order.done((residual + added(y_sums.take())).astype(BF))
    query_sums.send()
    out_sums.rest()
    out_grad = order.done(added(out_sums.take()))
    gain_terms = order.take(gain_terms)
    of_kv.settle()
    kv_sums = scatter_rows(of_kv.last(BF))
    query_sums.rest(1)
    kv_sums.send()
    query_sums.rest(1)
    kv_sums.rest(1)
    query_sums.rest(1)
    kv_sums.rest(1)
    query_sums.rest()
    query_sums = query_sums.take()
    kv_sums.rest(1)
    query_grad = order.done(added(query_sums))
    kv_sums.rest()
    kv_grad = order.done(added(kv_sums.take()))
    gain_grads = jnp.sum(gain_terms.astype(F32), axis=0)
    kv_width = key_matrix.shape[1]
    key_grad, value_grad = kv_grad[:, :kv_width], kv_grad[:, kv_width:]
    return (
        layer_out,
        tokens_grad,
        gain_grads[0],
        query_grad,
        key_grad,
        value_grad,
        out_grad,
        gain_grads[1],
        gate_grad,
        up_grad,
        down_grad,
    )


def solution(mesh):
    rows, vector = P(("fsdp", "ctx"), None), P(("fsdp", "ctx"))
    weight = P("fsdp", None)

    def layer(*arrays):
        return body(mesh.shape["ctx"], *arrays)

    return jax.shard_map(
        layer,
        mesh=mesh,
        in_specs=(
            rows, P("fsdp"), weight, weight, weight, weight, P("fsdp"), weight, weight, weight,
            weight, P(), rows,
        ),
        out_specs=(rows, rows, vector, rows, rows, rows, rows, vector, rows, rows, rows),
        check_vma=False,
    )
```

```python
import functools

import jax
import jax.numpy as jnp
from jax import lax
from jax.experimental import pallas as pl
from jax.experimental.pallas import tpu as pltpu
from jax.sharding import PartitionSpec as P

HEAD = 64
NORM_EPS = 1e-05
ROPE_BASE = 500000.0
MASKED = -1e30
VARIANTS = 10
BF = jnp.bfloat16
F32 = jnp.float32
MIB = 2**20


def dot(a, b):
    return jnp.dot(a, b, preferred_element_type=F32)


def dot_nt(a, b):
    return lax.dot_general(a, b, (((1,), (1,)), ((), ())), preferred_element_type=F32)


def fill_bias(sc, bias, own, block, ends_at, ends):
    for j in range(2):
        place = sc[own + j] * block + lax.broadcasted_iota(jnp.int32, bias.shape[1:], 0)
        key = lax.broadcasted_iota(jnp.int32, bias.shape[1:], 1)
        start = jnp.zeros_like(place)
        for s in range(ends):
            end = sc[ends_at + s]
            start = jnp.where(place >= end, end, start)
        bias[j] = jnp.where((key >= start) & (key <= place), 0.0, MASKED)


def fill_keys(sc, chunks, keys, values, block, blocks_at):
    for r, chunk in enumerate(chunks):
        for j in range(2):
            at = pl.multiple_of(sc[blocks_at + 2 * r + j] * block, 16)
            part = chunk[j * block : (j + 1) * block, :]
            for g in range(2):
                keys[g, pl.ds(at, block), :] = part[:, g * HEAD : (g + 1) * HEAD]
                values[g, pl.ds(at, block), :] = part[:, 2 * HEAD + g * HEAD : 2 * HEAD + (g + 1) * HEAD]


def split_heads(ref, out, block, group):
    for g in range(2):
        for j in range(2):
            for h in range(group):
                lane = (g * group + h) * HEAD
                out[g, j, h * block : (h + 1) * block, :] = ref[
                    j * block : (j + 1) * block, lane : lane + HEAD
                ]


def join_heads(out, block, group):
    rows = []
    for j in range(2):
        rows.append(
            jnp.concatenate(
                [out[g, j, h * block : (h + 1) * block, :] for g in range(2) for h in range(group)],
                axis=1,
            )
        )
    return jnp.concatenate(rows, axis=0)


def visible(sc, own, j, block, step):
    return (sc[own + j] * block + block - 1) // step + 1


def forward_kernel(n, group, ends, sc, q_ref, *rest):
    chunks, (o_ref, lse_ref), (bias, keys, values, queries, outs) = (
        rest[:n],
        rest[n : n + 2],
        rest[n + 2 :],
    )
    block = q_ref.shape[0] // 2
    total = keys.shape[1]
    step = total // VARIANTS
    pair = pl.program_id(0)

    @pl.when(pair == 0)
    def _():
        fill_bias(sc, bias, 1, block, 3 + 2 * n, ends)
        lse_ref[...] = jnp.zeros_like(lse_ref)

    fill_keys(sc, chunks, keys, values, block, 3)
    split_heads(q_ref, queries, block, group)

    def one(g, j, length):
        scores = dot_nt(queries[g, j], keys[g, :length, :])
        scores = (scores.reshape(group, block, length) + bias[j, :, :length][None]).reshape(
            group * block, length
        )
        peak = jnp.max(scores, axis=-1, keepdims=True)
        expd = jnp.exp(scores - peak)
        row_total = jnp.sum(expd, axis=-1, keepdims=True)
        mixed = dot(expd.astype(BF), values[g, :length, :])
        outs[g, j] = mixed / row_total
        lse = peak + jnp.log(row_total)
        lane = lax.broadcasted_iota(jnp.int32, (block, lse_ref.shape[1]), 1)
        rows = pl.ds(pl.multiple_of(j * block, 16), block)
        kept = lse_ref[rows, :]
        for h in range(group):
            kept = jnp.where(
                lane == (pair * 2 + g) * group + h, lse[h * block : (h + 1) * block], kept
            )
        lse_ref[rows, :] = kept

    def both(at, carry):
        g, j = at // 2, at % 2
        count = visible(sc, 1, j, block, step)
        for v in range(1, VARIANTS + 1):
            pl.when(count == v)(functools.partial(one, g, j, v * step))
        return carry

    lax.fori_loop(0, 4, both, 0)
    o_ref[...] = join_heads(outs, block, group).astype(o_ref.dtype)


def attention_forward(scalars, queries, chunks, ends):
    n = len(chunks)
    rows, width = queries.shape
    group = width // HEAD // 8
    block, total = rows // 2, rows * n
    pairs = 4
    return pl.pallas_call(
        functools.partial(forward_kernel, n, group, ends),
        grid_spec=pltpu.PrefetchScalarGridSpec(
            num_scalar_prefetch=1,
            grid=(pairs,),
            in_specs=[pl.BlockSpec((rows, width // pairs), lambda p, sc: (0, p))]
            + [pl.BlockSpec((rows, 4 * HEAD), lambda p, sc: (0, p))] * n,
            out_specs=[
                pl.BlockSpec((rows, width // pairs), lambda p, sc: (0, p ^ sc[0])),
                pl.BlockSpec((rows, 128), lambda p, sc: (0, 0)),
            ],
            scratch_shapes=[
                pltpu.VMEM((2, block, total), F32),
                pltpu.VMEM((2, total, HEAD), BF),
                pltpu.VMEM((2, total, HEAD), BF),
                pltpu.VMEM((2, 2, group * block, HEAD), BF),
                pltpu.VMEM((2, 2, group * block, HEAD), F32),
            ],
        ),
        out_shape=[
            jax.ShapeDtypeStruct((rows, width), BF),
            jax.ShapeDtypeStruct((rows, 128), F32),
        ],
        compiler_params=pltpu.CompilerParams(vmem_limit_bytes=48 * 2**20),
        cost_estimate=cost(18),
        name="attention_forward",
    )(scalars, queries, *chunks)


def backward_kernel(n, group, ends, first, sc, q_ref, do_ref, lse_ref, cos_ref, sin_ref, *rest):
    chunks, (dq_ref, dkv_ref), scratch = rest[:n], rest[n : n + 2], rest[n + 2 :]
    bias, keys, values, queries, grads, outs, dkeys, dvalues, flat = scratch
    block = q_ref.shape[0] // 2
    total = keys.shape[1]
    step = total // VARIANTS
    pair = pl.program_id(0) + first

    @pl.when(pair == first)
    def _():
        fill_bias(sc, bias, 1, block, 3 + 2 * n, ends)

    fill_keys(sc, chunks, keys, values, block, 3)
    split_heads(q_ref, queries, block, group)
    split_heads(do_ref, grads, block, group)
    dkeys[...] = jnp.zeros_like(dkeys)
    dvalues[...] = jnp.zeros_like(dvalues)

    def one(g, j, length):
        query, grad = queries[g, j], grads[g, j]
        key, value = keys[g, :length, :], values[g, :length, :]
        rows = pl.ds(pl.multiple_of(j * block, 16), block)
        kept = lse_ref[rows, :]
        lane = lax.broadcasted_iota(jnp.int32, kept.shape, 1)
        lse = jnp.concatenate(
            [
                jnp.sum(
                    jnp.where(lane == (pair * 2 + g) * group + h, kept, 0.0), axis=1, keepdims=True
                )
                for h in range(group)
            ],
            axis=0,
        )
        scores = dot_nt(query, key)
        scores = (scores.reshape(group, block, length) + bias[j, :, :length][None]).reshape(
            group * block, length
        )
        prob = jnp.exp(scores - lse)
        dprob = dot_nt(grad, value)
        weighted = prob * dprob
        row_dot = jnp.sum(weighted, axis=-1, keepdims=True)
        dscore = (weighted - prob * row_dot).astype(BF)
        outs[g, j] = dot(dscore, key)
        dkeys[g, :, :length] += dot(query.T, dscore)
        dvalues[g, :, :length] += dot(grad.T, prob.astype(BF))

    def both(at, carry):
        g, j = at // 2, at % 2
        count = visible(sc, 1, j, block, step)
        for v in range(1, VARIANTS + 1):
            pl.when(count == v)(functools.partial(one, g, j, v * step))
        return carry

    lax.fori_loop(0, 4, both, 0)
    dq = join_heads(outs, block, group) * (1.0 / 8.0)
    cosine, sine = cos_ref[...], sin_ref[...]
    low = lax.broadcasted_iota(jnp.int32, cosine.shape, 1) % HEAD < HEAD // 2
    for t in range(dq.shape[1] // 128):
        part = dq[:, t * 128 : (t + 1) * 128]
        turned = jnp.where(low, pltpu.roll(part, 96, 1), pltpu.roll(part, 32, 1))
        dq_ref[:, t * 128 : (t + 1) * 128] = (part * cosine - turned * sine).astype(dq_ref.dtype)
    flat[:, : 2 * HEAD] = jnp.concatenate([dkeys[0], dkeys[1]], axis=0).T
    flat[:, 2 * HEAD :] = jnp.concatenate([dvalues[0], dvalues[1]], axis=0).T
    for r in range(2 * n):
        at = pl.multiple_of(sc[3 + r] * block, 16)
        dkv_ref[r * block : (r + 1) * block, :] = flat[pl.ds(at, block), :].astype(dkv_ref.dtype)


def attention_backward(scalars, queries, grads, lse, cosine, sine, chunks, ends, pairs):
    n = len(chunks)
    rows, width = queries.shape
    group = width // HEAD // 8
    block, total = rows // 2, rows * n
    first, steps = pairs
    whole = pl.BlockSpec((rows, 128), lambda p, sc: (0, 0))
    wide = pl.BlockSpec((rows, width // 4), lambda p, sc: (0, p + first))
    return pl.pallas_call(
        functools.partial(backward_kernel, n, group, ends, first),
        grid_spec=pltpu.PrefetchScalarGridSpec(
            num_scalar_prefetch=1,
            grid=(steps,),
            in_specs=[
                wide,
                pl.BlockSpec((rows, width // 4), lambda p, sc: (0, (p + first) ^ sc[0])),
                whole,
                whole,
                whole,
            ]
            + [pl.BlockSpec((rows, 4 * HEAD), lambda p, sc: (0, p + first))] * n,
            out_specs=[
                pl.BlockSpec((rows, width // 4), lambda p, sc: (0, p)),
                pl.BlockSpec((total, 4 * HEAD), lambda p, sc: (0, p)),
            ],
            scratch_shapes=[
                pltpu.VMEM((2, block, total), F32),
                pltpu.VMEM((2, total, HEAD), BF),
                pltpu.VMEM((2, total, HEAD), BF),
                pltpu.VMEM((2, 2, group * block, HEAD), BF),
                pltpu.VMEM((2, 2, group * block, HEAD), BF),
                pltpu.VMEM((2, 2, group * block, HEAD), F32),
                pltpu.VMEM((2, HEAD, total), F32),
                pltpu.VMEM((2, HEAD, total), F32),
                pltpu.VMEM((total, 4 * HEAD), F32),
            ],
        ),
        out_shape=[
            jax.ShapeDtypeStruct((rows, steps * width // 4), BF),
            jax.ShapeDtypeStruct((total, steps * 4 * HEAD), BF),
        ],
        compiler_params=pltpu.CompilerParams(vmem_limit_bytes=56 * 2**20),
        cost_estimate=cost(26),
        name="attention_backward",
    )(scalars, queries, grads, lse, cosine, sine, *chunks)


def params(mib):
    return pltpu.CompilerParams(vmem_limit_bytes=mib * MIB)


def cost(micros):
    return pl.CostEstimate(flops=int(micros * 1e7), bytes_accessed=0, transcendentals=0)


def row_scale(values):
    return lax.rsqrt(jnp.mean(values * values, axis=-1, keepdims=True) + NORM_EPS)


def quarter(f, d, size):
    return pl.ds(pl.multiple_of((f ^ d) * size, size), size)


def norm_kernel(f_ref, x_ref, gain_ref, h_ref):
    inverse = row_scale(x_ref[...].astype(F32))
    size = x_ref.shape[1] // 4
    for d in range(4):
        part = x_ref[:, quarter(f_ref[0], d, size)].astype(F32) * inverse
        h_ref[:, d * size : (d + 1) * size] = (
            part * gain_ref[:, d * size : (d + 1) * size]
        ).astype(BF)


def smem():
    return pl.BlockSpec(memory_space=pltpu.SMEM)


def vmem():
    return pl.BlockSpec(memory_space=pltpu.VMEM)


def norm_rows(scalars, rows, gain):
    return pl.pallas_call(
        norm_kernel,
        in_specs=[smem(), vmem(), vmem()],
        out_specs=vmem(),
        out_shape=jax.ShapeDtypeStruct(rows.shape, BF),
        compiler_params=params(32),
        cost_estimate=cost(1),
        name="norm_rows",
    )(scalars, rows, gain)


def project_kernel(scale, turned_tiles, x_ref, cos_ref, sin_ref, *refs):
    weights, out_ref = refs[:-1], refs[-1]
    size = x_ref.shape[1] // 4
    parts = []
    for at in range(0, len(weights), 4):
        parts.append(
            sum(
                dot(x_ref[:, d * size : (d + 1) * size], w[...])
                for d, w in enumerate(weights[at : at + 4])
            )
        )
    cosine, sine = cos_ref[...], sin_ref[...]
    low = lax.broadcasted_iota(jnp.int32, cosine.shape, 1) % HEAD < HEAD // 2
    tiles = [p[:, t * 128 : (t + 1) * 128] for p in parts for t in range(p.shape[1] // 128)]
    for t, part in enumerate(tiles):
        if t < turned_tiles:
            turned = jnp.where(low, pltpu.roll(part, 96, 1), pltpu.roll(part, 32, 1))
            part = part * cosine + turned * sine
        part = part.astype(BF)
        if scale != 1.0:
            part = (part.astype(F32) * scale).astype(BF)
        out_ref[:, t * 128 : (t + 1) * 128] = part


def project(rows, cosine, sine, weights, turned_tiles, scale, micros):
    count, depth = rows.shape
    size, width = weights[0][0].shape
    run = 512 // len(weights)
    part = run // len(weights)
    whole = lambda a: pl.BlockSpec(a.shape, lambda j: (0, 0))
    return pl.pallas_call(
        functools.partial(project_kernel, scale, turned_tiles),
        grid=(width // part,),
        in_specs=[whole(rows), whole(cosine), whole(sine)]
        + [pl.BlockSpec((size, part), lambda j: (0, j))] * (4 * len(weights)),
        out_specs=pl.BlockSpec((count, run), lambda j: (0, j)),
        out_shape=jax.ShapeDtypeStruct((count, width * len(weights)), BF),
        compiler_params=params(32),
        cost_estimate=cost(micros),
        name="project",
    )(rows, cosine, sine, *[w for shards in weights for w in shards])


def out_kernel(f_ref, o_ref, x_ref, gain_ref, w0, w1, w2, w3, r_ref, h_ref):
    size = o_ref.shape[1] // 4
    tile = w0.shape[1]
    total = sum(
        dot(o_ref[:, d * size : (d + 1) * size], w[...]) for d, w in enumerate((w0, w1, w2, w3))
    )
    at = pl.ds(pl.multiple_of(pl.program_id(0) * tile, tile), tile)
    r_ref[:, at] = x_ref[:, at].astype(F32) + total

    @pl.when(pl.program_id(0) == pl.num_programs(0) - 1)
    def _():
        norm_kernel(f_ref, r_ref, gain_ref, h_ref)


def out_project(scalars, mixed, tokens, gain, weights):
    count, depth = mixed.shape
    size, width = weights[0].shape
    whole = lambda a: pl.BlockSpec(a.shape, lambda j: (0, 0))
    return pl.pallas_call(
        out_kernel,
        grid=(width // 512,),
        in_specs=[smem(), whole(mixed), whole(tokens), whole(gain)]
        + [pl.BlockSpec((size, 512), lambda j: (0, j))] * 4,
        out_specs=[whole(tokens), whole(tokens)],
        out_shape=[
            jax.ShapeDtypeStruct((count, width), F32),
            jax.ShapeDtypeStruct((count, width), BF),
        ],
        compiler_params=params(32),
        cost_estimate=cost(6),
        name="out_project",
    )(scalars, mixed, tokens, gain, *weights)


def norm_back_kernel(wide, f_ref, x_ref, gain_ref, base_ref, *rest):
    terms, outs = rest[:-wide], rest[-wide:]
    x = x_ref[...].astype(F32)
    inverse = row_scale(x)
    size = x_ref.shape[1] // 4
    f = f_ref[0]
    grads, normed = [], []
    dot_sum = 0.0
    for d in range(4):
        cols = slice(d * size, (d + 1) * size)
        grad = sum(t[:, cols].astype(F32) for t in terms)
        part = x_ref[:, quarter(f, d, size)].astype(F32) * inverse
        outs[1][:, cols] = jnp.sum(grad * part, axis=0, keepdims=True)
        grad = grad * gain_ref[:, cols]
        dot_sum += jnp.sum(grad * part, axis=-1, keepdims=True)
        grads.append(grad)
        normed.append(part)
    mean = dot_sum / x_ref.shape[1]
    for d in range(4):
        at = quarter(f, d, size)
        value = base_ref[:, at].astype(F32) + inverse * (grads[d] - normed[d] * mean)
        outs[0][:, at] = value
        if wide == 3:
            outs[2][:, at] = value.astype(BF)


def norm_back(scalars, rows, gain, base, terms, rounded):
    wide = 3 if rounded else 2
    shapes = [
        jax.ShapeDtypeStruct(rows.shape, F32),
        jax.ShapeDtypeStruct((1, rows.shape[1]), F32),
        jax.ShapeDtypeStruct(rows.shape, BF),
    ][:wide]
    return pl.pallas_call(
        functools.partial(norm_back_kernel, wide),
        in_specs=[smem()] + [vmem()] * (3 + len(terms)),
        out_specs=[vmem()] * wide,
        out_shape=shapes,
        compiler_params=params(40),
        cost_estimate=cost(2),
        name="norm_back",
    )(scalars, rows, gain, base, *terms)


def back_kernel(pairs, based, *refs):
    out_ref = refs[-1]
    step = pl.program_id(0)
    tile = refs[pairs].shape[0]
    size = tile * pl.num_programs(0)
    for d in range(4):
        at = pl.ds(pl.multiple_of(d * size + step * tile, tile), tile)
        total = sum(dot_nt(refs[i][...], refs[pairs + 4 * i + d][...]) for i in range(pairs))
        if based:
            total += refs[5 * pairs][:, at]
        out_ref[:, at] = total.astype(out_ref.dtype)


def back_project(rows, weights, kind, micros, base=None):
    count = rows[0].shape[0]
    size = weights[0][0].shape[0]
    whole = pl.BlockSpec((count, 4 * size), lambda j: (0, 0))
    extra = [] if base is None else [base]
    return pl.pallas_call(
        functools.partial(back_kernel, len(rows), base is not None),
        grid=(2,),
        in_specs=[pl.BlockSpec(r.shape, lambda j: (0, 0)) for r in rows]
        + [pl.BlockSpec((size // 2, w.shape[1]), lambda j: (j, 0)) for ws in weights for w in ws]
        + [whole] * len(extra),
        out_specs=whole,
        out_shape=jax.ShapeDtypeStruct((count, 4 * size), kind),
        compiler_params=params(40 if len(rows) == 1 else 60),
        cost_estimate=cost(micros),
        name="back_project",
    )(*rows, *[w for ws in weights for w in ws], *extra)


def cross(value):
    half = value.shape[1] // 2
    return jnp.concatenate([value[:, half:], value[:, :half]], axis=1)


def feed_kernel(m, kept, crossed, *refs):
    hidden, grads = refs[:m], refs[m : 2 * m]
    gates, ups = refs[2 * m : 2 * m + 4], refs[2 * m + 4 : 2 * m + 8]
    down_ref = refs[2 * m + 8]
    outs = refs[2 * m + 9 + kept :]
    rows_h, rows_dy, act_ref, dgu_ref, dh_ref, h_s, dy_s, dh_s = outs
    step = pl.program_id(0)
    count = hidden[0].shape[0]
    size = gates[0].shape[0]
    tile = gates[0].shape[1]

    @pl.when(step == 0)
    def _():
        for i in range(m):
            at = slice(i * count, (i + 1) * count)
            h_s[at], dy_s[at] = hidden[i][...], grads[i][...]
            rows_h[at], rows_dy[at] = hidden[i][...], grads[i][...]

    def ahead(weights):
        parts = [dot(h_s[:, d * size : (d + 1) * size], w[...]) for d, w in enumerate(weights)]
        if not crossed:
            return sum(parts)
        return parts[0] + parts[2] + cross(parts[1] + parts[3])

    gate, up = ahead(gates), ahead(ups)
    sig = jax.nn.sigmoid(gate)
    silu = gate * sig
    act_ref[...] = (silu * up).astype(BF)
    grad_act = dot_nt(dy_s[...], down_ref[...])
    grad_gate = (grad_act * up * sig * (1.0 + gate * (1.0 - sig))).astype(BF)
    grad_up = (grad_act * silu).astype(BF)
    dgu_ref[:, :tile] = grad_gate
    dgu_ref[:, tile:] = grad_up
    pairs = [(grad_gate, grad_up)] * 4
    if crossed:
        pairs[1] = pairs[3] = (cross(grad_gate), cross(grad_up))
    last = pl.num_programs(0) - 1
    for d in range(4):
        cols = slice(d * size, (d + 1) * size)
        dh = dot_nt(pairs[d][0], gates[d][...]) + dot_nt(pairs[d][1], ups[d][...])

        @pl.when(step == 0)
        def _():
            dh_s[:, cols] = dh

        @pl.when(step > 0)
        def _():
            dh_s[:, cols] += dh

    @pl.when(step == last)
    def _():
        dh_ref[...] = dh_s[...].astype(BF)


def feed_tile(units):
    crossed = units >= 128
    return (2 * units if crossed else 4 * units), crossed


def feed(hidden, grads, gate, up, down, slot, kept, n):
    m = len(hidden)
    count, depth = hidden[0].shape
    width = down.shape[0]
    tile, crossed = feed_tile(width // 4)
    steps = width // tile
    rows = m * count
    size = depth // 4

    def shard(d):
        flip = d >> 1 if crossed else 0
        return pl.BlockSpec((size, tile), lambda e: (0, e ^ flip))

    chunk = pl.BlockSpec((count, depth), lambda e: (0, 0))
    block = pl.BlockSpec((rows, depth), lambda e: (slot, 0))
    shapes = [
        jax.ShapeDtypeStruct((n * count, depth), BF),
        jax.ShapeDtypeStruct((n * count, depth), BF),
        jax.ShapeDtypeStruct((n * count, width), BF),
        jax.ShapeDtypeStruct((n * count, 2 * width), BF),
        jax.ShapeDtypeStruct((rows, depth), BF),
    ]
    first = 2 * m + 9
    *kept, dh = pl.pallas_call(
        functools.partial(feed_kernel, m, len(kept), crossed),
        grid=(steps,),
        in_specs=[chunk] * (2 * m)
        + [shard(d) for d in range(4)] * 2
        + [pl.BlockSpec((tile, depth), lambda e: (e, 0))]
        + [pl.BlockSpec(memory_space=pl.ANY)] * len(kept),
        out_specs=[
            block,
            block,
            pl.BlockSpec((rows, tile), lambda e: (slot, e)),
            pl.BlockSpec((rows, 2 * tile), lambda e: (slot, e)),
            pl.BlockSpec((rows, depth), lambda e: (0, 0)),
        ],
        scratch_shapes=[pltpu.VMEM((rows, depth), BF)] * 2 + [pltpu.VMEM((rows, depth), F32)],
        out_shape=shapes,
        input_output_aliases={first + i: i for i in range(len(kept))},
        compiler_params=params(48),
        cost_estimate=cost(8 + 4 * m),
        name="feed",
    )(*hidden, *grads, *gate, *up, down, *kept)
    return kept, dh


def down_kernel(act_ref, down_ref, y_ref):
    y_ref[...] = dot(act_ref[...], down_ref[...]).astype(BF)


def down_rows(act, down, n):
    count = act.shape[0] // n
    return pl.pallas_call(
        down_kernel,
        grid=(n // 2,),
        in_specs=[
            pl.BlockSpec((2 * count, act.shape[1]), lambda i: (i, 0)),
            pl.BlockSpec(down.shape, lambda i: (0, 0)),
        ],
        out_specs=pl.BlockSpec((2 * count, down.shape[1]), lambda i: (i, 0)),
        out_shape=jax.ShapeDtypeStruct((n * count, down.shape[1]), BF),
        compiler_params=params(32),
        cost_estimate=cost(8),
        name="down_rows",
    )(act, down)


def place_kernel(sc, *refs):
    out = refs[-1]
    count = refs[0].shape[0]
    for i, part in enumerate(refs[:-1]):
        out[pl.ds(pl.multiple_of(sc[i] * count, count), count), :] = part[...]


def place_rows(places, parts):
    count, width = parts[0].shape
    return pl.pallas_call(
        place_kernel,
        in_specs=[smem()] + [vmem()] * len(parts),
        out_specs=vmem(),
        out_shape=jax.ShapeDtypeStruct((count * len(parts), width), parts[0].dtype),
        compiler_params=params(24),
        cost_estimate=cost(2),
        name="place_rows",
    )(places, *parts)


def tn_kernel(adds, outs, left_ref, right_ref, *refs):
    turned = refs[-1]
    i, j = pl.program_id(0), pl.program_id(1)

    @pl.when(j == 0)
    def _():
        turned[...] = left_ref[...].T

    total = dot(turned[...], right_ref[...])
    for (low, high, crossed), extra in zip(adds, refs):
        extra = extra[...].astype(F32)
        if crossed:
            extra = cross(extra)
        if low is not None:
            extra = jnp.where((j >= low) & (j < high), extra, 0.0)
        total += extra
    for (row, low, high), out in zip(outs, refs[len(adds) :]):

        @pl.when((i == row) & (j >= low) & (j < high))
        def _():
            out[...] = total.astype(out.dtype)


def tn_blocks(left, right, blocks, kind, micros, adds=(), pieces=1):
    rows, depth = left.shape
    size, width = depth // 4, right.shape[1]
    tile = min(width, 512)
    steps = width // tile
    pieces = min(pieces, steps)
    if size % 128:
        result = []
        for block in blocks:
            total = lax.dot_general(
                left[:, block * size : (block + 1) * size],
                right,
                (((0,), (0,)), ((), ())),
                preferred_element_type=F32,
            )
            for array, part, parts, _, _ in adds:
                at = part * (width // parts)
                total = total.at[:, at : at + width // parts].add(array.astype(F32))
            result.append(jnp.split(total.astype(kind), pieces, axis=1))
        return result
    first = blocks[0]
    stride = blocks[1] - first if len(blocks) > 1 else 0

    def window(part, parts):
        count = max(1, steps // parts)
        return part * count, (part + 1) * count

    def added_spec(part, parts, flip):
        low, high = window(part, parts)
        if parts == 1:
            return pl.BlockSpec((size, tile), lambda i, j: (0, j ^ flip))
        return pl.BlockSpec((size, tile), lambda i, j: (0, jnp.clip(j - low, 0, high - low - 1)))

    def out_spec(row, low, high):
        def index(i, j):
            at = jnp.clip(j - low, 0, high - low - 1)
            return (0, jnp.where(i < row, 0, jnp.where(i > row, high - low - 1, at)))

        return pl.BlockSpec((size, tile), index)

    windows = [
        (*(window(part, parts) if parts > 1 and steps > 1 else (None, None)), crossed)
        for _, part, parts, _, crossed in adds
    ]
    outs = [(row, *window(piece, pieces)) for row in range(len(blocks)) for piece in range(pieces)]
    result = pl.pallas_call(
        functools.partial(tn_kernel, windows, outs),
        grid=(len(blocks), steps),
        in_specs=[
            pl.BlockSpec((rows, size), lambda i, j: (0, first + stride * i)),
            pl.BlockSpec((rows, tile), lambda i, j: (0, j)),
        ]
        + [added_spec(part, parts, flip) for _, part, parts, flip, _ in adds],
        out_specs=[out_spec(*out) for out in outs],
        out_shape=[jax.ShapeDtypeStruct((size, width // pieces), kind)] * len(outs),
        scratch_shapes=[pltpu.VMEM((size, rows), BF)],
        compiler_params=params(32),
        cost_estimate=cost(micros),
        name="tn_blocks",
    )(left, right, *[a[0] for a in adds])
    return [list(result[row * pieces : (row + 1) * pieces]) for row in range(len(blocks))]


def spread_kernel(units, tile, f_ref, all_ref, *outs):
    span = outs[0].shape[1] // 4
    c = pl.program_id(0)
    for e in range(4):
        step, at = divmod(e * units, tile)
        start = (f_ref[0] ^ e) * span + c * units
        for part in range(2):
            low = (2 * step + part) * tile + at
            value = all_ref[0, :, low : low + units].astype(F32)
            outs[part][:, pl.ds(pl.multiple_of(start, units), units)] = value


def spread(scalars, gathered, units, tile):
    n, rows, _ = gathered.shape
    width = 4 * n * units
    return pl.pallas_call(
        functools.partial(spread_kernel, units, tile),
        grid=(n,),
        in_specs=[smem(), pl.BlockSpec((1, *gathered.shape[1:]), lambda i: (i, 0, 0))],
        out_specs=[pl.BlockSpec((rows, width), lambda i: (0, 0))] * 2,
        out_shape=[jax.ShapeDtypeStruct((rows, width), F32)] * 2,
        compiler_params=params(32),
        cost_estimate=cost(4),
        name="spread",
    )(scalars, gathered)


def swap_fsdp(value, d):
    return lax.ppermute(value, "fsdp", [(i, i ^ d) for i in range(4)])


def after(value, *others):
    return lax.optimization_barrier((value, others))[0] if others else value


def gather_fsdp(shard):
    across = swap_fsdp(shard, 2)
    return [shard, swap_fsdp(shard, 1), across, swap_fsdp(across, 1)]


def xor_blocks(value, f, axis):
    size = value.shape[axis] // 4
    return jnp.concatenate(
        [lax.dynamic_slice_in_dim(value, (f ^ d) * size, size, axis) for d in range(4)], axis=axis
    )


def swap_cols(value, d, parts):
    width = value.shape[1] // (4 * parts)
    return jnp.concatenate(
        [
            value[:, (p * 4 + (e ^ d)) * width : (p * 4 + (e ^ d) + 1) * width]
            for p in range(parts)
            for e in range(4)
        ],
        axis=1,
    )


def ring_index(place, n):
    place = place % n
    return jnp.where(place < n // 2, 2 * place, 2 * (n - 1 - place) + 1)


def ring_shift(value, step, n):
    order = list(range(0, n, 2)) + list(range(n - 1, 0, -2))
    return lax.ppermute(value, "ctx", [(order[i], order[(i + step) % n]) for i in range(n)])


class Order:
    def __init__(self):
        self.last = ()

    def at(self, value):
        return after(value, *self.last)

    def done(self, value):
        self.last = (value,)
        return value

    def take(self, value):
        return self.done(self.at(value))

    def run(self, function, *args, **kwargs):
        return self.done(function(*self.at(args), **kwargs))


class Gather:
    def __init__(self, order, own, n):
        self.order, self.n, self.half, self.step = order, n, n // 2, 0
        self.chunks = {0: own}
        self.now = (own, own)
        self.width = own.shape[1] // 2

    def send(self):
        if self.step == self.half:
            return
        self.step += 1
        right, left = self.now
        if self.step == self.half:
            right, left = right[:, : self.width], left[:, self.width :]
        self.now = (ring_shift(right, 1, self.n), ring_shift(left, -1, self.n))

    def take(self):
        if self.half in self.chunks:
            return
        self.now = right, left = self.order.take(self.now)
        if self.step == self.half:
            self.chunks[self.half] = jnp.concatenate([right, left], axis=1)
        else:
            self.chunks[-self.step], self.chunks[self.step] = right, left

    def rest(self, hops=None):
        while self.step < self.half and hops != 0:
            self.take()
            self.send()
            hops = hops and hops - 1
        return self


class Scatter:
    def __init__(self, order, contrib, n):
        self.order, self.n, self.half, self.step = order, n, n // 2, 0
        self.contrib = contrib
        far = contrib(self.half)
        self.width = far.shape[1] // 2
        self.now = (far[:, : self.width].astype(BF), far[:, self.width :].astype(BF))

    def send(self):
        self.step += 1
        right, left = self.now
        self.now = (ring_shift(right, 1, self.n), ring_shift(left, -1, self.n))

    def take(self):
        self.now = got = self.order.take(self.now)
        r = self.half - self.step
        if r == 0:
            return (self.contrib(0), *got)
        got = [v.astype(F32) for v in got]
        width = self.width
        ahead, behind = self.contrib(r).astype(F32), self.contrib(-r).astype(F32)
        if self.step == 1:
            ahead = jnp.concatenate([ahead[:, :width] + got[0], ahead[:, width:]], axis=1)
            behind = jnp.concatenate([behind[:, :width], behind[:, width:] + got[1]], axis=1)
        else:
            ahead, behind = ahead + got[0], behind + got[1]
        self.now = self.order.done((ahead.astype(BF), behind.astype(BF)))

    def rest(self, hops=None):
        while self.step < self.half and hops != 0:
            self.take()
            self.send()
            hops = hops and hops - 1
        return self


def added(terms):
    return sum(t.astype(F32) for t in terms)


def deinterleave(both):
    runs = range(both.shape[1] // 256)
    return tuple(
        jnp.concatenate([both[:, p * 256 + o : p * 256 + o + 128] for p in runs], axis=1)
        for o in (0, 128)
    )


def turn_tables(block_ids, block, ends, starts):
    place = (block_ids[:, None] * block + jnp.arange(block, dtype=jnp.int32)[None, :]).reshape(-1)
    begin = jnp.max(jnp.where(place[:, None] >= starts[None, :], starts[None, :], 0), axis=1)
    freqs = ROPE_BASE ** (-(jnp.arange(HEAD // 2, dtype=F32) * 2.0 / HEAD))
    angle = (place - begin).astype(F32)[:, None] * freqs[None, :]
    cosine, sine = jnp.cos(angle), jnp.sin(angle)
    return (
        jnp.concatenate([cosine] * 4, axis=1),
        jnp.concatenate([-sine, sine, -sine, sine], axis=1),
    )


def turn_back(values, cosine, sine):
    parts = []
    for p in range(values.shape[1] // 128):
        part = values[:, p * 128 : (p + 1) * 128]
        if p % 2 == 0:
            low = lax.broadcasted_iota(jnp.int32, part.shape, 1) % HEAD < HEAD // 2
            turned = jnp.where(low, jnp.roll(part, -32, axis=1), jnp.roll(part, 32, axis=1))
            part = part * cosine - turned * sine
        parts.append(part)
    return jnp.concatenate(parts, axis=1)


def body(
    n,
    tokens,
    first_gain,
    query_weight,
    key_matrix,
    value_matrix,
    out_weight,
    second_gain,
    gate_weight,
    up_weight,
    down_weight,
    lengths,
    block_order,
    cotangent,
):
    token_rows, model = tokens.shape
    block = token_rows // 2
    c = lax.axis_index("ctx")
    f = lax.axis_index("fsdp")
    place = jnp.where(c % 2 == 0, c // 2, n - 1 - c // 2)
    half = n // 2
    rel = list(range(-(half - 1), half + 1))
    owners = ring_index(place + jnp.asarray(rel, jnp.int32), n)

    own_blocks = lax.dynamic_slice_in_dim(block_order, 2 * c, 2)
    key_blocks = jnp.take(block_order.reshape(n, 2), owners, axis=0).reshape(-1)
    seq_ends = jnp.cumsum(lengths[0])
    count = lengths.shape[1]
    groups = [(-1, 0, 1)] + [(-step, step) for step in range(2, half)] + [(half,)]
    slot_rel = [r for group in (groups[0], groups[-1], *groups[1:-1]) for r in group]
    scalars = jnp.concatenate([f[None], own_blocks, key_blocks, seq_ends]).astype(jnp.int32)
    cosine, sine = turn_tables(own_blocks, block, seq_ends, seq_ends - lengths[0])
    order = Order()

    units = gate_weight.shape[1] // (4 * n)
    span = gate_weight.shape[1] // 4
    width = 4 * units

    def own_units(weight):
        return jnp.concatenate(
            [
                lax.dynamic_slice_in_dim(weight, (f ^ e) * span + c * units, units, 1)
                for e in range(4)
            ],
            axis=1,
        )

    gains = gather_fsdp(jnp.stack([first_gain, second_gain]))
    gains = jnp.concatenate(gains, axis=1).astype(F32)
    gain_one, gain_two = gains[:1], gains[1:]
    out_part = out_weight.shape[0] // n
    out_across = swap_fsdp(lax.dynamic_slice_in_dim(out_weight, c * out_part, out_part, 0), 2)
    key_across, value_across = swap_fsdp(key_matrix, 2), swap_fsdp(value_matrix, 2)
    grad_out = Gather(order, cotangent, n)
    grad_out.send()
    key_core, value_core = swap_fsdp(key_matrix, 1), swap_fsdp(value_matrix, 1)
    out_core, query_core = swap_fsdp(out_weight, 1), swap_fsdp(query_weight, 1)
    def across(value):
        return swap_fsdp(order.at(value), 2)

    def shards(own, core, over):
        return [own, core, over, swap_fsdp(over, 1)]

    hidden_one = order.run(norm_rows, scalars, tokens, gain_one)
    out_across = order.take(out_across)
    out_parts = Gather(order, out_across, n)
    out_parts.send()
    weight_k = shards(key_matrix, key_core, order.take(key_across))
    out_parts.rest(1)
    weight_v = shards(value_matrix, value_core, order.take(value_across))
    query_across = across(query_weight)
    gate_own = order.run(own_units, gate_weight)
    up_own = order.run(own_units, up_weight)
    gate_core, up_core = swap_fsdp(gate_own, 1), swap_fsdp(up_own, 1)
    down_own = order.done(lax.dynamic_slice_in_dim(order.at(down_weight), c * units, units, 0))
    down_core = swap_fsdp(down_own, 1)
    out_parts.rest(1)
    grad_out.take()
    kv_own = order.run(project, hidden_one, cosine, sine, [weight_k, weight_v], turned_tiles=1, scale=1.0, micros=4)
    kv = Gather(order, kv_own, n)
    kv.send()
    kv.rest(1)
    kv.rest(1)
    out_parts.take()
    weight_q = shards(query_weight, query_core, order.take(query_across))
    gate_across = across(gate_own)
    kv.rest()
    kv.take()
    out_parts.send()
    kv_chunks = [kv.chunks[r] for r in rel]

    queries = order.run(project, hidden_one, cosine, sine, [weight_q], turned_tiles=4, scale=0.125, micros=7)
    out_parts.rest()
    out_parts.take()
    gate = shards(gate_own, gate_core, order.take(gate_across))
    up_across = across(up_own)
    grad_out.send()
    out_across = order.run(place_rows, owners.astype(jnp.int32), [out_parts.chunks[r] for r in rel])
    weight_o = shards(out_weight, out_core, out_across)
    mixed, lse = order.run(attention_forward, scalars, queries, kv_chunks, ends=count)
    up = shards(up_own, up_core, order.take(up_across))
    down_across = across(down_own)
    grad_out.take()
    residual, hidden_two = order.run(out_project, scalars, mixed, tokens, gain_two, weight_o)
    hidden = Gather(order, hidden_two, n)
    hidden.send()
    hidden.rest(1)
    grad_out.send()
    down = shards(down_own, down_core, order.take(down_across))
    if units < 128:
        gate = [swap_cols(part, d, 1) for d, part in enumerate(gate)]
        up = [swap_cols(part, d, 1) for d, part in enumerate(up)]
    down = order.done(jnp.concatenate(down, axis=0))

    kept, grads_two = [], {}
    for at, group in enumerate(groups):
        slot = slot_rel.index(group[0]) // len(group)
        kept, sums = order.run(
            feed,
            [hidden.chunks[r] for r in group],
            [grad_out.chunks[r] for r in group],
            gate,
            up,
            down,
            slot=slot,
            kept=kept,
            n=n,
        )
        grads_two.update((r, (sums, i)) for i, r in enumerate(group))
        if at < half - 1:
            hidden.take()
            hidden.send()
            grad_out.take()
            grad_out.send()

    rows_h, rows_dy, act, grads = kept
    tile, crossed = feed_tile(units)
    class Product:
        def __init__(self, left, right, micros, by_units=False):
            self.left, self.right, self.micros, self.by_units = left, right, micros, by_units

        def kernel(self, blocks, kind, adds=(), pieces=1):
            def run(left, right, *arrays):
                own = [(a, *rest) for a, (_, *rest) in zip(arrays, adds)]
                micros = self.micros * len(blocks)
                return tn_blocks(left, right, blocks, kind, micros, own, pieces)

            return order.run(run, self.left, self.right, *[a for a, *_ in adds])

        def from_partner(self, value, d):
            return swap_cols(value, d, 2) if self.by_units and not crossed else value

        def first(self):
            self.near = [
                [swap_fsdp(piece, 1) for piece in row] for row in self.kernel((1, 3), BF, (), 2)
            ]

        def pieces(self, row):
            turned = self.by_units and crossed
            got = [self.from_partner(v, 1) for v in order.take(self.near[row])]
            return [(v, p, len(got), 0, turned) for p, v in enumerate(got)]

        def second(self, halves=1):
            (mid,) = self.kernel((2,), BF, self.pieces(1), halves)
            self.mid = [swap_fsdp(v, 2) for v in mid]

        def settle(self):
            self.mid = order.take(self.mid)

        def last(self, kind):
            over = [self.from_partner(v, 2) for v in order.at(self.mid)]
            flip = 2 if self.by_units and crossed else 0
            adds = [(v, h, len(over), flip, False) for h, v in enumerate(over)]
            ((whole,),) = self.kernel((0,), kind, self.pieces(0) + adds)
            return whole

    def feed_contrib(r):
        value, i = grads_two[r]
        return value[i * token_rows : (i + 1) * token_rows]

    sums = Scatter(order, feed_contrib, n)
    sums.send()
    of_down = Product(act, rows_dy, 3)
    of_gate_up = Product(rows_h, grads, 5, True)
    of_gate_up.first()
    sums.rest(1)
    of_down.first()
    of_gate_up.second()
    sums.rest(1)
    y_rows = order.run(down_rows, act, down, n=n)
    of_down.second()
    sums.rest(1)
    sums.rest()
    grad_hidden_two = sums.take()
    grad_residual, gain_two_term, grad_branch = order.run(
        norm_back, scalars, residual, gain_two, cotangent, grad_hidden_two, rounded=True
    )
    grad_mixed = order.run(back_project, [grad_branch], [weight_o], kind=BF, micros=5)
    of_gate_up.settle()
    gate_up_grad = of_gate_up.last(BF)
    rows = gate_up_grad.shape[0] // n
    gate_up_all = lax.all_to_all(
        gate_up_grad.reshape(n, rows, 2 * width), "ctx", 0, 0, tiled=False
    )
    of_out = Product(mixed, grad_branch, 2)
    of_out.first()

    parts = []

    def attention_part(first):
        parts.append(
            order.run(
                attention_backward,
                scalars,
                queries,
                grad_mixed,
                lse,
                cosine,
                sine,
                kv_chunks,
                ends=count,
                pairs=(first, 2),
            )
        )

    attention_part(0)
    of_down.settle()
    attention_part(2)
    grad_query = jnp.concatenate([p[0] for p in parts], axis=1)

    def kv_contrib(r):
        start = rel.index(r) * token_rows
        return jnp.concatenate([p[1][start : start + token_rows] for p in parts], axis=1)

    def scatter_rows(within):
        rows = within.shape[0] // n

        def contrib(r):
            start = ring_index(place + r, n) * rows
            return lax.dynamic_slice_in_dim(within, start, rows, 0)

        return Scatter(order, contrib, n)

    grad_kv = Scatter(order, kv_contrib, n)
    grad_kv.send()
    of_out.second()
    of_query = Product(hidden_one, grad_query, 2)
    of_query.first()
    gate_up_all = order.take(gate_up_all)
    grad_kv.rest(1)
    grad_hidden_one = order.run(back_project, [grad_query], [weight_q], kind=F32, micros=5)
    grad_kv.rest(1)
    of_query.second()
    grad_kv.rest(1)

    def y_contrib(r):
        start = slot_rel.index(r) * token_rows
        return y_rows[start : start + token_rows]

    def spread_out():
        if crossed:
            return order.run(spread, scalars, gate_up_all, units=units, tile=tile)
        both = gate_up_all.reshape(n, rows, 2, 4, units).transpose(2, 1, 3, 0, 4)
        both = xor_blocks(both, f, 2).reshape(2, rows, n * width).astype(F32)
        return order.done((both[0], both[1]))

    y_sums = Scatter(order, y_contrib, n)
    y_sums.send()
    down_grad = of_down.last(F32)
    of_out.settle()
    out_sums = scatter_rows(of_out.last(BF))
    grad_kv.rest()
    grad_kv = added(grad_kv.take())
    out_sums.send()
    y_sums.rest(1)
    grad_kv = turn_back(grad_kv, cosine, sine).astype(BF)
    grad_key, grad_value = deinterleave(grad_kv)
    grad_kv = jnp.concatenate([grad_key, grad_value], axis=1)
    of_kv = Product(hidden_one, grad_kv, 1.5)
    of_kv.first()
    gate_grad, up_grad = spread_out()
    out_sums.rest(1)
    y_sums.rest(1)
    grad_hidden_one = order.run(
        back_project, [grad_key, grad_value], [weight_k, weight_v], base=grad_hidden_one, kind=F32, micros=3
    )
    of_kv.second()
    out_sums.rest(1)
    tokens_grad, gain_one_term = order.run(
        norm_back, scalars, tokens, gain_one, grad_residual, [grad_hidden_one], rounded=False
    )
    y_sums.rest(1)
    out_sums.rest(1)
    gain_terms = xor_blocks(jnp.concatenate([gain_one_term, gain_two_term], axis=0), f, 1)
    gain_terms = gain_terms.astype(BF).reshape(2, 4 * n, model // (4 * n)).transpose(1, 0, 2)
    gain_terms = lax.all_to_all(gain_terms, ("fsdp", "ctx"), 0, 0, tiled=False)
    of_query.settle()
    query_sums = scatter_rows(of_query.last(BF))
    y_sums.rest()
    layer_out = order.done((residual + added(y_sums.take())).astype(BF))
    query_sums.send()
    out_sums.rest()
    out_grad = order.done(added(out_sums.take()))
    gain_terms = order.take(gain_terms)
    of_kv.settle()
    kv_sums = scatter_rows(of_kv.last(BF))
    query_sums.rest(1)
    kv_sums.send()
    query_sums.rest(1)
    kv_sums.rest(1)
    query_sums.rest(1)
    kv_sums.rest(1)
    query_sums.rest()
    query_sums = query_sums.take()
    kv_sums.rest(1)
    query_grad = order.done(added(query_sums))
    kv_sums.rest()
    kv_grad = order.done(added(kv_sums.take()))
    gain_grads = jnp.sum(gain_terms.astype(F32), axis=0)
    kv_width = key_matrix.shape[1]
    key_grad, value_grad = kv_grad[:, :kv_width], kv_grad[:, kv_width:]
    return (
        layer_out,
        tokens_grad,
        gain_grads[0],
        query_grad,
        key_grad,
        value_grad,
        out_grad,
        gain_grads[1],
        gate_grad,
        up_grad,
        down_grad,
    )


def solution(mesh):
    rows, vector = P(("fsdp", "ctx"), None), P(("fsdp", "ctx"))
    weight = P("fsdp", None)

    def layer(*arrays):
        return body(mesh.shape["ctx"], *arrays)

    return jax.shard_map(
        layer,
        mesh=mesh,
        in_specs=(
            rows, P("fsdp"), weight, weight, weight, weight, P("fsdp"), weight, weight, weight,
            weight, P(), rows,
        ),
        out_specs=(rows, rows, vector, rows, rows, rows, rows, vector, rows, rows, rows),
        check_vma=False,
    )
```
